32 devices in a mesh: tower: 2 (over x), items: 16 (over z, y, core).
Axes of the slice: x: 2, y: 2, z: 4, core: 2. Of those that a mesh axis runs over, the one named last changes fastest.
Arguments:
- states: bfloat16 [2, 2, 16, 512, 768], P('tower', None, 'items'), may hold values from -6 to 6
- proj_weight: bfloat16 [2, 768, 768], P('tower'), may hold values from -0.21875 to 0.21875
- proj_bias: float32 [2, 768], P('tower'), may hold values from -2 to 2
- cls_row: float32 [768], replicated, may hold values from -6 to 6
- norm1_gain: float32 [768], replicated, may hold values from 0.25 to 1.75
- norm1_shift: float32 [768], replicated, may hold values from -2 to 2
- qkv_weight: bfloat16 [768, 2304], replicated, may hold values from -0.3125 to 0.3125
- qv_bias: float32 [1536], replicated, may hold values from -2 to 2
- out_weight: bfloat16 [768, 768], replicated, may hold values from -3.5 to 3.5
- out_bias: float32 [768], replicated, may hold values from -2 to 2
- norm2_gain: float32 [768], replicated, may hold values from 0.25 to 1.75
- norm2_shift: float32 [768], replicated, may hold values from -2 to 2
- up_weight: bfloat16 [768, 3072], replicated, may hold values from -0.21875 to 0.21875
- up_bias: float32 [3072], replicated, may hold values from -2 to 2
- down_weight: bfloat16 [3072, 768], replicated, may hold values from -0.109375 to 0.109375
- down_bias: float32 [768], replicated, may hold values from -2 to 2
- image_group: int32 [2, 16], P('tower', 'items'), may hold values from 0 to 1
- caption_len: int32 [2, 16], P('tower', 'items'), may hold values from 64 to 512, as said below
- out_grad: bfloat16 [2, 16, 838, 768], P('tower', 'items'), may hold values from -6 to 6
Outputs:
- layer_out: bfloat16 [2, 16, 838, 768], P('tower', 'items')
- state_grad: bfloat16 [2, 2, 16, 512, 768], P('tower', None, 'items')
- proj_weight_grad: float32 [2, 768, 768], P('tower', 'items')
- proj_bias_grad: float32 [2, 768], P('tower', 'items')
- cls_grad: float32 [768], P('items')
- norm1_gain_grad: float32 [768], P('items')
- norm1_shift_grad: float32 [768], P('items')
- qkv_weight_grad: float32 [768, 2304], P('items')
- qv_bias_grad: float32 [1536], P('items')
- out_weight_grad: float32 [768, 768], P('items')
- out_bias_grad: float32 [768], P('items')
- norm2_gain_grad: float32 [768], P('items')
- norm2_shift_grad: float32 [768], P('items')
- up_weight_grad: float32 [768, 3072], P('items')
- up_bias_grad: float32 [3072], P('items')
- down_weight_grad: float32 [3072, 768], P('items')
- down_bias_grad: float32 [768], P('items')
The draws below stay inside these ranges and needn't reach their ends.
Inputs may be any that keep to these rules, and one draw needn't show every extreme that they name: `image_group`: an image has 197 patch rows where its group is 0 and 325 where it is 1. `caption_len`: some item's caption fills all 512 slots.
All inputs are finite; a program needn't handle non-finite values.
Results may differ from the reference program's by a relative error of at most 0.015.
The reference program's roundings to bfloat16 on the way count: a program that leaves them out, or rounds other values in their place, can miss the bound.
Values may be sent and summed in bfloat16 or wider, within the bound.
A program may use at most 256 MiB of HBM per device.

```python
import jax
import jax.numpy as jnp
from jax import lax

D = 768
HEADS = 12
HEAD_DIM = 64
FF = 3072
PATCH_SMALL = 197
PATCH_BIG = 325
CAPTION = 512
HALF = 16
JOINT = 838


def draw_caption_len(key, part):
    key = jax.random.fold_in(key, 7)
    key_len, key_spot = jax.random.split(key)
    random_len = jax.random.randint(key_len, (2, HALF), CAPTION // 8, CAPTION + 1)
    chosen = jax.random.randint(key_spot, (), 0, 2 * HALF)
    slot_index = jnp.arange(2 * HALF, dtype=jnp.int32).reshape(2, HALF)
    return jnp.where(slot_index == chosen, CAPTION, random_len).astype(jnp.int32)


def with_ends(array, stream_key, least, high):
    longest = array.shape.index(max(array.shape))
    spots = []
    for shift in (0, 1):
        where = [jax.random.randint(jax.random.fold_in(stream_key, axis), (), 0, length) for axis, length in enumerate(array.shape)]
        where[longest] = (where[longest] + shift) % array.shape[longest]
        spots.append(tuple(where))
    return array.at[spots[0]].set(least).at[spots[1]].set(high)


def strengthened(values, own_key, source, target, parts, factor):
    owner, partner = [(jnp.arange(values.shape[dim]) // (values.shape[dim] // parts)).reshape([-1 if axis == dim else 1 for axis in range(values.ndim)]) for dim in (source, target)]
    chosen = jax.random.permutation(own_key, parts)[partner]
    strong = (owner == chosen) | (owner == (partner + parts // 2) % parts)
    return jnp.where(strong, factor * values, values)


def levels(key, shape, cuts, least, high):
    gain = 1.0
    for dim, shards_of in cuts:
        heights = jax.random.uniform(jax.random.fold_in(jax.random.fold_in(key, 6), dim), (shards_of,), jnp.float32, least / len(cuts), high / len(cuts))
        gain = gain * jnp.repeat(jnp.exp(heights), shape[dim] // shards_of).reshape((-1,) + (1,) * (len(shape) - 1 - dim))
    return gain


def bell_draw(stream_key, dims, width, reach, cuts=(), kind=jnp.bfloat16):
    gain = levels(stream_key, dims, cuts, -0.22, 0.18) if cuts else 1.0
    drawn = jax.random.normal(stream_key, dims, jnp.float32) * width * gain
    return jnp.minimum(jnp.maximum(drawn, -reach), reach).astype(kind)


def noise_with(own_key, shape, width, bound, cuts, heavy, kind=jnp.bfloat16):
    values = width * jax.random.normal(own_key, shape, jnp.float32)
    if cuts:
        values = values * levels(own_key, shape, cuts, -0.22, 0.18)
    return jnp.clip(strengthened(values, jax.random.fold_in(own_key, 3), *heavy), -bound, bound).astype(kind)


def setup_inputs(seed: int = 0) -> dict:
    arg_keys = jax.random.split(jax.random.key(seed), 20)
    return {
        "states": bell_draw(arg_keys[0], (2, 2, HALF, CAPTION, D), 1.0, 6.0, ((0, 2), (2, 16))),
        "proj_weight": bell_draw(arg_keys[1], (2, D, D), D ** -0.5, 0.21875, ((0, 2),)),
        "proj_bias": bell_draw(arg_keys[2], (2, D), 0.3, 2.0, ((0, 2),), jnp.float32),
        "cls_row": bell_draw(arg_keys[3], (D,), 1.0, 6.0, (), jnp.float32),
        "norm1_gain": jnp.clip(1.0 + 0.15 * jax.random.normal(arg_keys[4], (D,), jnp.float32), 0.25, 1.75),
        "norm1_shift": bell_draw(arg_keys[5], (D,), 0.3, 2.0, (), jnp.float32),
        "qkv_weight": bell_draw(arg_keys[6], (D, 3 * D), (D // 2) ** -0.5, 0.3125),
        "qv_bias": bell_draw(arg_keys[7], (2 * D,), 0.3, 2.0, (), jnp.float32),
        "out_weight": bell_draw(arg_keys[8], (D, D), (max(D * 4 // JOINT, 1)) ** -0.5, 3.5),
        "out_bias": bell_draw(arg_keys[9], (D,), 0.3, 2.0, (), jnp.float32),
        "norm2_gain": jnp.clip(1.0 + 0.15 * jax.random.normal(arg_keys[10], (D,), jnp.float32), 0.25, 1.75),
        "norm2_shift": bell_draw(arg_keys[11], (D,), 0.3, 2.0, (), jnp.float32),
        "up_weight": bell_draw(arg_keys[12], (D, FF), D ** -0.5, 0.21875),
        "up_bias": bell_draw(arg_keys[13], (FF,), 0.3, 2.0, (), jnp.float32),
        "down_weight": bell_draw(arg_keys[14], (FF, D), FF ** -0.5, 0.109375),
        "down_bias": bell_draw(arg_keys[15], (D,), 0.3, 2.0, (), jnp.float32),
        "image_group": with_ends(jax.random.randint(arg_keys[16], (2, HALF), 0, 2), jax.random.fold_in(arg_keys[16], 1), 0, 1).astype(jnp.int32),
        "caption_len": draw_caption_len(jax.random.fold_in(arg_keys[19], 71), 0),
        "out_grad": noise_with(arg_keys[18], (2, HALF, JOINT, D), 1.0, 6.0, ((0, 2), (1, 16)), (1, 3, 16, 2.0)),
    }


EPSILON = 1e-06
MASKED = -1000000000.0
SCALE = 0.125

@jax.custom_vjp
def low(v):
    return lax.optimization_barrier(v.astype(jnp.bfloat16)).astype(jnp.float32)

@jax.custom_vjp
def low_back(v):
    return v

def low_keep(v):
    return (low(v), None)

def low_pass(kept, grad):
    return (grad,)

def back_keep(v):
    return (v, None)

def back_low(kept, grad):
    return (low(grad),)
low.defvjp(low_keep, low_pass)
low_back.defvjp(back_keep, back_low)

def matmul(left, right):
    return jnp.dot(left, right, precision=lax.Precision.HIGHEST, preferred_element_type=jnp.float32)

def layer_norm(inputs, norm_gain, norm_shift):
    row_mean = lax.optimization_barrier(jnp.mean(inputs, axis=-1, keepdims=True))
    centered = inputs - row_mean
    variance = lax.optimization_barrier(jnp.mean(centered * centered, axis=-1, keepdims=True))
    return centered * lax.rsqrt(variance + EPSILON) * norm_gain + norm_shift

def item_forward(layer_params, image_state, text_state, group, length):
    proj_weight, proj_bias, cls_row, norm1_gain, norm1_shift, qkv_weight, qv_bias, out_weight, out_bias, norm2_gain, norm2_shift, up_weight, up_bias, down_weight, down_bias = layer_params
    model_width = cls_row.shape[0]
    image_rows = low(low_back(matmul(image_state, proj_weight[0]) + proj_bias[0]))
    text_rows = low(low_back(matmul(text_state, proj_weight[1]) + proj_bias[1]))
    joined = jnp.concatenate([cls_row[None, :], image_rows[:PATCH_BIG], text_rows], axis=0)
    extent = joined.shape[0]
    position = jnp.arange(extent, dtype=jnp.int32)
    patches = PATCH_SMALL + (PATCH_BIG - PATCH_SMALL) * group
    live_rows = (position == 0) | (position >= 1) & (position <= patches) | (position > PATCH_BIG) & (position - PATCH_BIG - 1 < length)
    first_normed = low(layer_norm(joined, norm1_gain, norm1_shift))
    projected_qkv = matmul(first_normed, qkv_weight)
    queries = low(low_back(projected_qkv[:, :model_width] + qv_bias[:model_width])).reshape(extent, HEADS, HEAD_DIM)
    key_rows = low(low_back(projected_qkv[:, model_width:2 * model_width])).reshape(extent, HEADS, HEAD_DIM)
    value_rows = low(low_back(projected_qkv[:, 2 * model_width:] + qv_bias[model_width:])).reshape(extent, HEADS, HEAD_DIM)
    raw_scores = jnp.einsum('qhe,khe->hqk', queries, key_rows, precision=lax.Precision.HIGHEST) * SCALE
    scores = low_back(jnp.where(live_rows[None, None, :], raw_scores, MASKED))
    attn_weights = low(jax.nn.softmax(scores, axis=-1))
    attended = jnp.einsum('hqk,khe->qhe', attn_weights, value_rows, precision=lax.Precision.HIGHEST)
    attended = low(low_back(attended.reshape(extent, model_width)))
    middle = joined + low_back(matmul(attended, out_weight) + out_bias)
    second_normed = low(layer_norm(middle, norm2_gain, norm2_shift))
    hidden_pre = low_back(matmul(second_normed, up_weight) + up_bias)
    activated = low(jax.nn.gelu(hidden_pre, approximate=False))
    result = middle + matmul(activated, down_weight) + down_bias
    return result * live_rows[:, None].astype(jnp.float32)

def reference(states, proj_weight, proj_bias, cls_row, norm1_gain, norm1_shift, qkv_weight, qv_bias, out_weight, out_bias, norm2_gain, norm2_shift, up_weight, up_bias, down_weight, down_bias, image_group, caption_len, out_grad):
    layer_params = tuple((item.astype(jnp.float32) for item in (proj_weight, proj_bias, cls_row, norm1_gain, norm1_shift, qkv_weight, qv_bias, out_weight, out_bias, norm2_gain, norm2_shift, up_weight, up_bias, down_weight, down_bias)))
    model_width = cls_row.shape[0]
    image_all = states[0].reshape(2 * HALF, CAPTION, model_width).astype(jnp.float32)
    text_all = states[1].reshape(2 * HALF, CAPTION, model_width).astype(jnp.float32)
    groups = image_group.reshape(2 * HALF).astype(jnp.int32)
    lengths = caption_len.reshape(2 * HALF).astype(jnp.int32)
    item_step = jax.checkpoint(item_forward)

    def forward(weights, image_in, text_in):
        return lax.map(lambda pieces: item_step(weights, pieces[0], pieces[1], pieces[2], pieces[3]), (image_in, text_in, groups, lengths))
    result, pullback = jax.vjp(forward, layer_params, image_all, text_all)
    layer_grads, grad_image, grad_text = pullback(out_grad.reshape(2 * HALF, JOINT, model_width).astype(jnp.float32))
    layer_out = result.reshape(2, HALF, JOINT, model_width).astype(jnp.bfloat16)
    state_grad = jnp.stack([grad_image, grad_text]).reshape(2, 2, HALF, CAPTION, model_width).astype(jnp.bfloat16)
    return (layer_out, state_grad, layer_grads[0], layer_grads[1], layer_grads[2], layer_grads[3], layer_grads[4], layer_grads[5], layer_grads[6], layer_grads[7], layer_grads[8], layer_grads[9], layer_grads[10], layer_grads[11], layer_grads[12], layer_grads[13], layer_grads[14])
```

```python
import functools

import jax
import jax.numpy as jnp
from jax import lax
from jax.experimental import pallas as pl
from jax.experimental.pallas import tpu as pltpu
from jax.sharding import PartitionSpec as P

HEADS = 12
HEAD_DIM = 64
PATCH_SMALL = 197
PATCH_BIG = 325
EPSILON = 1e-06
MASKED = -1000000000.0
SCALE = 0.125
ROWS = 896
LANES = 128
TILE_ROWS = 16

F32 = jnp.float32
BF16 = jnp.bfloat16
NN = (((1,), (0,)), ((), ()))
NT = (((1,), (1,)), ((), ()))
TN = (((0,), (0,)), ((), ()))
MESH = pl.DeviceIdType.MESH


def dot(left, right, numbers=NN):
    return lax.dot_general(left, right, numbers, preferred_element_type=F32)


def live_column(group, length, text_rows):
    row = lax.broadcasted_iota(jnp.int32, (ROWS, 1), 0)
    patches = PATCH_SMALL + (PATCH_BIG - PATCH_SMALL) * group
    image = (row >= text_rows) & (row < text_rows + patches)
    return (row < length) | image | (row == text_rows + PATCH_BIG)


def key_lanes(group, length, text_rows):
    lane = lax.broadcasted_iota(jnp.int32, (ROWS, LANES), 1)
    row = lax.broadcasted_iota(jnp.int32, (ROWS, LANES), 0)
    patches = PATCH_SMALL + (PATCH_BIG - PATCH_SMALL) * group
    image = (row >= text_rows) & (row < text_rows + patches)
    live = (row < length) | image | (row == text_rows + PATCH_BIG)
    bias = jnp.where(live, 0.0, MASKED)
    return jnp.where(lane == 0, bias, jnp.where(lane < 4, 1.0, 0.0)).astype(BF16)


def query_lanes(first, column):
    lane = lax.broadcasted_iota(jnp.int32, (ROWS, LANES), 1)
    upper = column.astype(BF16).astype(F32)
    rest = column - upper
    inner = rest.astype(BF16).astype(F32)
    lower = rest - inner
    lanes = jnp.where(lane == 0, first, 0.0)
    lanes = jnp.where(lane == 1, -upper, lanes)
    lanes = jnp.where(lane == 2, -inner, lanes)
    return jnp.where(lane == 3, -lower, lanes).astype(BF16)


def head_part(block, head):
    lane = lax.broadcasted_iota(jnp.int32, block.shape, 1)
    keep = lane < HEAD_DIM if head == 0 else lane >= HEAD_DIM
    return jnp.where(keep, block, jnp.zeros_like(block))


def attention_kernel(text_rows, group_ref, length_ref, qkv_ref, out_ref, total_ref, key_ref):
    width = out_ref.shape[1]
    key_ref[...] = key_lanes(group_ref[0, 0], length_ref[0, 0], text_rows)
    lane = lax.broadcasted_iota(jnp.int32, (ROWS, LANES), 1)
    plain = jnp.where(lane == 0, 1.0, 0.0).astype(BF16)

    @pl.loop(0, width // LANES)
    def pair(index):
        at = pl.multiple_of(index * LANES, LANES)
        queries = qkv_ref[:, pl.ds(at, LANES)]
        keys = qkv_ref[:, pl.ds(pl.multiple_of(width + at, LANES), LANES)]
        values = qkv_ref[:, pl.ds(pl.multiple_of(2 * width + at, LANES), LANES)]
        keys = jnp.concatenate([keys, key_ref[...]], axis=1)
        values = jnp.concatenate([values, key_ref[...]], axis=1)
        scores = []
        for head in range(2):
            own = jnp.concatenate([head_part(queries, head), plain], axis=1)
            scores.append(dot(own, keys, NT))
        outs, totals = [], []
        for head in range(2):
            row_max = jnp.max(scores[head], axis=1, keepdims=True)
            weights = jnp.exp(scores[head] - row_max).astype(BF16)
            mixed = dot(weights, values)
            row_total = mixed[:, LANES + 1 : LANES + 2]
            outs.append(mixed[:, :LANES] / row_total)
            totals.append(row_max + jnp.log(row_total))
        out_ref[:, pl.ds(at, LANES)] = jnp.where(lane < HEAD_DIM, outs[0], outs[1]).astype(BF16)
        total_ref[index] = jnp.where(lane < HEAD_DIM, totals[0], totals[1])


def attention(text_rows, group, length, qkv):
    width = qkv.shape[1] // 3
    pairs = width // LANES
    return pl.pallas_call(
        functools.partial(attention_kernel, text_rows),
        out_shape=(
            jax.ShapeDtypeStruct((ROWS, width), BF16),
            jax.ShapeDtypeStruct((pairs, ROWS, LANES), F32),
        ),
        in_specs=[
            pl.BlockSpec(memory_space=pltpu.SMEM),
            pl.BlockSpec(memory_space=pltpu.SMEM),
            pl.BlockSpec(memory_space=pltpu.VMEM),
        ],
        scratch_shapes=[pltpu.VMEM((ROWS, LANES), BF16)],
        compiler_params=pltpu.CompilerParams(vmem_limit_bytes=52 << 20),
        name="attention_forward",
    )(group, length, qkv)


def attention_back_kernel(
    text_rows, group_ref, length_ref, qkv_ref, total_ref, out_ref, grad_ref, back_ref, key_ref
):
    width = out_ref.shape[1]
    key_ref[...] = key_lanes(group_ref[0, 0], length_ref[0, 0], text_rows)

    @pl.loop(0, width // LANES)
    def pair(index):
        at = pl.multiple_of(index * LANES, LANES)
        key_at = pl.multiple_of(width + at, LANES)
        value_at = pl.multiple_of(2 * width + at, LANES)
        queries = qkv_ref[:, pl.ds(at, LANES)]
        keys = qkv_ref[:, pl.ds(key_at, LANES)]
        values = qkv_ref[:, pl.ds(value_at, LANES)]
        grads = grad_ref[:, pl.ds(at, LANES)]
        product = grads.astype(F32) * out_ref[:, pl.ds(at, LANES)].astype(F32)
        wide_keys = jnp.concatenate([keys, key_ref[...]], axis=1)
        wide_values = jnp.concatenate([values, key_ref[...]], axis=1)
        keys_across = keys.T
        query_grad, key_grad, value_grad = [], None, None
        for head in range(2):
            own_queries = head_part(queries, head)
            own_grads = head_part(grads, head)
            log_total = total_ref[index, :, HEAD_DIM * head : HEAD_DIM * head + 1]
            inner = jnp.sum(head_part(product, head), axis=1, keepdims=True)
            left = jnp.concatenate([own_queries, query_lanes(1.0, log_total)], axis=1)
            right = jnp.concatenate([own_grads, query_lanes(0.0, inner)], axis=1)
            weights = jnp.exp(dot(wide_keys, left, NT))
            score_grad = (weights * dot(wide_values, right, NT)).astype(BF16)
            value_part = dot(weights.astype(BF16), own_grads)
            key_part = dot(score_grad, own_queries)
            value_grad = value_part if value_grad is None else value_grad + value_part
            key_grad = key_part if key_grad is None else key_grad + key_part
            query_grad.append(
                dot(keys_across[HEAD_DIM * head : HEAD_DIM * (head + 1)], score_grad)
            )
        across = jnp.concatenate(query_grad, axis=0).T
        back_ref[:, pl.ds(at, LANES)] = (SCALE * across).astype(BF16)
        back_ref[:, pl.ds(key_at, LANES)] = key_grad.astype(BF16)
        back_ref[:, pl.ds(value_at, LANES)] = value_grad.astype(BF16)


def attention_back(text_rows, group, length, qkv, log_total, attended, grad_attended):
    return pl.pallas_call(
        functools.partial(attention_back_kernel, text_rows),
        out_shape=jax.ShapeDtypeStruct(qkv.shape, BF16),
        in_specs=[pl.BlockSpec(memory_space=pltpu.SMEM)] * 2
        + [pl.BlockSpec(memory_space=pltpu.VMEM)] * 4,
        scratch_shapes=[pltpu.VMEM((ROWS, LANES), BF16)],
        compiler_params=pltpu.CompilerParams(vmem_limit_bytes=56 << 20),
        name="attention_backward",
    )(group, length, qkv, log_total, attended, grad_attended)


def tower_partner():
    return {"tower": 1 - lax.axis_index("tower")}


def item_partner(bit):
    me = lax.axis_index("items")
    low = lax.rem(me // (1 << bit), 2)
    return {"items": me + (1 - 2 * low) * (1 << bit)}, low


def reduce_kernel(bits, units, shared, own_rows, *refs):
    grads, vectors, out_ref, vector_out = refs[:4]
    landed = refs[4 : 4 + bits]
    crossing, crossed, held, vector_here, vector_there = refs[4 + bits : 9 + bits]
    load_sem, send_sem, recv_sem, vector_send, vector_recv = refs[9 + bits :]
    steps = bits + 1

    barrier = pltpu.get_barrier_semaphore()
    partners = [item_partner(bit) for bit in range(bits)]
    for partner, _ in partners:
        pl.semaphore_signal(barrier, inc=1, device_id=partner, device_id_type=MESH)
    pl.semaphore_signal(barrier, inc=1, device_id=tower_partner(), device_id_type=MESH)
    pl.semaphore_wait(barrier, steps)

    lead = (slice(None),)

    def piece(ref, unit, bit, side):
        return ref.at[(unit,) + lead * (bits - 1 - bit) + (side,)]

    def load(unit):
        return pltpu.make_async_copy(
            piece(grads, unit, 0, partners[0][1]), held.at[unit], load_sem.at[unit]
        )

    def send(unit, step):
        if step < bits:
            partner, low = partners[step]
            source = grads if step == 0 else landed[step - 1]
            return pltpu.make_async_remote_copy(
                src_ref=piece(source, unit, step, 1 - low),
                dst_ref=landed[step].at[unit],
                send_sem=send_sem.at[unit, step],
                recv_sem=recv_sem.at[unit, step],
                device_id=partner,
                device_id_type=MESH,
            )
        return pltpu.make_async_remote_copy(
            src_ref=crossing.at[unit],
            dst_ref=crossed.at[unit],
            send_sem=send_sem.at[unit, step],
            recv_sem=recv_sem.at[unit, step],
            device_id=tower_partner(),
            device_id_type=MESH,
        )

    def add(unit, step):
        if step == 0:
            load(unit).wait()
        mine = held.at[unit] if step == 0 else piece(landed[step - 1], unit, step, partners[step][1])
        there = landed[step].at[unit]
        rows = there.shape[-2]
        count = 1 << (bits - 1 - step)

        @pl.loop(0, count)
        def _(number):
            place = tuple(lax.rem(number // (1 << low), 2) for low in reversed(range(bits - 1 - step)))
            total = mine[place].astype(F32) + there[place].astype(F32)
            if step < bits - 1:
                there[place] = total.astype(BF16)
            else:
                crossing[unit] = total.astype(BF16)
                out_ref[unit] = total

    @pl.loop(0, units)
    def _(unit):
        load(unit).start()

    def vector_send_step(step):
        partner = partners[step][0] if step < bits else tower_partner()
        return pltpu.make_async_remote_copy(
            src_ref=vector_here.at[step],
            dst_ref=vector_there.at[step],
            send_sem=vector_send.at[step],
            recv_sem=vector_recv.at[step],
            device_id=partner,
            device_id_type=MESH,
        )

    vector_here[0] = vectors[...]
    vector_send_step(0).start()

    @pl.loop(0, units)
    def _(unit):
        send(unit, 0).start()

    for step in range(steps):
        vector_send_step(step).wait()
        total = vector_here[step] + vector_there[step]
        if step < bits:
            vector_here[step + 1] = total
            vector_send_step(step + 1).start()
        else:
            row = lax.broadcasted_iota(jnp.int32, total.shape, 0)
            vector_out[...] = jnp.where(row == own_rows, vector_here[step], total)

    @pl.loop(0, units + steps - 1)
    def _(wave):
        for step in range(steps):
            unit = wave - step

            @pl.when((unit >= 0) & (unit < (units if step < bits else shared)))
            def _():
                send(unit, step).wait()
                if step < bits:
                    add(unit, step)
                    if step + 1 < bits:
                        send(unit, step + 1).start()
                    else:

                        @pl.when(unit < shared)
                        def _():
                            send(unit, step + 1).start()

                else:
                    out_ref[unit] = crossing[unit].astype(F32) + crossed[unit].astype(F32)


def reduce_all(grads, vectors, bits, shared, own_rows):
    units, rows, width = grads.shape[0], grads.shape[-2], grads.shape[-1]
    landed = [
        pltpu.VMEM((units,) + (2,) * (bits - 1 - step) + (rows, width), BF16)
        for step in range(bits)
    ]
    steps = bits + 1
    return pl.pallas_call(
        functools.partial(reduce_kernel, bits, units, shared, own_rows),
        out_shape=(
            jax.ShapeDtypeStruct((units, rows, width), F32),
            jax.ShapeDtypeStruct(vectors.shape, F32),
        ),
        in_specs=[pl.BlockSpec(memory_space=pl.ANY), pl.BlockSpec(memory_space=pltpu.VMEM)],
        scratch_shapes=landed
        + [
            pltpu.VMEM((units, rows, width), BF16),
            pltpu.VMEM((units, rows, width), BF16),
            pltpu.VMEM((units,) + (2,) * (bits - 1) + (rows, width), BF16),
            pltpu.VMEM((steps,) + vectors.shape, F32),
            pltpu.VMEM((steps,) + vectors.shape, F32),
            pltpu.SemaphoreType.DMA((units,)),
            pltpu.SemaphoreType.DMA((units, steps)),
            pltpu.SemaphoreType.DMA((units, steps)),
            pltpu.SemaphoreType.DMA((steps,)),
            pltpu.SemaphoreType.DMA((steps,)),
        ],
        compiler_params=pltpu.CompilerParams(
            collective_id=1, has_side_effects=True, vmem_limit_bytes=52 << 20
        ),
        name="reduce_gradients",
    )(grads, vectors)


VECTOR_ROWS = 16


def spread_kernel(layout, sums_ref, vectors_ref, *outs):
    me = lax.axis_index("items")
    for (kind, first, count), out_ref in zip(layout, outs):
        if kind == "columns":
            rows, width = sums_ref.shape[1:]
            for part in range(count):
                out_ref[:, part * width : (part + 1) * width] = sums_ref[first + part]
        elif kind == "rows":
            rows = sums_ref.shape[1]
            for part in range(count):
                out_ref[part * rows : (part + 1) * rows, :] = sums_ref[first + part]
        else:
            line = jnp.concatenate(
                [vectors_ref[first + part : first + part + 1, :] for part in range(count)], axis=1
            )
            share = out_ref.shape[1]
            line = jnp.broadcast_to(line, (8, line.shape[1]))
            line = pltpu.roll(line, lax.rem(line.shape[1] - me * share, line.shape[1]), 1)
            out_ref[...] = line[0:1, :share]


def spread(layout, shapes, sums, vectors):
    return pl.pallas_call(
        functools.partial(spread_kernel, layout),
        out_shape=tuple(jax.ShapeDtypeStruct(shape, F32) for shape in shapes),
        in_specs=[pl.BlockSpec(memory_space=pltpu.VMEM)] * 2,
        out_specs=tuple(pl.BlockSpec(memory_space=pltpu.VMEM) for _ in shapes),
        compiler_params=pltpu.CompilerParams(vmem_limit_bytes=32 << 20),
        name="spread_shares",
    )(sums, vectors)


def from_partner(block, axis, apart):
    count = lax.axis_size(axis)
    route = []
    for low in range(count):
        high = low | 1 << apart
        if high != low and high < count:
            route += [(low, high), (high, low)]
    return lax.ppermute(block, axis, route)


def layer_norm(inputs, norm_gain, norm_shift):
    row_mean = jnp.mean(inputs, axis=-1, keepdims=True)
    centered = inputs - row_mean
    variance = jnp.mean(centered * centered, axis=-1, keepdims=True)
    return centered * lax.rsqrt(variance + EPSILON) * norm_gain + norm_shift


def exact_gelu(inputs):
    return jax.nn.gelu(inputs, approximate=False)


def body(
    states,
    proj_weight,
    proj_bias,
    cls_row,
    norm1_gain,
    norm1_shift,
    qkv_weight,
    qv_bias,
    out_weight,
    out_bias,
    norm2_gain,
    norm2_shift,
    up_weight,
    up_bias,
    down_weight,
    down_bias,
    image_group,
    caption_len,
    out_grad,
):
    side = lax.axis_index("tower")
    on_image_side = side == 0
    width = states.shape[-1]
    text_rows = states.shape[3]
    hidden = up_weight.shape[1]
    extent = out_grad.shape[2]
    padding = ROWS - extent
    own_states = states[0].reshape(2 * text_rows, width)
    projected = (dot(own_states, proj_weight[0]) + proj_bias[0]).astype(BF16)
    projected = projected.reshape(2, text_rows, width)
    kept_rows = jnp.where(on_image_side, projected[0], projected[1])
    sent_rows = jnp.where(on_image_side, projected[1], projected[0])
    arrived = from_partner(sent_rows, "tower", 0)
    image_rows = jnp.where(on_image_side, kept_rows, arrived)
    caption_rows = jnp.where(on_image_side, arrived, kept_rows)
    joined = jnp.concatenate(
        [
            caption_rows.astype(F32),
            image_rows[:PATCH_BIG].astype(F32),
            cls_row[None],
            jnp.zeros((padding, width), F32),
        ],
        axis=0,
    )
    group, length = image_group, caption_len
    row_mask = live_column(group[0, 0], length[0, 0], text_rows).astype(F32)
    first_normed, norm1_back = jax.vjp(layer_norm, joined, norm1_gain, norm1_shift)
    first_input = first_normed.astype(BF16)
    scale = jnp.concatenate([jnp.full((width,), SCALE, F32), jnp.ones((2 * width,), F32)])
    bias = jnp.concatenate([qv_bias[:width], jnp.zeros((width,), F32), qv_bias[width:]])
    qkv = ((dot(first_input, qkv_weight) + bias) * scale).astype(BF16)
    attended, log_total = attention(text_rows, group, length, qkv)
    middle = joined + (dot(attended, out_weight) + out_bias)
    second_normed, norm2_back = jax.vjp(layer_norm, middle, norm2_gain, norm2_shift)
    second_input = second_normed.astype(BF16)
    hidden_pre = dot(second_input, up_weight) + up_bias
    activated, gelu_back = jax.vjp(exact_gelu, hidden_pre)
    activated = activated.astype(BF16)
    result = middle + dot(activated, down_weight) + down_bias
    masked = (result * row_mask).astype(BF16)
    layer_out = jnp.concatenate(
        [
            masked[text_rows + PATCH_BIG : extent],
            masked[text_rows : text_rows + PATCH_BIG],
            masked[:text_rows],
        ],
        axis=0,
    )[None, None]
    given = out_grad[0, 0]
    given = jnp.concatenate(
        [
            given[1 + PATCH_BIG :],
            given[1 : 1 + PATCH_BIG],
            given[:1],
            jnp.zeros((padding, width), BF16),
        ],
        axis=0,
    )
    grad_result = given.astype(F32) * row_mask
    grad_low = grad_result.astype(BF16)
    down_grad = dot(activated, grad_low, TN)
    down_bias_part = jnp.sum(grad_result, axis=0)
    grad_hidden = gelu_back(dot(grad_low, down_weight, NT))[0].astype(BF16)
    up_grad = dot(second_input, grad_hidden, TN)
    up_bias_part = jnp.sum(grad_hidden, axis=0, dtype=F32)
    grad_second = dot(grad_hidden, up_weight, NT)
    grad_middle_norm, norm2_gain_part, norm2_shift_part = norm2_back(grad_second)
    grad_middle = grad_result + grad_middle_norm
    grad_branch = grad_middle.astype(BF16)
    out_grad_part = dot(attended, grad_branch, TN)
    out_bias_part = jnp.sum(grad_branch, axis=0, dtype=F32)
    grad_attended = dot(grad_branch, out_weight, NT).astype(BF16)
    grad_qkv = attention_back(text_rows, group, length, qkv, log_total, attended, grad_attended)
    qkv_grad = dot(first_input, grad_qkv, TN)
    bias_sums = jnp.sum(grad_qkv, axis=0, dtype=F32)
    grad_first = dot(grad_qkv, qkv_weight, NT)
    grad_first_norm, norm1_gain_part, norm1_shift_part = norm1_back(grad_first)
    grad_joined = grad_middle + grad_first_norm
    cls_part = grad_joined[text_rows + PATCH_BIG]
    grad_image = grad_joined[text_rows : text_rows + PATCH_BIG].astype(BF16)
    grad_image = jnp.concatenate(
        [grad_image, jnp.zeros((text_rows - PATCH_BIG, width), BF16)], axis=0
    )
    grad_text = grad_joined[:text_rows].astype(BF16)
    grad_kept = jnp.where(on_image_side, grad_image, grad_text)
    grad_sent = jnp.where(on_image_side, grad_text, grad_image)
    grad_returned = from_partner(grad_sent, "tower", 0)
    flat_grad = jnp.where(
        on_image_side,
        jnp.concatenate([grad_kept, grad_returned]),
        jnp.concatenate([grad_returned, grad_kept]),
    )
    proj_grad = dot(own_states, flat_grad, TN)
    proj_bias_part = jnp.sum(flat_grad, axis=0, dtype=F32)
    state_grad = dot(flat_grad, proj_weight[0], NT).astype(BF16).reshape(states.shape)

    items = lax.axis_size("items")
    share = width // items
    bits = items.bit_length() - 1
    parts = hidden // width
    vectors = [
        cls_part, norm1_gain_part, norm1_shift_part, bias_sums[:width], bias_sums[2 * width :],
        out_bias_part, norm2_gain_part, norm2_shift_part, up_bias_part, down_bias_part,
        proj_bias_part,
    ]
    if items != 1 << bits or share % TILE_ROWS:
        return (layer_out, state_grad) + plain_sums(
            proj_grad, qkv_grad, out_grad_part, up_grad, down_grad, vectors
        )
    whole = (2,) * bits
    units = jnp.concatenate(
        [
            up_grad.astype(BF16).reshape(width, parts, width).transpose(1, 0, 2)
            .reshape((parts,) + whole + (share, width)),
            down_grad.astype(BF16).reshape(items, parts, share, width).transpose(1, 0, 2, 3)
            .reshape((parts,) + whole + (share, width)),
            qkv_grad.astype(BF16).reshape(width, 3, width).transpose(1, 0, 2)
            .reshape((3,) + whole + (share, width)),
            out_grad_part.astype(BF16).reshape((1,) + whole + (share, width)),
            proj_grad.astype(BF16).reshape((1,) + whole + (share, width)),
        ],
        axis=0,
    )
    lines = jnp.concatenate(vectors)
    count = lines.shape[0] // width
    lines = jnp.pad(lines, (0, VECTOR_ROWS * width - lines.shape[0])).reshape(VECTOR_ROWS, width)
    shared = 2 * parts + 4
    sums, line_sums = reduce_all(units, lines, bits, shared, count - 1)
    layout = (
        ("rows", shared, 1), ("line", count - 1, 1), ("line", 0, 1), ("line", 1, 1),
        ("line", 2, 1), ("columns", 2 * parts, 3), ("line", 3, 2), ("columns", 2 * parts + 3, 1),
        ("line", 5, 1), ("line", 6, 1), ("line", 7, 1), ("columns", 0, parts),
        ("line", 8, parts), ("rows", parts, parts), ("line", 8 + parts, 1),
    )
    shapes = []
    for kind, _, number in layout:
        if kind == "columns":
            shapes.append((share, number * width))
        elif kind == "rows":
            shapes.append((number * share, width))
        else:
            shapes.append((1, number * share))
    shares = spread(layout, shapes, sums, line_sums)
    shares = [
        piece.reshape(-1) if kind == "line" else piece
        for piece, (kind, _, _) in zip(shares, layout)
    ]
    return (layer_out, state_grad, shares[0][None], shares[1][None]) + tuple(shares[2:])


def plain_sums(proj_grad, qkv_grad, out_grad_part, up_grad, down_grad, vectors):
    def over_items(part):
        return lax.psum_scatter(part, "items", scatter_dimension=0, tiled=True)

    def over_both(part):
        return lax.psum(over_items(part).astype(BF16), "tower").astype(F32)

    cls_part, gain1, shift1, query, value, out_bias, gain2, shift2, up_bias, down_bias, proj = (
        vectors
    )
    return (
        over_items(proj_grad)[None],
        over_items(proj)[None],
        over_both(cls_part),
        over_both(gain1),
        over_both(shift1),
        over_both(qkv_grad),
        over_both(jnp.concatenate([query, value])),
        over_both(out_grad_part),
        over_both(out_bias),
        over_both(gain2),
        over_both(shift2),
        over_both(up_grad),
        over_both(up_bias),
        over_both(down_grad),
        over_both(down_bias),
    )


def solution(mesh):
    in_specs = (
        P("tower", None, "items", None, None),
        P("tower", None, None),
        P("tower", None),
        P(),
        P(),
        P(),
        P(),
        P(),
        P(),
        P(),
        P(),
        P(),
        P(),
        P(),
        P(),
        P(),
        P("tower", "items"),
        P("tower", "items"),
        P("tower", "items", None, None),
    )
    out_specs = (
        P("tower", "items", None, None),
        P("tower", None, "items", None, None),
        P("tower", "items", None),
        P("tower", "items"),
        P("items"),
        P("items"),
        P("items"),
        P("items", None),
        P("items"),
        P("items", None),
        P("items"),
        P("items"),
        P("items"),
        P("items", None),
        P("items"),
        P("items", None),
        P("items"),
    )
    return jax.shard_map(body, mesh=mesh, in_specs=in_specs, out_specs=out_specs, check_vma=False)
```

```python
import functools

import jax
import jax.numpy as jnp
from jax import lax
from jax.experimental import pallas as pl
from jax.experimental.pallas import tpu as pltpu
from jax.sharding import PartitionSpec as P

HEADS = 12
HEAD_DIM = 64
PATCH_SMALL = 197
PATCH_BIG = 325
EPSILON = 1e-06
MASKED = -1000000000.0
SCALE = 0.125
ROWS = 896
LANES = 128
TILE_ROWS = 16
GROUPS = 16
SLOTS = 4
VECTOR_ROWS = 16

F32 = jnp.float32
BF16 = jnp.bfloat16
NN = (((1,), (0,)), ((), ()))
NT = (((1,), (1,)), ((), ()))
TN = (((0,), (0,)), ((), ()))
MESH = pl.DeviceIdType.MESH


def dot(left, right, numbers=NN):
    return lax.dot_general(left, right, numbers, preferred_element_type=F32)


def live_rows(shape, group, length, text_rows):
    row = lax.broadcasted_iota(jnp.int32, shape, 0)
    patches = PATCH_SMALL + (PATCH_BIG - PATCH_SMALL) * group
    image = (row >= text_rows) & (row < text_rows + patches)
    return (row < length) | image | (row == text_rows + PATCH_BIG)


def key_lanes(group, length, text_rows):
    lane = lax.broadcasted_iota(jnp.int32, (ROWS, LANES), 1)
    bias = jnp.where(live_rows((ROWS, LANES), group, length, text_rows), 0.0, MASKED)
    return jnp.where(lane == 0, bias, jnp.where(lane < 4, 1.0, 0.0)).astype(BF16)


def query_lanes(first, column):
    lane = lax.broadcasted_iota(jnp.int32, (ROWS, LANES), 1)
    upper = column.astype(BF16).astype(F32)
    rest = column - upper
    inner = rest.astype(BF16).astype(F32)
    lower = rest - inner
    lanes = jnp.where(lane == 0, first, 0.0)
    lanes = jnp.where(lane == 1, -upper, lanes)
    lanes = jnp.where(lane == 2, -inner, lanes)
    return jnp.where(lane == 3, -lower, lanes).astype(BF16)


def head_part(block, head):
    lane = lax.broadcasted_iota(jnp.int32, block.shape, 1)
    keep = lane < HEAD_DIM if head == 0 else lane >= HEAD_DIM
    return jnp.where(keep, block, jnp.zeros_like(block))


def column_sum(block):
    return jnp.sum(block, axis=0, keepdims=True)


def row_mean(block):
    return jnp.mean(block, axis=1, keepdims=True)


def normalize(block):
    centered = block - row_mean(block)
    inverse = lax.rsqrt(row_mean(centered * centered) + EPSILON)
    return centered * inverse, inverse


def in_vmem(count=1):
    return [pl.BlockSpec(memory_space=pltpu.VMEM)] * count


def in_smem(count=1):
    return [pl.BlockSpec(memory_space=pltpu.SMEM)] * count


def anywhere(count=1):
    return [pl.BlockSpec(memory_space=pl.ANY)] * count


def tower_partner():
    return {"tower": 1 - lax.axis_index("tower")}


def item_partner(bit):
    me = lax.axis_index("items")
    low = lax.rem(me // (1 << bit), 2)
    return {"items": me + (1 - 2 * low) * (1 << bit)}, low


def chunks_of(side, text_rows):
    half = text_rows // 2
    if side == 1:
        return (0, half), (half, half)
    return (0, half), (half, ROWS - text_rows - half)


def crossing_copy(source, target, slot, chunk, send_sem, recv_sem, number):
    first, count = chunk
    return pltpu.make_async_remote_copy(
        src_ref=source.at[pl.ds(first, count)],
        dst_ref=target.at[slot, pl.ds(first, count)],
        send_sem=send_sem.at[number],
        recv_sem=recv_sem.at[number],
        device_id=tower_partner(),
        device_id_type=MESH,
    )


def entry_kernel(
    text_rows, states_ref, proj_ref, proj_bias_ref, cls_ref, gain_ref, shift_ref, qkv_hbm, bias_ref,
    joined_ref, first_ref, qkv_ref, arrived, leaving, qkv_weight, load_sem, send_sem, recv_sem,
):
    side = lax.axis_index("tower")
    width = joined_ref.shape[1]
    barrier = pltpu.get_barrier_semaphore()
    pl.semaphore_signal(barrier, inc=1, device_id=tower_partner(), device_id_type=MESH)
    load = pltpu.make_async_copy(qkv_hbm, qkv_weight, load_sem)
    load.start()
    pl.semaphore_wait(barrier, 1)

    def project(rows):
        return (dot(rows, proj_ref[...]) + proj_bias_ref[...]).astype(BF16)

    def copy(own, slot, number):
        chunk = chunks_of(own, text_rows)[number]
        return crossing_copy(leaving, arrived, slot, chunk, send_sem, recv_sem, number)

    half = text_rows // 2
    for number in range(2):
        rows = pl.ds(number * half, half)
        leaving[rows, :] = project(states_ref[1 - side, rows, :])
        for own in range(2):

            @pl.when(side == own)
            def _():
                copy(own, own, number).start()

    arrived[side] = project(states_ref[side])
    load.wait()

    def process(first, count):
        rows = pl.ds(first, count)
        if first < text_rows:
            block = arrived[1, rows, :].astype(F32)
        else:
            block = arrived[0, pl.ds(first - text_rows, count), :].astype(F32)
            row = first + lax.broadcasted_iota(jnp.int32, block.shape, 0)
            block = jnp.where(row == text_rows + PATCH_BIG, cls_ref[...], block)
            block = jnp.where(row > text_rows + PATCH_BIG, 0.0, block)
        joined_ref[rows, :] = block
        scaled, _ = normalize(block)
        normed = (scaled * gain_ref[...] + shift_ref[...]).astype(BF16)
        first_ref[rows, :] = normed
        for part in range(3):
            columns = slice(part * width, (part + 1) * width)
            product = dot(normed, qkv_weight[:, columns]) + bias_ref[:, columns]
            qkv_ref[rows, columns] = (product * SCALE if part == 0 else product).astype(BF16)

    for own in range(2):

        @pl.when(side == own)
        def _():
            if own == 1:
                process(0, text_rows)
            else:
                process(text_rows, ROWS - text_rows)
            for number in range(2):
                other = 1 - own
                copy(other, other, number).wait_recv()
                first, count = chunks_of(other, text_rows)[number]
                process(first if other == 1 else text_rows + first, count)
            for number in range(2):
                copy(own, own, number).wait_send()


def entry(states, proj_weight, proj_bias, cls_row, gain, shift, qkv_weight, qkv_bias):
    text_rows, width = states.shape[1:]
    return pl.pallas_call(
        functools.partial(entry_kernel, text_rows),
        out_shape=(
            jax.ShapeDtypeStruct((ROWS, width), F32),
            jax.ShapeDtypeStruct((ROWS, width), BF16),
            jax.ShapeDtypeStruct((ROWS, 3 * width), BF16),
        ),
        in_specs=in_vmem(6) + anywhere() + in_vmem(),
        out_specs=tuple(in_vmem(3)),
        scratch_shapes=[
            pltpu.VMEM((2, text_rows, width), BF16),
            pltpu.VMEM((text_rows, width), BF16),
            pltpu.VMEM(qkv_weight.shape, BF16),
            pltpu.SemaphoreType.DMA,
            pltpu.SemaphoreType.DMA((2,)),
            pltpu.SemaphoreType.DMA((2,)),
        ],
        compiler_params=pltpu.CompilerParams(
            collective_id=0, has_side_effects=True, vmem_limit_bytes=40 << 20
        ),
        name="entry",
    )(states, proj_weight, proj_bias, cls_row, gain, shift, qkv_weight, qkv_bias)


def attention_kernel(text_rows, group_ref, length_ref, qkv_ref, out_ref, total_ref, key_ref):
    width = out_ref.shape[1]
    key_ref[...] = key_lanes(group_ref[0, 0], length_ref[0, 0], text_rows)
    lane = lax.broadcasted_iota(jnp.int32, (ROWS, LANES), 1)
    plain = jnp.where(lane == 0, 1.0, 0.0).astype(BF16)

    @pl.loop(0, width // LANES)
    def pair(index):
        at = pl.multiple_of(index * LANES, LANES)
        queries = qkv_ref[:, pl.ds(at, LANES)]
        keys = qkv_ref[:, pl.ds(pl.multiple_of(width + at, LANES), LANES)]
        values = qkv_ref[:, pl.ds(pl.multiple_of(2 * width + at, LANES), LANES)]
        keys = jnp.concatenate([keys, key_ref[...]], axis=1)
        values = jnp.concatenate([values, key_ref[...]], axis=1)
        scores = []
        for head in range(2):
            own = jnp.concatenate([head_part(queries, head), plain], axis=1)
            scores.append(dot(own, keys, NT))
        outs, totals = [], []
        for head in range(2):
            row_max = jnp.max(scores[head], axis=1, keepdims=True)
            weights = jnp.exp(scores[head] - row_max).astype(BF16)
            mixed = dot(weights, values)
            row_total = mixed[:, LANES + 1 : LANES + 2]
            outs.append(mixed[:, :LANES] / row_total)
            totals.append(row_max + jnp.log(row_total))
        out_ref[:, pl.ds(at, LANES)] = jnp.where(lane < HEAD_DIM, outs[0], outs[1]).astype(BF16)
        total_ref[index] = jnp.where(lane < HEAD_DIM, totals[0], totals[1])


def attention(text_rows, group, length, qkv):
    width = qkv.shape[1] // 3
    pairs = width // LANES
    return pl.pallas_call(
        functools.partial(attention_kernel, text_rows),
        out_shape=(
            jax.ShapeDtypeStruct((ROWS, width), BF16),
            jax.ShapeDtypeStruct((pairs, ROWS, LANES), F32),
            jax.ShapeDtypeStruct((ROWS, LANES), BF16),
        ),
        in_specs=in_smem(2) + in_vmem(),
        out_specs=tuple(in_vmem(3)),
        compiler_params=pltpu.CompilerParams(vmem_limit_bytes=52 << 20),
        name="attention_forward",
    )(group, length, qkv)


def middle_kernel(
    text_rows, group_ref, length_ref, joined_ref, attended_ref, given_ref,
    out_hbm, up_hbm, down_hbm, out_bias_ref, gain_ref, shift_ref, up_bias_ref, down_bias_ref,
    layer_ref, grad_middle_ref, grad_attended_ref, vector_ref, grads_hbm,
    out_weight, up_weight, down_weight, wide, result, grad_second, normed, across, grad_low, grads,
    load_sem, store_sem,
):
    width = joined_ref.shape[1]
    hidden = up_weight.shape[1]
    extent = given_ref.shape[0]
    parts = hidden // width
    share = width // GROUPS
    text_end, image_end = text_rows, text_rows + PATCH_BIG
    loads = [
        pltpu.make_async_copy(source, target, load_sem.at[number])
        for number, (source, target) in enumerate(
            ((out_hbm, out_weight), (up_hbm, up_weight), (down_hbm, down_weight))
        )
    ]
    for load in loads:
        load.start()

    def store(unit):
        return pltpu.make_async_copy(grads.at[unit], grads_hbm.at[unit], store_sem.at[unit])

    mask = live_rows((ROWS, 1), group_ref[0, 0], length_ref[0, 0], text_rows).astype(F32)
    wide[0:extent, :] = given_ref[...].astype(F32)
    result[0:text_end, :] = wide[1 + PATCH_BIG : extent, :]
    result[text_end:image_end, :] = wide[1 : 1 + PATCH_BIG, :]
    result[image_end:extent, :] = wide[0:1, :]
    result[extent:ROWS, :] = jnp.zeros((ROWS - extent, width), F32)
    grad_result = result[...] * mask
    grad_low[...] = grad_result.astype(BF16)
    vector_ref[0:1, :] = column_sum(grad_result)
    loads[0].wait()
    middle = joined_ref[...] + (dot(attended_ref[...], out_weight[...]) + out_bias_ref[...])
    scaled, inverse = normalize(middle)
    second = scaled * gain_ref[...] + shift_ref[...]
    normed[...] = second.astype(BF16)
    across[...] = second.T.astype(BF16)
    wide[...] = scaled
    result[...] = middle + down_bias_ref[...]
    grad_second[...] = jnp.zeros_like(grad_second)
    loads[1].wait()
    loads[2].wait()

    @pl.loop(0, parts)
    def tile(part):
        columns = pl.ds(pl.multiple_of(part * width, width), width)
        up, down = up_weight[:, columns], down_weight[columns, :]
        before = dot(normed[...], up) + up_bias_ref[:, columns]
        below = 0.5 + 0.5 * lax.erf(before * 0.7071067811865476)
        density = jnp.exp(-0.5 * before * before) * 0.3989422804014327
        activated = (before * below).astype(BF16)
        grad_hidden = dot(grad_low[...], down, NT) * (below + before * density)
        hidden_low = grad_hidden.astype(BF16)
        result[...] += dot(activated, down)
        grad_second[...] += dot(hidden_low, up, NT)
        vector_ref[pl.ds(1 + part, 1), :] = column_sum(hidden_low.astype(F32))
        grads[part] = dot(across[...], hidden_low).astype(BF16).reshape(GROUPS, share, width)
        store(part).start()
        down_grad = dot(activated, grad_low[...], TN).astype(BF16)
        rows = GROUPS // parts
        for group in range(rows):
            for piece in range(parts):
                first = (group * parts + piece) * share
                grads[parts + piece, pl.ds(part * rows + group, 1)] = down_grad[
                    first : first + share
                ].reshape(1, share, width)

    for piece in range(parts):
        store(parts + piece).start()
    result[...] = result[...] * mask
    second_grad = grad_second[...]
    scaled = wide[...]
    vector_ref[1 + parts : 2 + parts, :] = column_sum(second_grad * scaled)
    vector_ref[2 + parts : 3 + parts, :] = column_sum(second_grad)
    second_grad = second_grad * gain_ref[...]
    grad_middle = grad_low[...].astype(F32) + inverse * (
        second_grad - row_mean(second_grad) - scaled * row_mean(second_grad * scaled)
    )
    grad_middle_ref[...] = grad_middle
    grad_branch = grad_middle.astype(BF16)
    vector_ref[3 + parts : 4 + parts, :] = column_sum(grad_branch.astype(F32))
    out_grad = dot(attended_ref[...], grad_branch, TN).astype(BF16)
    grads[2 * parts] = out_grad.reshape(GROUPS, share, width)
    store(2 * parts).start()
    grad_attended_ref[...] = dot(grad_branch, out_weight[...], NT).astype(BF16)
    wide[0:1, :] = result[image_end:extent, :]
    wide[1 : 1 + PATCH_BIG, :] = result[text_end:image_end, :]
    wide[1 + PATCH_BIG : extent, :] = result[0:text_end, :]
    layer_ref[...] = wide[0:extent, :].astype(BF16)
    for unit in range(2 * parts + 1):
        store(unit).wait()


def middle_layer(
    text_rows, group, length, joined, attended, given, out_weight, up_weight, down_weight,
    out_bias, gain, shift, up_bias, down_bias,
):
    width, hidden = up_weight.shape
    parts = hidden // width
    units = 2 * parts + 1
    share = width // GROUPS
    return pl.pallas_call(
        functools.partial(middle_kernel, text_rows),
        out_shape=(
            jax.ShapeDtypeStruct(given.shape, BF16),
            jax.ShapeDtypeStruct((ROWS, width), F32),
            jax.ShapeDtypeStruct((ROWS, width), BF16),
            jax.ShapeDtypeStruct((4 + parts, width), F32),
            jax.ShapeDtypeStruct((units, GROUPS, share, width), BF16),
        ),
        in_specs=in_smem(2) + in_vmem(3) + anywhere(3) + in_vmem(5),
        out_specs=tuple(in_vmem(4) + anywhere()),
        scratch_shapes=[
            pltpu.VMEM(out_weight.shape, BF16),
            pltpu.VMEM(up_weight.shape, BF16),
            pltpu.VMEM(down_weight.shape, BF16),
            pltpu.VMEM((ROWS, width), F32),
            pltpu.VMEM((ROWS, width), F32),
            pltpu.VMEM((ROWS, width), F32),
            pltpu.VMEM((ROWS, width), BF16),
            pltpu.VMEM((width, ROWS), BF16),
            pltpu.VMEM((ROWS, width), BF16),
            pltpu.VMEM((units, GROUPS, share, width), BF16),
            pltpu.SemaphoreType.DMA((3,)),
            pltpu.SemaphoreType.DMA((units,)),
        ],
        compiler_params=pltpu.CompilerParams(vmem_limit_bytes=60 << 20),
        name="middle_layer",
    )(
        group, length, joined, attended, given, out_weight, up_weight, down_weight,
        out_bias, gain, shift, up_bias, down_bias,
    )


class Reducer:
    def __init__(self, bits, early, shared, refs):
        (
            self.grads, self.late, self.landed, self.crossing, self.crossed, self.held, self.sums,
            self.load_sem, self.send_sem, self.recv_sem,
        ) = refs
        self.bits, self.early, self.shared = bits, early, shared
        self.units = early + self.late.shape[0]
        self.partners = [item_partner(bit) for bit in range(bits)]

    def greet(self):
        barrier = pltpu.get_barrier_semaphore()
        for partner, _ in self.partners:
            pl.semaphore_signal(barrier, inc=1, device_id=partner, device_id_type=MESH)

    def part(self, ref, first, bit, side):
        return ref.at[(first,) + (slice(None),) * (self.bits - 1 - bit) + (side,)]

    def slot(self, unit):
        return lax.rem(unit, SLOTS)

    def is_late(self, unit):
        return isinstance(unit, int) and unit >= self.early

    def load(self, unit):
        slot = lax.rem(unit, 2)
        return pltpu.make_async_copy(
            self.part(self.grads, unit, 0, self.partners[0][1]),
            self.held.at[slot],
            self.load_sem.at[slot],
        )

    def send(self, unit, step):
        partner = tower_partner()
        if step == self.bits:
            source, target = self.crossing.at[unit], self.crossed.at[unit]
        else:
            partner, low = self.partners[step]
            target = self.landed[step].at[self.slot(unit)]
            if step:
                source = self.part(self.landed[step - 1], self.slot(unit), step, 1 - low)
            elif self.is_late(unit):
                source = self.part(self.late, unit - self.early, 0, 1 - low)
            else:
                source = self.part(self.grads, unit, 0, 1 - low)
        return pltpu.make_async_remote_copy(
            src_ref=source,
            dst_ref=target,
            send_sem=self.send_sem.at[unit, step],
            recv_sem=self.recv_sem.at[unit, step],
            device_id=partner,
            device_id_type=MESH,
        )

    def add(self, unit, step):
        low = self.partners[step][1]
        if step:
            mine = self.part(self.landed[step - 1], self.slot(unit), step, low)
        elif self.is_late(unit):
            mine = self.part(self.late, unit - self.early, 0, low)
        else:
            self.load(unit).wait()
            mine = self.held.at[lax.rem(unit, 2)]
        there = self.landed[step].at[self.slot(unit)]
        depth = self.bits - 1 - step

        @pl.loop(0, 1 << depth)
        def _(number):
            place = tuple(lax.rem(number // (1 << low_bit), 2) for low_bit in reversed(range(depth)))
            total = mine[place].astype(F32) + there[place].astype(F32)
            if step < self.bits - 1:
                there[place] = total.astype(BF16)
            else:
                self.crossing[unit] = total.astype(BF16)
                self.sums[unit] = total

    def settle(self, unit, step):
        self.send(unit, step).wait()
        if step == self.bits:
            self.sums[unit] = self.crossing[unit].astype(F32) + self.crossed[unit].astype(F32)
            return
        self.add(unit, step)
        if step + 1 < self.bits:
            self.send(unit, step + 1).start()
        elif isinstance(unit, int):
            if unit < self.shared:
                self.send(unit, step + 1).start()
        else:
            self.send(unit, step + 1).start()

    def wave(self, number):
        fixed = isinstance(number, int)
        for step in reversed(range(self.bits + 1)):
            unit = number - 1 - step
            if fixed:
                if 0 <= unit < (self.units if step < self.bits else self.shared):
                    self.settle(unit, step)
            else:
                pl.when(unit >= 0)(functools.partial(self.settle, unit, step))
        if not fixed or number < self.units:
            if not self.is_late(number):
                self.load(number).start()
            self.send(number, 0).start()


def back_kernel(text_rows, bits, early, *refs):
    (
        key_ref, states_ref, proj_ref, gain_ref, vector_ref,
        qkv_hbm, total_hbm, attended_hbm, grad_attended_hbm, first_hbm, joined_hbm, grad_middle_hbm,
        qkv_weight_hbm, grads,
        state_grad_ref, sums, line_out,
        grad_qkv, qkv_weight, across, late, returned, leaving, proj_grad, lines,
        load_sem, pair_sem, send_sem, recv_sem,
    ) = refs[:29]
    reducing = bits > 0
    width = states_ref.shape[2]
    pairs = width // LANES
    share = width // GROUPS
    per_unit = 2
    side = lax.axis_index("tower")
    reducer = None
    if reducing:
        landed = refs[29 : 29 + bits]
        crossing, crossed, held, held_sem, unit_send, unit_recv = refs[29 + bits : 35 + bits]
        line_here, line_there, line_send, line_recv = refs[35 + bits :]
        reducer = Reducer(
            bits, early, early + late.shape[0] - 1,
            (grads, late, landed, crossing, crossed, held, sums, held_sem, unit_send, unit_recv),
        )
        reducer.greet()

    def wave(number):
        if reducing:
            reducer.wave(number)

    barrier = pltpu.get_barrier_semaphore()
    pl.semaphore_signal(barrier, inc=1, device_id=tower_partner(), device_id_type=MESH)
    weight_load = pltpu.make_async_copy(qkv_weight_hbm, qkv_weight, load_sem.at[0])

    def attention_phase(first, blocks, totals):
        def loads(index, slot):
            at = pl.multiple_of(index * LANES, LANES)
            sources = [
                qkv_hbm.at[:, pl.ds(at, LANES)],
                qkv_hbm.at[:, pl.ds(pl.multiple_of(width + at, LANES), LANES)],
                qkv_hbm.at[:, pl.ds(pl.multiple_of(2 * width + at, LANES), LANES)],
                attended_hbm.at[:, pl.ds(at, LANES)],
                grad_attended_hbm.at[:, pl.ds(at, LANES)],
            ]
            copies = [
                pltpu.make_async_copy(source, blocks.at[slot, number], pair_sem.at[slot, number])
                for number, source in enumerate(sources)
            ]
            copies.append(
                pltpu.make_async_copy(
                    total_hbm.at[index], totals.at[slot], pair_sem.at[slot, len(sources)]
                )
            )
            return copies

        first_load = pltpu.make_async_copy(first_hbm, first, load_sem.at[1])
        for copy in loads(0, 0):
            copy.start()
        first_load.start()
        weight_load.start()
        pl.semaphore_wait(barrier, bits + 1)
        first_load.wait()
        across[...] = first[...].T

        @pl.loop(0, pairs)
        def pair(index):
            slot = lax.rem(index, 2)
            for copy in loads(index, slot):
                copy.wait()

            @pl.when(index + 1 < pairs)
            def _():
                for copy in loads(index + 1, 1 - slot):
                    copy.start()

            at = pl.multiple_of(index * LANES, LANES)
            key_at = pl.multiple_of(width + at, LANES)
            value_at = pl.multiple_of(2 * width + at, LANES)
            queries, keys, values = blocks[slot, 0], blocks[slot, 1], blocks[slot, 2]
            back = blocks[slot, 4]
            product = back.astype(F32) * blocks[slot, 3].astype(F32)
            wide_keys = jnp.concatenate([keys, key_ref[...]], axis=1)
            wide_values = jnp.concatenate([values, key_ref[...]], axis=1)
            keys_across = keys.T
            query_grad, key_grad, value_grad = [], None, None
            for head in range(2):
                own_queries = head_part(queries, head)
                own_back = head_part(back, head)
                log_total = totals[slot, :, HEAD_DIM * head : HEAD_DIM * head + 1]
                inner = jnp.sum(head_part(product, head), axis=1, keepdims=True)
                left = jnp.concatenate([own_queries, query_lanes(1.0, log_total)], axis=1)
                right = jnp.concatenate([own_back, query_lanes(0.0, inner)], axis=1)
                weights = jnp.exp(dot(wide_keys, left, NT))
                score_grad = (weights * dot(wide_values, right, NT)).astype(BF16)
                value_part = dot(weights.astype(BF16), own_back)
                key_part = dot(score_grad, own_queries)
                value_grad = value_part if value_grad is None else value_grad + value_part
                key_grad = key_part if key_grad is None else key_grad + key_part
                query_grad.append(
                    dot(keys_across[HEAD_DIM * head : HEAD_DIM * (head + 1)], score_grad)
                )
            query_grad = (SCALE * jnp.concatenate(query_grad, axis=0).T).astype(BF16)
            key_grad, value_grad = key_grad.astype(BF16), value_grad.astype(BF16)
            grad_qkv[:, pl.ds(at, LANES)] = query_grad
            grad_qkv[:, pl.ds(key_at, LANES)] = key_grad
            grad_qkv[:, pl.ds(value_at, LANES)] = value_grad
            lines[3:4, pl.ds(at, LANES)] = column_sum(query_grad.astype(F32))
            lines[4:5, pl.ds(at, LANES)] = column_sum(value_grad.astype(F32))
            both = jnp.concatenate([query_grad, key_grad, value_grad], axis=1)
            weight_grad = dot(across[...], both).astype(BF16)
            weight_grad = weight_grad.reshape((GROUPS, share, 3 * LANES))
            for place in range(per_unit):

                @pl.when(lax.rem(index, per_unit) == place)
                def _():
                    columns = slice(3 * LANES * place, 3 * LANES * (place + 1))
                    store_unit(index // per_unit, weight_grad, columns)

            wave(index)

    def store_unit(unit, block, columns):
        if not reducing:
            late[unit, :, :, columns] = block
            return
        for number in range(GROUPS):
            place = tuple((number >> bit) & 1 for bit in reversed(range(bits)))
            late[(unit,) + place + (slice(None), columns)] = block[number]

    pl.run_scoped(
        attention_phase,
        pltpu.VMEM((ROWS, width), BF16),
        pltpu.VMEM((2, 5, ROWS, LANES), BF16),
        pltpu.VMEM((2, ROWS, LANES), F32),
    )

    def copy(own, slot, number):
        chunk = chunks_of(own, text_rows)[number]
        return crossing_copy(leaving, returned, slot, chunk, send_sem, recv_sem, number)

    def row_phase(joined, grad_middle):
        joined_load = pltpu.make_async_copy(joined_hbm, joined, load_sem.at[1])
        middle_load = pltpu.make_async_copy(grad_middle_hbm, grad_middle, load_sem.at[2])
        joined_load.start()
        middle_load.start()
        weight_load.wait()
        joined_load.wait()
        middle_load.wait()
        lines[1:3, :] = jnp.zeros((2, width), F32)

        def rows_back(first, count):
            rows = pl.ds(first, count)
            grad_first = dot(grad_qkv[rows, :], qkv_weight[...], NT)
            scaled, inverse = normalize(joined[rows, :])
            lines[1:2, :] += column_sum(grad_first * scaled)
            lines[2:3, :] += column_sum(grad_first)
            grad_first = grad_first * gain_ref[...]
            grad_joined = grad_middle[rows, :] + inverse * (
                grad_first - row_mean(grad_first) - scaled * row_mean(grad_first * scaled)
            )
            if first + count == ROWS:
                cls = text_rows + PATCH_BIG - first
                lines[0:1, :] = grad_joined[cls : cls + 1, :]
                row = lax.broadcasted_iota(jnp.int32, grad_joined.shape, 0)
                grad_joined = jnp.where(row < cls, grad_joined, 0.0)
            return grad_joined.astype(BF16)

        for own in range(2):

            @pl.when(side == own)
            def _():
                sent = 1 - own
                for number, (first, count) in enumerate(chunks_of(sent, text_rows)):
                    start = first if sent == 1 else text_rows + first
                    leaving[first : first + count, :] = rows_back(start, count)
                    copy(sent, own, number).start()
                if own == 1:
                    returned[1] = rows_back(0, text_rows)
                else:
                    kept = ROWS - text_rows
                    returned[0, 0:kept, :] = rows_back(text_rows, kept)
                    for home in range(2):
                        returned[home, kept:text_rows, :] = jnp.zeros(
                            (text_rows - kept, width), BF16
                        )

    pl.run_scoped(row_phase, pltpu.VMEM((ROWS, width), F32), pltpu.VMEM((ROWS, width), F32))

    step = pairs
    wave(step)
    kept = returned[side]
    proj_grad[...] = dot(states_ref[side], kept, TN)
    state_grad_ref[side] = dot(kept, proj_ref[...], NT).astype(BF16)
    lines[13:14, :] = column_sum(kept.astype(F32))
    wave(step + 1)
    wave(step + 2)
    for own in range(2):

        @pl.when(side == own)
        def _():
            for number in range(2):
                copy(own, 1 - own, number).wait_recv()
                copy(1 - own, own, number).wait_send()

    arrived = returned[1 - side]
    total = proj_grad[...] + dot(states_ref[1 - side], arrived, TN)
    store_unit(late.shape[0] - 1, total.astype(BF16).reshape(GROUPS, share, width), slice(0, width))
    lines[13:14, :] += column_sum(arrived.astype(F32))
    parts = vector_ref.shape[0] - 4
    lines[5:6, :] = vector_ref[3 + parts : 4 + parts, :]
    lines[6:8, :] = vector_ref[1 + parts : 3 + parts, :]
    lines[8 : 8 + parts, :] = vector_ref[1 : 1 + parts, :]
    lines[8 + parts : 9 + parts, :] = vector_ref[0:1, :]
    state_grad_ref[1 - side] = dot(arrived, proj_ref[...], NT).astype(BF16)
    if not reducing:
        line_out[...] = lines[...]
        sums[...] = late[...]
        return

    def line_copy(number):
        partner = reducer.partners[number][0] if number < bits else tower_partner()
        return pltpu.make_async_remote_copy(
            src_ref=line_here.at[number],
            dst_ref=line_there.at[number],
            send_sem=line_send.at[number],
            recv_sem=line_recv.at[number],
            device_id=partner,
            device_id_type=MESH,
        )

    def line_step(number):
        line_copy(number).wait()
        total = line_here[number] + line_there[number]
        if number < bits:
            line_here[number + 1] = total
            line_copy(number + 1).start()
        else:
            row = lax.broadcasted_iota(jnp.int32, total.shape, 0)
            line_out[...] = jnp.where(row == 13, line_here[number], total)

    line_here[0] = lines[...]
    line_copy(0).start()
    number = 0
    last = reducer.units + bits
    for at in range(step + 3, last + 1):
        wave(at)
        if number <= bits and at > step + 3:
            line_step(number)
            number += 1
    for rest in range(number, bits + 1):
        line_step(rest)


def back_layer(
    text_rows, bits, keys, states, proj_weight, gain, vectors, qkv, log_total, attended,
    grad_attended, first_normed, joined, grad_middle, qkv_weight, grads,
):
    width = states.shape[2]
    share = width // GROUPS
    early, later = grads.shape[0], width // LANES // 2 + 1
    units = early + later
    whole = (2,) * bits if bits else (GROUPS,)
    line_shape = (VECTOR_ROWS, width)
    steps = bits + 1
    reducing = []
    if bits:
        reducing = [
            pltpu.VMEM((SLOTS,) + (2,) * (bits - 1 - step) + (share, width), BF16)
            for step in range(bits)
        ] + [
            pltpu.VMEM((units, share, width), BF16),
            pltpu.VMEM((units, share, width), BF16),
            pltpu.VMEM((2,) + (2,) * (bits - 1) + (share, width), BF16),
            pltpu.SemaphoreType.DMA((2,)),
            pltpu.SemaphoreType.DMA((units, steps)),
            pltpu.SemaphoreType.DMA((units, steps)),
            pltpu.VMEM((steps,) + line_shape, F32),
            pltpu.VMEM((steps,) + line_shape, F32),
            pltpu.SemaphoreType.DMA((steps,)),
            pltpu.SemaphoreType.DMA((steps,)),
        ]
    sums = (units, share, width) if bits else (later, GROUPS, share, width)
    return pl.pallas_call(
        functools.partial(back_kernel, text_rows, bits, early),
        out_shape=(
            jax.ShapeDtypeStruct(states.shape, BF16),
            jax.ShapeDtypeStruct(sums, F32 if bits else BF16),
            jax.ShapeDtypeStruct(line_shape, F32),
        ),
        in_specs=in_vmem(5) + anywhere(9),
        out_specs=tuple(in_vmem(3)),
        scratch_shapes=[
            pltpu.VMEM(qkv.shape, BF16),
            pltpu.VMEM(qkv_weight.shape, BF16),
            pltpu.VMEM((width, ROWS), BF16),
            pltpu.VMEM((later,) + whole + (share, width), BF16),
            pltpu.VMEM((2, text_rows, width), BF16),
            pltpu.VMEM((text_rows, width), BF16),
            pltpu.VMEM((width, width), F32),
            pltpu.VMEM(line_shape, F32),
            pltpu.SemaphoreType.DMA((3,)),
            pltpu.SemaphoreType.DMA((2, 6)),
            pltpu.SemaphoreType.DMA((2,)),
            pltpu.SemaphoreType.DMA((2,)),
        ]
        + reducing,
        compiler_params=pltpu.CompilerParams(
            collective_id=1, has_side_effects=True, vmem_limit_bytes=60 << 20
        ),
        name="back_layer",
    )(
        keys, states, proj_weight, gain, vectors, qkv, log_total, attended, grad_attended,
        first_normed, joined, grad_middle, qkv_weight, grads.reshape((early,) + whole + (share, width)),
    )


def spread_kernel(layout, sums_ref, lines_ref, *outs):
    me = lax.axis_index("items")
    rows, width = sums_ref.shape[1:]
    for (kind, first, count), out_ref in zip(layout, outs):
        if kind == "columns":
            for part in range(count):
                out_ref[:, part * width : (part + 1) * width] = sums_ref[first + part]
        elif kind == "heads":
            for part in range(count):
                for place in range(2):
                    for which in range(3):
                        source = (3 * place + which) * LANES
                        target = which * width + (2 * part + place) * LANES
                        out_ref[:, target : target + LANES] = sums_ref[
                            first + part, :, source : source + LANES
                        ]
        elif kind == "rows":
            for part in range(count):
                out_ref[part * rows : (part + 1) * rows, :] = sums_ref[first + part]
        else:
            line = jnp.concatenate(
                [lines_ref[first + part : first + part + 1, :] for part in range(count)], axis=1
            )
            share = out_ref.shape[1]
            line = jnp.broadcast_to(line, (8, line.shape[1]))
            line = pltpu.roll(line, lax.rem(line.shape[1] - me * share, line.shape[1]), 1)
            out_ref[...] = line[0:1, :share]


def spread(layout, shapes, sums, lines):
    return pl.pallas_call(
        functools.partial(spread_kernel, layout),
        out_shape=tuple(jax.ShapeDtypeStruct(shape, F32) for shape in shapes),
        in_specs=in_vmem(2),
        out_specs=tuple(in_vmem(len(shapes))),
        compiler_params=pltpu.CompilerParams(vmem_limit_bytes=32 << 20),
        name="spread_shares",
    )(sums, lines)


def body(
    states,
    proj_weight,
    proj_bias,
    cls_row,
    norm1_gain,
    norm1_shift,
    qkv_weight,
    qv_bias,
    out_weight,
    out_bias,
    norm2_gain,
    norm2_shift,
    up_weight,
    up_bias,
    down_weight,
    down_bias,
    image_group,
    caption_len,
    out_grad,
):
    width = states.shape[-1]
    text_rows = states.shape[3]
    hidden = up_weight.shape[1]
    parts = hidden // width
    own_states = states.reshape(2, text_rows, width)
    gain = norm1_gain[None]
    qkv_bias = jnp.concatenate([qv_bias[:width], jnp.zeros((width,), F32), qv_bias[width:]])[None]
    joined, first_normed, qkv = entry(
        own_states, proj_weight[0], proj_bias, cls_row[None], gain, norm1_shift[None],
        qkv_weight, qkv_bias,
    )
    attended, log_total, keys = attention(text_rows, image_group, caption_len, qkv)
    layer_out, grad_middle, grad_attended, vectors, grads = middle_layer(
        text_rows, image_group, caption_len, joined, attended, out_grad[0, 0], out_weight,
        up_weight, down_weight, out_bias[None], norm2_gain[None], norm2_shift[None], up_bias[None],
        down_bias[None],
    )
    layer_out = layer_out[None, None]
    items = lax.axis_size("items")
    share = width // items
    bits = items.bit_length() - 1
    if items != GROUPS or share % TILE_ROWS:
        bits = 0
    state_grad, sums, lines = back_layer(
        text_rows, bits, keys, own_states, proj_weight[0], gain, vectors, qkv, log_total, attended,
        grad_attended, first_normed, joined, grad_middle, qkv_weight, grads,
    )
    state_grad = state_grad.reshape(states.shape)
    if not bits:
        return (layer_out, state_grad) + plain_sums(grads, sums, lines, parts)
    heads = width // LANES // 2
    last = 2 * parts + 1 + heads
    layout = (
        ("rows", last, 1), ("line", 9 + parts, 1), ("line", 0, 1), ("line", 1, 1),
        ("line", 2, 1), ("heads", 2 * parts + 1, heads), ("line", 3, 2), ("rows", 2 * parts, 1),
        ("line", 5, 1), ("line", 6, 1), ("line", 7, 1), ("columns", 0, parts),
        ("line", 8, parts), ("rows", parts, parts), ("line", 8 + parts, 1),
    )
    shapes = []
    for kind, _, number in layout:
        if kind == "columns":
            shapes.append((share, number * width))
        elif kind == "heads":
            shapes.append((share, 3 * width))
        elif kind == "rows":
            shapes.append((number * share, width))
        else:
            shapes.append((1, number * share))
    shares = spread(layout, shapes, sums, lines)
    shares = [
        piece.reshape(-1) if kind == "line" else piece
        for piece, (kind, _, _) in zip(shares, layout)
    ]
    return (layer_out, state_grad, shares[0][None], shares[1][None]) + tuple(shares[2:])


def plain_sums(grads, later, lines, parts):
    def over_items(part):
        return lax.psum_scatter(part.astype(F32), "items", scatter_dimension=0, tiled=True)

    def over_both(part):
        return lax.psum(over_items(part).astype(BF16), "tower").astype(F32)

    width = lines.shape[1]
    heads = later.shape[0] - 1
    up_grad = grads[:parts].transpose(1, 2, 0, 3).reshape(width, parts * width)
    down_grad = grads[parts : 2 * parts].transpose(1, 0, 2, 3).reshape(parts * width, width)
    out_grad = grads[2 * parts].reshape(width, width)
    qkv_grad = later[:heads].reshape(heads, width, 2, 3, LANES).transpose(1, 3, 0, 2, 4)
    qkv_grad = qkv_grad.reshape(width, 3 * width)
    return (
        over_items(later[heads].reshape(width, width))[None],
        over_items(lines[9 + parts])[None],
        over_both(lines[0]),
        over_both(lines[1]),
        over_both(lines[2]),
        over_both(qkv_grad),
        over_both(lines[3:5].reshape(-1)),
        over_both(out_grad),
        over_both(lines[5]),
        over_both(lines[6]),
        over_both(lines[7]),
        over_both(up_grad),
        over_both(lines[8 : 8 + parts].reshape(-1)),
        over_both(down_grad),
        over_both(lines[8 + parts]),
    )


def solution(mesh):
    in_specs = (
        P("tower", None, "items", None, None),
        P("tower", None, None),
        P("tower", None),
        P(),
        P(),
        P(),
        P(),
        P(),
        P(),
        P(),
        P(),
        P(),
        P(),
        P(),
        P(),
        P(),
        P("tower", "items"),
        P("tower", "items"),
        P("tower", "items", None, None),
    )
    out_specs = (
        P("tower", "items", None, None),
        P("tower", None, "items", None, None),
        P("tower", "items", None),
        P("tower", "items"),
        P("items"),
        P("items"),
        P("items"),
        P("items", None),
        P("items"),
        P("items", None),
        P("items"),
        P("items"),
        P("items"),
        P("items", None),
        P("items"),
        P("items", None),
        P("items"),
    )
    return jax.shard_map(body, mesh=mesh, in_specs=in_specs, out_specs=out_specs, check_vma=False)
```

```python
import functools

import jax
import jax.numpy as jnp
from jax import lax
from jax.experimental import pallas as pl
from jax.experimental.pallas import tpu as pltpu
from jax.sharding import PartitionSpec as P

HEADS = 12
HEAD_DIM = 64
PATCH_SMALL = 197
PATCH_BIG = 325
EPSILON = 1e-06
MASKED = -1000000000.0
SCALE = 0.125
ROWS = 896
LANES = 128
TILE_ROWS = 16
GROUPS = 16
SLOTS = 4
VECTOR_ROWS = 16

F32 = jnp.float32
BF16 = jnp.bfloat16
NN = (((1,), (0,)), ((), ()))
NT = (((1,), (1,)), ((), ()))
TN = (((0,), (0,)), ((), ()))
MESH = pl.DeviceIdType.MESH


def dot(left, right, numbers=NN):
    return lax.dot_general(left, right, numbers, preferred_element_type=F32)


def live_rows(shape, group, length, text_rows):
    row = lax.broadcasted_iota(jnp.int32, shape, 0)
    patches = PATCH_SMALL + (PATCH_BIG - PATCH_SMALL) * group
    image = (row >= text_rows) & (row < text_rows + patches)
    return (row < length) | image | (row == text_rows + PATCH_BIG)


def key_lanes(group, length, text_rows):
    lane = lax.broadcasted_iota(jnp.int32, (ROWS, LANES), 1)
    bias = jnp.where(live_rows((ROWS, LANES), group, length, text_rows), 0.0, MASKED)
    return jnp.where(lane == 0, bias, jnp.where(lane < 4, 1.0, 0.0)).astype(BF16)


def query_lanes(first, column):
    lane = lax.broadcasted_iota(jnp.int32, (ROWS, LANES), 1)
    upper = column.astype(BF16).astype(F32)
    rest = column - upper
    inner = rest.astype(BF16).astype(F32)
    lower = rest - inner
    lanes = jnp.where(lane == 0, first, 0.0)
    lanes = jnp.where(lane == 1, -upper, lanes)
    lanes = jnp.where(lane == 2, -inner, lanes)
    return jnp.where(lane == 3, -lower, lanes).astype(BF16)


def head_part(block, head):
    lane = lax.broadcasted_iota(jnp.int32, block.shape, 1)
    keep = lane < HEAD_DIM if head == 0 else lane >= HEAD_DIM
    return jnp.where(keep, block, jnp.zeros_like(block))


def column_sum(block):
    return jnp.sum(block, axis=0, keepdims=True)


def row_mean(block):
    return jnp.mean(block, axis=1, keepdims=True)


def normalize(block):
    centered = block - row_mean(block)
    inverse = lax.rsqrt(row_mean(centered * centered) + EPSILON)
    return centered * inverse, inverse


def in_vmem(count=1):
    return [pl.BlockSpec(memory_space=pltpu.VMEM)] * count


def in_smem(count=1):
    return [pl.BlockSpec(memory_space=pltpu.SMEM)] * count


def anywhere(count=1):
    return [pl.BlockSpec(memory_space=pl.ANY)] * count


def tower_partner():
    return {"tower": 1 - lax.axis_index("tower")}


def item_partner(bit):
    me = lax.axis_index("items")
    low = lax.rem(me // (1 << bit), 2)
    return {"items": me + (1 - 2 * low) * (1 << bit)}, low


def chunks_of(side, text_rows):
    half = text_rows // 2
    if side == 1:
        return (0, half), (half, half)
    return (0, half), (half, ROWS - text_rows - half)


def crossing_copy(source, target, slot, chunk, send_sem, recv_sem, number):
    first, count = chunk
    return pltpu.make_async_remote_copy(
        src_ref=source.at[pl.ds(first, count)],
        dst_ref=target.at[slot, pl.ds(first, count)],
        send_sem=send_sem.at[number],
        recv_sem=recv_sem.at[number],
        device_id=tower_partner(),
        device_id_type=MESH,
    )


def place_of(number, bits):
    if not bits:
        return (number,)
    if isinstance(number, int):
        return tuple((number >> bit) & 1 for bit in reversed(range(bits)))
    return tuple(lax.rem(number // (1 << bit), 2) for bit in reversed(range(bits)))


def entry_kernel(
    text_rows, states_hbm, proj_hbm, proj_bias_ref, cls_ref, gain_ref, shift_ref, qkv_hbm, bias_ref,
    joined_hbm, first_hbm, qkv_out_hbm,
    arrived, leaving, states, proj_weight, qkv_weight, joined, first_normed, qkv,
    load_sem, store_sem, send_sem, recv_sem,
):
    side = lax.axis_index("tower")
    width = joined.shape[1]
    barrier = pltpu.get_barrier_semaphore()
    pl.semaphore_signal(barrier, inc=1, device_id=tower_partner(), device_id_type=MESH)
    sources = (
        (proj_hbm, proj_weight),
        (states_hbm.at[1 - side], states.at[1 - side]),
        (states_hbm.at[side], states.at[side]),
        (qkv_hbm, qkv_weight),
    )
    loads = [
        pltpu.make_async_copy(source, target, load_sem.at[number])
        for number, (source, target) in enumerate(sources)
    ]
    for load in loads:
        load.start()
    pl.semaphore_wait(barrier, 1)

    def project(rows):
        return (dot(rows, proj_weight[...]) + proj_bias_ref[...]).astype(BF16)

    def copy(own, slot, number):
        chunk = chunks_of(own, text_rows)[number]
        return crossing_copy(leaving, arrived, slot, chunk, send_sem, recv_sem, number)

    half = text_rows // 2
    loads[0].wait()
    loads[1].wait()
    for number in range(2):
        rows = pl.ds(number * half, half)
        leaving[rows, :] = project(states[1 - side, rows, :])
        for own in range(2):

            @pl.when(side == own)
            def _():
                copy(own, own, number).start()

    loads[2].wait()
    arrived[side] = project(states[side])
    loads[3].wait()

    def stores(first, count, number):
        rows = pl.ds(first, count)
        return [
            pltpu.make_async_copy(source.at[rows], target.at[rows], store_sem.at[number, place])
            for place, (source, target) in enumerate(
                ((joined, joined_hbm), (first_normed, first_hbm), (qkv, qkv_out_hbm))
            )
        ]

    def process(first, count, number):
        rows = pl.ds(first, count)
        if first < text_rows:
            block = arrived[1, rows, :].astype(F32)
        else:
            block = arrived[0, pl.ds(first - text_rows, count), :].astype(F32)
            row = first + lax.broadcasted_iota(jnp.int32, block.shape, 0)
            block = jnp.where(row == text_rows + PATCH_BIG, cls_ref[...], block)
            block = jnp.where(row > text_rows + PATCH_BIG, 0.0, block)
        joined[rows, :] = block
        scaled, _ = normalize(block)
        normed = (scaled * gain_ref[...] + shift_ref[...]).astype(BF16)
        first_normed[rows, :] = normed
        for part in range(3):
            columns = slice(part * width, (part + 1) * width)
            product = dot(normed, qkv_weight[:, columns]) + bias_ref[:, columns]
            qkv[rows, columns] = (product * SCALE if part == 0 else product).astype(BF16)
        for store in stores(first, count, number):
            store.start()

    for own in range(2):

        @pl.when(side == own)
        def _():
            other = 1 - own
            kept = (0, text_rows) if own == 1 else (text_rows, ROWS - text_rows)
            order = [kept]
            for first, count in chunks_of(other, text_rows):
                order.append((first if other == 1 else text_rows + first, count))
            for number, (first, count) in enumerate(order):
                if number:
                    copy(other, other, number - 1).wait_recv()
                process(first, count, number)
            for number in range(2):
                copy(own, own, number).wait_send()
            for number, (first, count) in enumerate(order):
                for store in stores(first, count, number):
                    store.wait()


def entry(states, proj_weight, proj_bias, cls_row, gain, shift, qkv_weight, qkv_bias):
    text_rows, width = states.shape[1:]
    shapes = (((ROWS, width), F32), ((ROWS, width), BF16), ((ROWS, 3 * width), BF16))
    return pl.pallas_call(
        functools.partial(entry_kernel, text_rows),
        out_shape=tuple(jax.ShapeDtypeStruct(shape, kind) for shape, kind in shapes),
        in_specs=anywhere(2) + in_vmem(4) + anywhere() + in_vmem(),
        out_specs=tuple(anywhere(3)),
        scratch_shapes=[
            pltpu.VMEM((2, text_rows, width), BF16),
            pltpu.VMEM((text_rows, width), BF16),
            pltpu.VMEM((2, text_rows, width), BF16),
            pltpu.VMEM(proj_weight.shape, BF16),
            pltpu.VMEM(qkv_weight.shape, BF16),
        ]
        + [pltpu.VMEM(shape, kind) for shape, kind in shapes]
        + [
            pltpu.SemaphoreType.DMA((4,)),
            pltpu.SemaphoreType.DMA((3, 3)),
            pltpu.SemaphoreType.DMA((2,)),
            pltpu.SemaphoreType.DMA((2,)),
        ],
        compiler_params=pltpu.CompilerParams(
            collective_id=0, has_side_effects=True, vmem_limit_bytes=56 << 20
        ),
        name="entry",
    )(states, proj_weight, proj_bias, cls_row, gain, shift, qkv_weight, qkv_bias)


def attention_kernel(
    text_rows, group_ref, length_ref, qkv_hbm, out_hbm, total_hbm,
    blocks, outs, totals, keys_ref, load_sem, store_sem,
):
    pairs = total_hbm.shape[0]
    width = pairs * LANES

    def loads(index, slot):
        return [
            pltpu.make_async_copy(
                qkv_hbm.at[:, pl.ds(pl.multiple_of(part * width + index * LANES, LANES), LANES)],
                blocks.at[slot, part],
                load_sem.at[slot, part],
            )
            for part in range(3)
        ]

    def stores(index, slot):
        columns = pl.ds(pl.multiple_of(index * LANES, LANES), LANES)
        return [
            pltpu.make_async_copy(outs.at[slot], out_hbm.at[:, columns], store_sem.at[slot, 0]),
            pltpu.make_async_copy(totals.at[slot], total_hbm.at[index], store_sem.at[slot, 1]),
        ]

    for load in loads(0, 0):
        load.start()
    keys_ref[...] = key_lanes(group_ref[0, 0], length_ref[0, 0], text_rows)
    lane = lax.broadcasted_iota(jnp.int32, (ROWS, LANES), 1)
    plain = jnp.where(lane == 0, 1.0, 0.0).astype(BF16)

    @pl.loop(0, pairs)
    def pair(index):
        slot = lax.rem(index, 2)
        for load in loads(index, slot):
            load.wait()

        @pl.when(index + 1 < pairs)
        def _():
            for load in loads(index + 1, 1 - slot):
                load.start()

        queries = blocks[slot, 0]
        keys = jnp.concatenate([blocks[slot, 1], keys_ref[...]], axis=1)
        values = jnp.concatenate([blocks[slot, 2], keys_ref[...]], axis=1)
        scores = []
        for head in range(2):
            own = jnp.concatenate([head_part(queries, head), plain], axis=1)
            scores.append(dot(own, keys, NT))
        mixes, logs = [], []
        for head in range(2):
            row_max = jnp.max(scores[head], axis=1, keepdims=True)
            weights = jnp.exp(scores[head] - row_max).astype(BF16)
            mixed = dot(weights, values)
            row_total = mixed[:, LANES + 1 : LANES + 2]
            mixes.append(mixed[:, :LANES] / row_total)
            logs.append(row_max + jnp.log(row_total))

        @pl.when(index >= 2)
        def _():
            for store in stores(index - 2, slot):
                store.wait()

        outs[slot] = jnp.where(lane < HEAD_DIM, mixes[0], mixes[1]).astype(BF16)
        totals[slot] = jnp.where(lane < HEAD_DIM, logs[0], logs[1])
        for store in stores(index, slot):
            store.start()

    for index in (pairs - 2, pairs - 1):
        for store in stores(index, index % 2):
            store.wait()


def attention(text_rows, group, length, qkv):
    width = qkv.shape[1] // 3
    pairs = width // LANES
    return pl.pallas_call(
        functools.partial(attention_kernel, text_rows),
        out_shape=(
            jax.ShapeDtypeStruct((ROWS, width), BF16),
            jax.ShapeDtypeStruct((pairs, ROWS, LANES), F32),
        ),
        in_specs=in_smem(2) + anywhere(),
        out_specs=tuple(anywhere(2)),
        scratch_shapes=[
            pltpu.VMEM((2, 3, ROWS, LANES), BF16),
            pltpu.VMEM((2, ROWS, LANES), BF16),
            pltpu.VMEM((2, ROWS, LANES), F32),
            pltpu.VMEM((ROWS, LANES), BF16),
            pltpu.SemaphoreType.DMA((2, 3)),
            pltpu.SemaphoreType.DMA((2, 2)),
        ],
        compiler_params=pltpu.CompilerParams(vmem_limit_bytes=52 << 20),
        name="attention_forward",
    )(group, length, qkv)


class Reducer:
    def __init__(self, bits, early, units, refs):
        (
            self.grads, self.late, self.landed, self.crossing, self.crossed, self.held, self.sums,
            self.load_sem, self.send_sem, self.recv_sem,
        ) = refs
        self.bits, self.early, self.units = bits, early, units
        self.partners = [item_partner(bit) for bit in range(bits)]

    def greet(self):
        barrier = pltpu.get_barrier_semaphore()
        for partner, _ in self.partners:
            pl.semaphore_signal(barrier, inc=1, device_id=partner, device_id_type=MESH)

    def part(self, ref, first, bit, side):
        return ref.at[(first,) + (slice(None),) * (self.bits - 1 - bit) + (side,)]

    def load(self, unit):
        slot = lax.rem(unit, 2)
        return pltpu.make_async_copy(
            self.part(self.grads, unit, 0, self.partners[0][1]),
            self.held.at[slot],
            self.load_sem.at[slot],
        )

    def send(self, unit, step, late=False):
        slot = lax.rem(unit, SLOTS)
        partner = tower_partner()
        if step == self.bits:
            source, target = self.crossing.at[unit], self.crossed.at[unit]
        else:
            partner, low = self.partners[step]
            target = self.landed[step].at[slot]
            if step:
                source = self.part(self.landed[step - 1], slot, step, 1 - low)
            elif late:
                source = self.part(self.late, unit - self.early, 0, 1 - low)
            else:
                source = self.part(self.grads, unit, 0, 1 - low)
        return pltpu.make_async_remote_copy(
            src_ref=source,
            dst_ref=target,
            send_sem=self.send_sem.at[unit, step],
            recv_sem=self.recv_sem.at[unit, step],
            device_id=partner,
            device_id_type=MESH,
        )

    def add(self, mine, there, depth, last):
        @pl.loop(0, 1 << depth)
        def _(number):
            place = place_of(number, depth) if depth else ()
            if last is None:
                there[place] = mine[place] + there[place]
            else:
                self.crossing[last] = (
                    mine[...].astype(F32) + there[...].astype(F32)
                ).astype(BF16)

    def settle(self, unit, step, late=False):
        self.send(unit, step, late).wait()
        if step == self.bits:
            self.sums[unit] = self.crossing[unit].astype(F32) + self.crossed[unit].astype(F32)
            return
        low = self.partners[step][1]
        slot = lax.rem(unit, SLOTS)
        if step:
            mine = self.part(self.landed[step - 1], slot, step, low)
        elif late:
            mine = self.part(self.late, unit - self.early, 0, low)
        else:
            self.load(unit).wait()
            mine = self.held.at[lax.rem(unit, 2)]
        depth = self.bits - 1 - step
        self.add(mine, self.landed[step].at[slot], depth, None if depth else unit)
        self.send(unit, step + 1).start()

    def begin(self, unit, late=False):
        if not late:
            self.load(unit).start()
        self.send(unit, 0, late).start()

    def either(self, act, unit, late):
        if isinstance(unit, int):
            act(late=unit >= self.early)
        elif not late:
            act(late=False)
        else:
            pl.when(unit < self.early)(functools.partial(act, late=False))
            pl.when(unit >= self.early)(functools.partial(act, late=True))

    def wave(self, number, late=False):
        fixed = isinstance(number, int)
        for step in reversed(range(self.bits + 1)):
            unit = number - 1 - step
            if fixed:
                if not 0 <= unit < self.units:
                    continue

            def go():
                if step:
                    self.settle(unit, step)
                else:
                    self.either(functools.partial(self.settle, unit, 0), unit, late)

            if fixed:
                go()
            else:
                pl.when(unit >= 0)(go)
        if not fixed or number < self.units:
            self.either(functools.partial(self.begin, number), number, late)


class LastReducer:
    def __init__(self, bits, orders, refs):
        (self.late, self.landed, self.crossing, self.crossed, self.sums, self.send_sem, self.recv_sem) = refs
        self.bits, self.orders = bits, orders
        self.partners = [item_partner(bit) for bit in range(bits)]

    def part(self, step, unit, mine):
        bit = self.orders[unit][step]
        ahead = sum(1 for other in self.orders[unit][step:] if other > bit)
        partner, low = self.partners[bit]
        side = low if mine else 1 - low
        ref = self.landed[step - 1].at[unit] if step else self.late[unit]
        return ref.at[(slice(None),) * ahead + (side,)], partner

    def send(self, unit, step):
        source, partner = self.part(step, unit, False)
        return pltpu.make_async_remote_copy(
            src_ref=source,
            dst_ref=self.landed[step].at[unit],
            send_sem=self.send_sem.at[unit, step],
            recv_sem=self.recv_sem.at[unit, step],
            device_id=partner,
            device_id_type=MESH,
        )

    def settle(self, step):
        for unit in range(2):
            self.send(unit, step).wait()
            mine, _ = self.part(step, unit, True)
            there = self.landed[step].at[unit]
            depth = self.bits - 1 - step
            if depth:

                @pl.loop(0, 1 << depth)
                def _(number):
                    place = place_of(number, depth)
                    there[place] = mine[place] + there[place]

                self.send(unit, step + 1).start()
            else:
                self.crossing[unit] = (mine[...].astype(F32) + there[...].astype(F32)).astype(BF16)

    def cross(self):
        side = lax.axis_index("tower")
        return pltpu.make_async_remote_copy(
            src_ref=self.crossing.at[1 - side],
            dst_ref=self.crossed,
            send_sem=self.send_sem.at[0, self.bits],
            recv_sem=self.recv_sem.at[0, self.bits],
            device_id=tower_partner(),
            device_id_type=MESH,
        )

    def finish(self):
        side = lax.axis_index("tower")
        self.cross().wait()
        self.sums[self.sums.shape[0] - 1] = self.crossing[side].astype(F32) + self.crossed[
            ...
        ].astype(F32)


def layer_kernel(text_rows, bits, *refs):
    refs = list(refs)

    def take(count):
        taken = refs[:count]
        del refs[:count]
        return taken

    (
        group_ref, length_ref, out_bias_ref, gain2_ref, shift2_ref, up_bias_ref, down_bias_ref,
        gain1_ref,
    ) = take(8)
    (
        joined_hbm, attended_hbm, given_hbm, out_weight_hbm, up_weight_hbm, down_weight_hbm,
        qkv_hbm, total_hbm, first_hbm, qkv_weight_hbm, states_hbm, proj_hbm,
    ) = take(12)
    layer_hbm, state_grad_hbm, sums, line_out, grads_hbm, middle_hbm = take(6)
    keys_ref, grad_attended, returned, leaving, foreign, lines = take(6)
    load_sem, store_sem, pair_sem, send_sem, recv_sem = take(5)
    reducing = bits > 0
    width = joined_hbm.shape[1]
    extent = given_hbm.shape[0]
    hidden = up_weight_hbm.shape[1]
    parts = hidden // width
    pairs = width // LANES
    heads = pairs // 2
    share = width // GROUPS
    early = 2 * parts + 1
    whole = (2,) * bits if bits else (GROUPS,)
    unit_shape = whole + (share, width)
    text_end, image_end = text_rows, text_rows + PATCH_BIG
    side = lax.axis_index("tower")
    barrier = pltpu.get_barrier_semaphore()
    pl.semaphore_signal(barrier, inc=1, device_id=tower_partner(), device_id_type=MESH)
    state = {"late": None}
    if reducing:
        landed, last_landed = take(bits), take(bits)
        (
            crossing, crossed, last_crossing, last_crossed, held, held_sem, unit_send, unit_recv,
            last_send, last_recv, line_here, line_there, line_send, line_recv,
        ) = take(14)

        def reducer_of(late):
            return Reducer(
                bits, early, early + heads,
                (grads_hbm, late, landed, crossing, crossed, held, sums, held_sem, unit_send, unit_recv),
            )

        reducer_of(None).greet()

    def wave(number, late=False):
        if reducing:
            reducer_of(state["late"]).wave(number, late)

    def local(source, target, sem):
        return pltpu.make_async_copy(source, target, sem)

    foreign_copy = pltpu.make_async_remote_copy(
        src_ref=states_hbm.at[1 - side],
        dst_ref=foreign,
        send_sem=send_sem.at[2],
        recv_sem=recv_sem.at[2],
        device_id=tower_partner(),
        device_id_type=MESH,
    )

    def middle_phase(
        out_weight, up_weight, down_weight, attended, given,
        wide, result, grad_second, normed, across, grad_low, up_stage, down_stage, out_stage,
    ):
        loads = [
            local(source, target, load_sem.at[number])
            for number, (source, target) in enumerate(
                (
                    (given_hbm, given), (out_weight_hbm, out_weight), (attended_hbm, attended),
                    (joined_hbm, grad_second), (up_weight_hbm, up_weight), (down_weight_hbm, down_weight),
                )
            )
        ]
        for load in loads:
            load.start()
        keys_ref[...] = key_lanes(group_ref[0, 0], length_ref[0, 0], text_rows)
        pl.semaphore_wait(barrier, bits + 1)
        foreign_copy.start()

        def store(unit):
            if isinstance(unit, int):
                source = out_stage if unit == 2 * parts else down_stage.at[unit - parts]
            else:
                source = up_stage.at[lax.rem(unit, 2)]
            return local(source, grads_hbm.at[unit], store_sem.at[unit])

        mask = live_rows((ROWS, 1), group_ref[0, 0], length_ref[0, 0], text_rows).astype(F32)
        loads[0].wait()
        wide[0:extent, :] = given[...].astype(F32)
        result[0:text_end, :] = wide[1 + PATCH_BIG : extent, :]
        result[text_end:image_end, :] = wide[1 : 1 + PATCH_BIG, :]
        result[image_end:extent, :] = wide[0:1, :]
        result[extent:ROWS, :] = jnp.zeros((ROWS - extent, width), F32)
        grad_result = result[...] * mask
        grad_low[...] = grad_result.astype(BF16)
        lines[8 + parts : 9 + parts, :] = column_sum(grad_result)
        for load in loads[1:4]:
            load.wait()
        middle = grad_second[...] + (dot(attended[...], out_weight[...]) + out_bias_ref[...])
        scaled, inverse = normalize(middle)
        second = scaled * gain2_ref[...] + shift2_ref[...]
        normed[...] = second.astype(BF16)
        across[...] = second.T.astype(BF16)
        wide[...] = scaled
        result[...] = middle + down_bias_ref[...]
        grad_second[...] = jnp.zeros_like(grad_second)
        for load in loads[4:]:
            load.wait()

        @pl.loop(0, parts)
        def tile(part):
            columns = pl.ds(pl.multiple_of(part * width, width), width)
            up, down = up_weight[:, columns], down_weight[columns, :]
            before = dot(normed[...], up) + up_bias_ref[:, columns]
            below = 0.5 + 0.5 * lax.erf(before * 0.7071067811865476)
            density = jnp.exp(-0.5 * before * before) * 0.3989422804014327
            activated = (before * below).astype(BF16)
            grad_hidden = dot(grad_low[...], down, NT) * (below + before * density)
            hidden_low = grad_hidden.astype(BF16)
            up_stage[lax.rem(part, 2)] = (
                dot(across[...], hidden_low).astype(BF16).reshape(unit_shape)
            )
            store(part).start()
            result[...] += dot(activated, down)
            grad_second[...] += dot(hidden_low, up, NT)
            lines[pl.ds(8 + part, 1), :] = column_sum(hidden_low.astype(F32))
            down_grad = dot(activated, grad_low[...], TN).astype(BF16)
            rows = GROUPS // parts
            for group in range(rows):
                for piece in range(parts):
                    first = (group * parts + piece) * share
                    place = place_of(part * rows + group, bits)
                    down_stage[(piece,) + place] = down_grad[first : first + share]
            store(part).wait()
            wave(part)

        for piece in range(parts):
            store(parts + piece).start()
        result[...] = result[...] * mask
        second_grad = grad_second[...]
        scaled = wide[...]
        lines[6:7, :] = column_sum(second_grad * scaled)
        lines[7:8, :] = column_sum(second_grad)
        second_grad = second_grad * gain2_ref[...]
        grad_middle = grad_low[...].astype(F32) + inverse * (
            second_grad - row_mean(second_grad) - scaled * row_mean(second_grad * scaled)
        )
        grad_second[...] = grad_middle
        middle_store = local(grad_second, middle_hbm, load_sem.at[0])
        middle_store.start()
        for piece in range(parts):
            store(parts + piece).wait()
        wave(parts)
        grad_branch = grad_middle.astype(BF16)
        lines[5:6, :] = column_sum(grad_branch.astype(F32))
        out_grad = dot(attended[...], grad_branch, TN).astype(BF16)
        out_stage[...] = out_grad.reshape(unit_shape)
        store(2 * parts).start()
        grad_attended[...] = dot(grad_branch, out_weight[...], NT).astype(BF16)
        wide[0:1, :] = result[image_end:extent, :]
        wide[1 : 1 + PATCH_BIG, :] = result[text_end:image_end, :]
        wide[1 + PATCH_BIG : extent, :] = result[0:text_end, :]
        given[...] = wide[0:extent, :].astype(BF16)
        layer_store = local(given, layer_hbm, load_sem.at[1])
        layer_store.start()
        wave(parts + 1)
        store(2 * parts).wait()
        middle_store.wait()
        layer_store.wait()

    pl.run_scoped(
        middle_phase,
        pltpu.VMEM((width, width), BF16),
        pltpu.VMEM((width, hidden), BF16),
        pltpu.VMEM((hidden, width), BF16),
        pltpu.VMEM((ROWS, width), BF16),
        pltpu.VMEM((extent, width), BF16),
        pltpu.VMEM((ROWS, width), F32),
        pltpu.VMEM((ROWS, width), F32),
        pltpu.VMEM((ROWS, width), F32),
        pltpu.VMEM((ROWS, width), BF16),
        pltpu.VMEM((width, ROWS), BF16),
        pltpu.VMEM((ROWS, width), BF16),
        pltpu.VMEM((2,) + unit_shape, BF16),
        pltpu.VMEM((parts,) + unit_shape, BF16),
        pltpu.VMEM(unit_shape, BF16),
    )

    def store_unit(late, unit, block, columns):
        for number in range(GROUPS):
            late[(unit,) + place_of(number, bits) + (slice(None), columns)] = block[number]

    def attention_phase(late, grad_qkv, first, across, blocks, totals):
        state["late"] = late

        def loads(index, slot):
            at = pl.multiple_of(index * LANES, LANES)
            sources = [
                qkv_hbm.at[:, pl.ds(at, LANES)],
                qkv_hbm.at[:, pl.ds(pl.multiple_of(width + at, LANES), LANES)],
                qkv_hbm.at[:, pl.ds(pl.multiple_of(2 * width + at, LANES), LANES)],
                attended_hbm.at[:, pl.ds(at, LANES)],
            ]
            copies = [
                local(source, blocks.at[slot, number], pair_sem.at[slot, number])
                for number, source in enumerate(sources)
            ]
            copies.append(
                local(total_hbm.at[index], totals.at[slot], pair_sem.at[slot, len(sources)])
            )
            return copies

        first_load = local(first_hbm, first, load_sem.at[1])
        for copy in loads(0, 0):
            copy.start()
        first_load.start()
        first_load.wait()
        across[...] = first[...].T

        @pl.loop(0, pairs)
        def pair(index):
            slot = lax.rem(index, 2)
            for copy in loads(index, slot):
                copy.wait()

            @pl.when(index + 1 < pairs)
            def _():
                for copy in loads(index + 1, 1 - slot):
                    copy.start()

            at = pl.multiple_of(index * LANES, LANES)
            key_at = pl.multiple_of(width + at, LANES)
            value_at = pl.multiple_of(2 * width + at, LANES)
            queries, keys, values = blocks[slot, 0], blocks[slot, 1], blocks[slot, 2]
            back = grad_attended[:, pl.ds(at, LANES)]
            product = back.astype(F32) * blocks[slot, 3].astype(F32)
            wide_keys = jnp.concatenate([keys, keys_ref[...]], axis=1)
            wide_values = jnp.concatenate([values, keys_ref[...]], axis=1)
            keys_across = keys.T
            query_grad, key_grad, value_grad = [], None, None
            for head in range(2):
                own_queries = head_part(queries, head)
                own_back = head_part(back, head)
                log_total = totals[slot, :, HEAD_DIM * head : HEAD_DIM * head + 1]
                inner = jnp.sum(head_part(product, head), axis=1, keepdims=True)
                left = jnp.concatenate([own_queries, query_lanes(1.0, log_total)], axis=1)
                right = jnp.concatenate([own_back, query_lanes(0.0, inner)], axis=1)
                weights = jnp.exp(dot(wide_keys, left, NT))
                score_grad = (weights * dot(wide_values, right, NT)).astype(BF16)
                value_part = dot(weights.astype(BF16), own_back)
                key_part = dot(score_grad, own_queries)
                value_grad = value_part if value_grad is None else value_grad + value_part
                key_grad = key_part if key_grad is None else key_grad + key_part
                query_grad.append(
                    dot(keys_across[HEAD_DIM * head : HEAD_DIM * (head + 1)], score_grad)
                )
            query_grad = (SCALE * jnp.concatenate(query_grad, axis=0).T).astype(BF16)
            key_grad, value_grad = key_grad.astype(BF16), value_grad.astype(BF16)
            grad_qkv[:, pl.ds(at, LANES)] = query_grad
            grad_qkv[:, pl.ds(key_at, LANES)] = key_grad
            grad_qkv[:, pl.ds(value_at, LANES)] = value_grad
            lines[3:4, pl.ds(at, LANES)] = column_sum(query_grad.astype(F32))
            lines[4:5, pl.ds(at, LANES)] = column_sum(value_grad.astype(F32))
            both = jnp.concatenate([query_grad, key_grad, value_grad], axis=1)
            weight_grad = dot(across[...], both).astype(BF16)
            weight_grad = weight_grad.reshape((GROUPS, share, 3 * LANES))
            for place in range(2):

                @pl.when(lax.rem(index, 2) == place)
                def _():
                    columns = slice(3 * LANES * place, 3 * LANES * (place + 1))
                    store_unit(late, index // 2, weight_grad, columns)

            wave(parts + 2 + index, late=True)

    def copy(own, slot, number):
        chunk = chunks_of(own, text_rows)[number]
        return crossing_copy(leaving, returned, slot, chunk, send_sem, recv_sem, number)

    def row_phase(grad_qkv, qkv_weight, joined, grad_middle):
        loads = [
            local(qkv_weight_hbm, qkv_weight, load_sem.at[0]),
            local(joined_hbm, joined, load_sem.at[1]),
            local(middle_hbm, grad_middle, load_sem.at[2]),
        ]
        for load in loads:
            load.start()
        for load in loads:
            load.wait()
        lines[1:3, :] = jnp.zeros((2, width), F32)

        def rows_back(first, count):
            rows = pl.ds(first, count)
            grad_first = dot(grad_qkv[rows, :], qkv_weight[...], NT)
            scaled, inverse = normalize(joined[rows, :])
            lines[1:2, :] += column_sum(grad_first * scaled)
            lines[2:3, :] += column_sum(grad_first)
            grad_first = grad_first * gain1_ref[...]
            grad_joined = grad_middle[rows, :] + inverse * (
                grad_first - row_mean(grad_first) - scaled * row_mean(grad_first * scaled)
            )
            if first + count == ROWS:
                cls = text_rows + PATCH_BIG - first
                lines[0:1, :] = grad_joined[cls : cls + 1, :]
                row = lax.broadcasted_iota(jnp.int32, grad_joined.shape, 0)
                grad_joined = jnp.where(row < cls, grad_joined, 0.0)
            return grad_joined.astype(BF16)

        for own in range(2):

            @pl.when(side == own)
            def _():
                sent = 1 - own
                for number, (first, count) in enumerate(chunks_of(sent, text_rows)):
                    start = first if sent == 1 else text_rows + first
                    leaving[first : first + count, :] = rows_back(start, count)
                    copy(sent, own, number).start()
                if own == 1:
                    returned[1] = rows_back(0, text_rows)
                else:
                    kept = ROWS - text_rows
                    returned[0, 0:kept, :] = rows_back(text_rows, kept)
                    for home in range(2):
                        returned[home, kept:text_rows, :] = jnp.zeros(
                            (text_rows - kept, width), BF16
                        )

    def line_copy(number):
        partner = item_partner(number)[0] if number < bits else tower_partner()
        return pltpu.make_async_remote_copy(
            src_ref=line_here.at[number],
            dst_ref=line_there.at[number],
            send_sem=line_send.at[number],
            recv_sem=line_recv.at[number],
            device_id=partner,
            device_id_type=MESH,
        )

    def line_step(number):
        if not reducing:
            return
        line_copy(number).wait()
        total = line_here[number] + line_there[number]
        if number < bits:
            line_here[number + 1] = total
            line_copy(number + 1).start()
        else:
            line_out[...] = total

    def last_phase(late, last_late, states, proj_weight, state_grad):
        loads = [
            local(states_hbm.at[side], states, load_sem.at[0]),
            local(proj_hbm, proj_weight, load_sem.at[1]),
        ]
        for load in loads:
            load.start()
        foreign_copy.wait()
        for load in loads:
            load.wait()
        kept_rows = ROWS - text_rows
        last = None
        if reducing:
            last = LastReducer(
                bits, ((0, 1, 2, 3), (0, 2, 3, 1)),
                ((last_late.at[0], last_late.at[1]), last_landed, last_crossing, last_crossed, sums, last_send, last_recv),
            )
        for unit in range(2):
            for own in range(2):

                @pl.when(side == own)
                def _():
                    count = kept_rows if unit == 0 else text_rows
                    rows = pl.ds(0, count)
                    grad = returned[own, rows, :] if unit == own else leaving[rows, :]
                    given = states[rows, :] if unit == own else foreign[rows, :]
                    block = dot(given, grad, TN).astype(BF16)
                    last_late[unit] = block.reshape(unit_shape)
                    lines[13 + unit : 14 + unit, :] = column_sum(grad.astype(F32))

            if reducing:
                last.send(unit, 0).start()
        if reducing:
            line_here[0] = lines[...]
            line_copy(0).start()
        total_units = early + heads
        wave(total_units)
        state_grad[side] = dot(returned[side], proj_weight[...], NT).astype(BF16)
        grad_store = [
            local(state_grad.at[home], state_grad_hbm.at[home], load_sem.at[2 + number])
            for number, home in enumerate((side, 1 - side))
        ]
        grad_store[0].start()
        if reducing:
            last.settle(0)
        line_step(0)
        wave(total_units + 1)
        if reducing:
            last.settle(1)
        line_step(1)
        wave(total_units + 2)
        for own in range(2):

            @pl.when(side == own)
            def _():
                for number in range(2):
                    copy(own, 1 - own, number).wait_recv()
                    copy(1 - own, own, number).wait_send()

        state_grad[1 - side] = dot(returned[1 - side], proj_weight[...], NT).astype(BF16)
        grad_store[1].start()
        if reducing:
            last.settle(2)
        line_step(2)
        wave(total_units + 3)
        if reducing:
            last.settle(3)
            last.cross().start()
        line_step(3)
        wave(total_units + 4)
        line_step(4)
        if reducing:
            last.finish()
        else:
            line_out[...] = lines[...]
            sums[0:heads] = late[...]
            sums[heads : heads + 2] = last_late[...]
        for store in grad_store:
            store.wait()

    def late_phase(late):
        def qkv_phase(grad_qkv):
            pl.run_scoped(
                functools.partial(attention_phase, late, grad_qkv),
                pltpu.VMEM((ROWS, width), BF16),
                pltpu.VMEM((width, ROWS), BF16),
                pltpu.VMEM((2, 4, ROWS, LANES), BF16),
                pltpu.VMEM((2, ROWS, LANES), F32),
            )
            pl.run_scoped(
                functools.partial(row_phase, grad_qkv),
                pltpu.VMEM((width, 3 * width), BF16),
                pltpu.VMEM((ROWS, width), F32),
                pltpu.VMEM((ROWS, width), F32),
            )

        pl.run_scoped(qkv_phase, pltpu.VMEM((ROWS, 3 * width), BF16))
        pl.run_scoped(
            functools.partial(last_phase, late),
            pltpu.VMEM((2,) + unit_shape, BF16),
            pltpu.VMEM((text_rows, width), BF16),
            pltpu.VMEM((width, width), BF16),
            pltpu.VMEM((2, text_rows, width), BF16),
        )

    pl.run_scoped(late_phase, pltpu.VMEM((heads,) + unit_shape, BF16))


def layer(
    text_rows, bits, group, length, out_bias, gain2, shift2, up_bias, down_bias, gain1,
    joined, attended, given, out_weight, up_weight, down_weight, qkv, log_total, first_normed,
    qkv_weight, states, proj_weight,
):
    width, hidden = up_weight.shape
    parts = hidden // width
    share = width // GROUPS
    early, heads = 2 * parts + 1, width // LANES // 2
    units = early + heads
    whole = (2,) * bits if bits else (GROUPS,)
    line_shape = (VECTOR_ROWS, width)
    steps = bits + 1
    reducing = []
    if bits:
        for slots in (SLOTS, 2):
            reducing += [
                pltpu.VMEM((slots,) + (2,) * (bits - 1 - step) + (share, width), BF16)
                for step in range(bits)
            ]
        reducing += [
            pltpu.VMEM((units, share, width), BF16),
            pltpu.VMEM((units, share, width), BF16),
            pltpu.VMEM((2, share, width), BF16),
            pltpu.VMEM((share, width), BF16),
            pltpu.VMEM((2,) + (2,) * (bits - 1) + (share, width), BF16),
            pltpu.SemaphoreType.DMA((2,)),
            pltpu.SemaphoreType.DMA((units, steps)),
            pltpu.SemaphoreType.DMA((units, steps)),
            pltpu.SemaphoreType.DMA((2, steps)),
            pltpu.SemaphoreType.DMA((2, steps)),
            pltpu.VMEM((steps,) + line_shape, F32),
            pltpu.VMEM((steps,) + line_shape, F32),
            pltpu.SemaphoreType.DMA((steps,)),
            pltpu.SemaphoreType.DMA((steps,)),
        ]
    sums = (units + 1, share, width) if bits else (heads + 2, GROUPS, share, width)
    outs = pl.pallas_call(
        functools.partial(layer_kernel, text_rows, bits),
        out_shape=(
            jax.ShapeDtypeStruct(given.shape, BF16),
            jax.ShapeDtypeStruct(states.shape, BF16),
            jax.ShapeDtypeStruct(sums, F32 if bits else BF16),
            jax.ShapeDtypeStruct(line_shape, F32),
            jax.ShapeDtypeStruct((early,) + whole + (share, width), BF16),
            jax.ShapeDtypeStruct((ROWS, width), F32),
        ),
        in_specs=in_smem(2) + in_vmem(6) + anywhere(12),
        out_specs=tuple(anywhere(2) + in_vmem(2) + anywhere(2)),
        scratch_shapes=[
            pltpu.VMEM((ROWS, LANES), BF16),
            pltpu.VMEM((ROWS, width), BF16),
            pltpu.VMEM((2, text_rows, width), BF16),
            pltpu.VMEM((text_rows, width), BF16),
            pltpu.VMEM((text_rows, width), BF16),
            pltpu.VMEM(line_shape, F32),
            pltpu.SemaphoreType.DMA((6,)),
            pltpu.SemaphoreType.DMA((early,)),
            pltpu.SemaphoreType.DMA((2, 5)),
            pltpu.SemaphoreType.DMA((3,)),
            pltpu.SemaphoreType.DMA((3,)),
        ]
        + reducing,
        compiler_params=pltpu.CompilerParams(
            collective_id=1, has_side_effects=True, vmem_limit_bytes=62 << 20
        ),
        name="layer",
    )(
        group, length, out_bias, gain2, shift2, up_bias, down_bias, gain1,
        joined, attended, given, out_weight, up_weight, down_weight, qkv, log_total, first_normed,
        qkv_weight, states, proj_weight,
    )
    return outs[:5]


def spread_kernel(layout, sums_ref, lines_ref, *outs):
    me = lax.axis_index("items")
    rows, width = sums_ref.shape[1:]
    for (kind, first, count), out_ref in zip(layout, outs):
        if kind == "columns":
            for part in range(count):
                out_ref[:, part * width : (part + 1) * width] = sums_ref[first + part]
        elif kind == "heads":
            for part in range(count):
                for place in range(2):
                    for which in range(3):
                        source = (3 * place + which) * LANES
                        target = which * width + (2 * part + place) * LANES
                        out_ref[:, target : target + LANES] = sums_ref[
                            first + part, :, source : source + LANES
                        ]
        elif kind == "rows":
            for part in range(count):
                out_ref[part * rows : (part + 1) * rows, :] = sums_ref[first + part]
        else:
            line = jnp.concatenate(
                [lines_ref[first + part : first + part + 1, :] for part in range(count)], axis=1
            )
            if kind == "side":
                line = jnp.where(
                    lax.axis_index("tower") == 0,
                    lines_ref[first : first + 1, :],
                    lines_ref[first + 1 : first + 2, :],
                )
            share = out_ref.shape[1]
            line = jnp.broadcast_to(line, (8, line.shape[1]))
            line = pltpu.roll(line, lax.rem(line.shape[1] - me * share, line.shape[1]), 1)
            out_ref[...] = line[0:1, :share]


def spread(layout, shapes, sums, lines):
    return pl.pallas_call(
        functools.partial(spread_kernel, layout),
        out_shape=tuple(jax.ShapeDtypeStruct(shape, F32) for shape in shapes),
        in_specs=in_vmem(2),
        out_specs=tuple(in_vmem(len(shapes))),
        compiler_params=pltpu.CompilerParams(vmem_limit_bytes=32 << 20),
        name="spread_shares",
    )(sums, lines)


def body(
    states,
    proj_weight,
    proj_bias,
    cls_row,
    norm1_gain,
    norm1_shift,
    qkv_weight,
    qv_bias,
    out_weight,
    out_bias,
    norm2_gain,
    norm2_shift,
    up_weight,
    up_bias,
    down_weight,
    down_bias,
    image_group,
    caption_len,
    out_grad,
):
    width = states.shape[-1]
    text_rows = states.shape[3]
    hidden = up_weight.shape[1]
    parts = hidden // width
    own_states = states.reshape(2, text_rows, width)
    gain = norm1_gain[None]
    qkv_bias = jnp.concatenate([qv_bias[:width], jnp.zeros((width,), F32), qv_bias[width:]])[None]
    joined, first_normed, qkv = entry(
        own_states, proj_weight[0], proj_bias, cls_row[None], gain, norm1_shift[None],
        qkv_weight, qkv_bias,
    )
    attended, log_total = attention(text_rows, image_group, caption_len, qkv)
    items = lax.axis_size("items")
    share = width // items
    bits = items.bit_length() - 1
    if items != GROUPS or share % TILE_ROWS:
        bits = 0
    layer_out, state_grad, sums, lines, grads = layer(
        text_rows, bits, image_group, caption_len, out_bias[None], norm2_gain[None],
        norm2_shift[None], up_bias[None], down_bias[None], gain, joined, attended, out_grad[0, 0],
        out_weight, up_weight, down_weight, qkv, log_total, first_normed, qkv_weight, own_states,
        proj_weight[0],
    )
    layer_out = layer_out[None, None]
    state_grad = state_grad.reshape(states.shape)
    if not bits:
        return (layer_out, state_grad) + plain_sums(grads, sums, lines, parts)
    heads = width // LANES // 2
    last = 2 * parts + 1 + heads
    layout = (
        ("rows", last, 1), ("side", 9 + parts, 1), ("line", 0, 1), ("line", 1, 1),
        ("line", 2, 1), ("heads", 2 * parts + 1, heads), ("line", 3, 2), ("rows", 2 * parts, 1),
        ("line", 5, 1), ("line", 6, 1), ("line", 7, 1), ("columns", 0, parts),
        ("line", 8, parts), ("rows", parts, parts), ("line", 8 + parts, 1),
    )
    shapes = []
    for kind, _, number in layout:
        if kind == "columns":
            shapes.append((share, number * width))
        elif kind == "heads":
            shapes.append((share, 3 * width))
        elif kind == "rows":
            shapes.append((number * share, width))
        else:
            shapes.append((1, number * share))
    shares = spread(layout, shapes, sums, lines)
    shares = [
        piece.reshape(-1) if kind in ("line", "side") else piece
        for piece, (kind, _, _) in zip(shares, layout)
    ]
    return (layer_out, state_grad, shares[0][None], shares[1][None]) + tuple(shares[2:])


def plain_sums(grads, later, lines, parts):
    def over_items(part):
        return lax.psum_scatter(part.astype(F32), "items", scatter_dimension=0, tiled=True)

    def over_both(part):
        return lax.psum(over_items(part).astype(BF16), "tower").astype(F32)

    def over_sides(first, second):
        first, second = over_both(first), over_both(second)
        return jnp.where(lax.axis_index("tower") == 0, first, second)[None]

    width = lines.shape[1]
    heads = later.shape[0] - 2
    up_grad = grads[:parts].transpose(1, 2, 0, 3).reshape(width, parts * width)
    down_grad = grads[parts : 2 * parts].transpose(1, 0, 2, 3).reshape(parts * width, width)
    out_grad = grads[2 * parts].reshape(width, width)
    qkv_grad = later[:heads].reshape(heads, width, 2, 3, LANES).transpose(1, 3, 0, 2, 4)
    qkv_grad = qkv_grad.reshape(width, 3 * width)
    return (
        over_sides(later[heads].reshape(width, width), later[heads + 1].reshape(width, width)),
        over_sides(lines[9 + parts], lines[10 + parts]),
        over_both(lines[0]),
        over_both(lines[1]),
        over_both(lines[2]),
        over_both(qkv_grad),
        over_both(lines[3:5].reshape(-1)),
        over_both(out_grad),
        over_both(lines[5]),
        over_both(lines[6]),
        over_both(lines[7]),
        over_both(up_grad),
        over_both(lines[8 : 8 + parts].reshape(-1)),
        over_both(down_grad),
        over_both(lines[8 + parts]),
    )


def solution(mesh):
    in_specs = (
        P("tower", None, "items", None, None),
        P("tower", None, None),
        P("tower", None),
        P(),
        P(),
        P(),
        P(),
        P(),
        P(),
        P(),
        P(),
        P(),
        P(),
        P(),
        P(),
        P(),
        P("tower", "items"),
        P("tower", "items"),
        P("tower", "items", None, None),
    )
    out_specs = (
        P("tower", "items", None, None),
        P("tower", None, "items", None, None),
        P("tower", "items", None),
        P("tower", "items"),
        P("items"),
        P("items"),
        P("items"),
        P("items", None),
        P("items"),
        P("items", None),
        P("items"),
        P("items"),
        P("items"),
        P("items", None),
        P("items"),
        P("items", None),
        P("items"),
    )
    return jax.shard_map(body, mesh=mesh, in_specs=in_specs, out_specs=out_specs, check_vma=False)
```

```python
import functools

import jax
import jax.numpy as jnp
from jax import lax
from jax.experimental import pallas as pl
from jax.experimental.pallas import tpu as pltpu
from jax.sharding import PartitionSpec as P

HEADS = 12
HEAD_DIM = 64
PATCH_SMALL = 197
PATCH_BIG = 325
EPSILON = 1e-06
MASKED = -1000000000.0
SCALE = 0.125
ROWS = 896
LANES = 128
TILE_ROWS = 16
GROUPS = 16
STARTS = (0, 1, 3, 4, 5)
SLOTS = (5, 6, 4, 3)
VECTOR_ROWS = 16
LAST_ORDERS = ((0, 1, 2, 3), (0, 2, 3, 1))

F32 = jnp.float32
BF16 = jnp.bfloat16
NN = (((1,), (0,)), ((), ()))
NT = (((1,), (1,)), ((), ()))
TN = (((0,), (0,)), ((), ()))
MESH = pl.DeviceIdType.MESH


def dot(left, right, numbers=NN):
    return lax.dot_general(left, right, numbers, preferred_element_type=F32)


def live_rows(shape, group, length, text_rows):
    row = lax.broadcasted_iota(jnp.int32, shape, 0)
    patches = PATCH_SMALL + (PATCH_BIG - PATCH_SMALL) * group
    image = (row >= text_rows) & (row < text_rows + patches)
    return (row < length) | image | (row == text_rows + PATCH_BIG)


def key_lanes(group, length, text_rows):
    lane = lax.broadcasted_iota(jnp.int32, (ROWS, LANES), 1)
    bias = jnp.where(live_rows((ROWS, LANES), group, length, text_rows), 0.0, MASKED)
    return jnp.where(lane == 0, bias, jnp.where(lane < 4, 1.0, 0.0)).astype(BF16)


def query_lanes(first, column):
    lane = lax.broadcasted_iota(jnp.int32, (ROWS, LANES), 1)
    upper = column.astype(BF16).astype(F32)
    rest = column - upper
    inner = rest.astype(BF16).astype(F32)
    lower = rest - inner
    lanes = jnp.where(lane == 0, first, 0.0)
    lanes = jnp.where(lane == 1, -upper, lanes)
    lanes = jnp.where(lane == 2, -inner, lanes)
    return jnp.where(lane == 3, -lower, lanes).astype(BF16)


def head_part(block, head):
    lane = lax.broadcasted_iota(jnp.int32, block.shape, 1)
    keep = lane < HEAD_DIM if head == 0 else lane >= HEAD_DIM
    return jnp.where(keep, block, jnp.zeros_like(block))


def column_sum(block):
    return jnp.sum(block, axis=0, keepdims=True)


def line_of(ref):
    return ref[...].reshape(1, ref.shape[0])


def row_mean(block):
    return jnp.mean(block, axis=1, keepdims=True)


def normalize(block):
    centered = block - row_mean(block)
    inverse = lax.rsqrt(row_mean(centered * centered) + EPSILON)
    return centered * inverse, inverse


def in_vmem(count=1):
    return [pl.BlockSpec(memory_space=pltpu.VMEM)] * count


def in_smem(count=1):
    return [pl.BlockSpec(memory_space=pltpu.SMEM)] * count


def anywhere(count=1):
    return [pl.BlockSpec(memory_space=pl.ANY)] * count


def tower_partner():
    return {"tower": 1 - lax.axis_index("tower")}


def item_partner(bit):
    me = lax.axis_index("items")
    low = lax.rem(me // (1 << bit), 2)
    return {"items": me + (1 - 2 * low) * (1 << bit)}, low


def chunks_of(side, text_rows):
    half = text_rows // 2
    if side == 1:
        return (0, half), (half, half)
    return (0, half), (half, ROWS - text_rows - half)


def crossing_copy(source, target, slot, chunk, send_sem, recv_sem, number):
    first, count = chunk
    return pltpu.make_async_remote_copy(
        src_ref=source.at[pl.ds(first, count)],
        dst_ref=target.at[slot, pl.ds(first, count)],
        send_sem=send_sem.at[number],
        recv_sem=recv_sem.at[number],
        device_id=tower_partner(),
        device_id_type=MESH,
    )


def place_of(number, bits):
    if not bits:
        return (number,)
    if isinstance(number, int):
        return tuple((number >> bit) & 1 for bit in range(bits))
    return tuple(lax.rem(number // (1 << bit), 2) for bit in range(bits))


def entry_kernel(
    text_rows, states_hbm, proj_hbm, proj_bias_ref, cls_ref, gain_ref, shift_ref, qkv_hbm, bias_ref,
    joined_hbm, first_hbm, qkv_out_hbm,
    arrived, leaving, states, proj_weight, qkv_weight, joined, first_normed, qkv,
    load_sem, store_sem, send_sem, recv_sem,
):
    side = lax.axis_index("tower")
    width = joined.shape[1]
    barrier = pltpu.get_barrier_semaphore()
    pl.semaphore_signal(barrier, inc=1, device_id=tower_partner(), device_id_type=MESH)
    sources = (
        (proj_hbm, proj_weight),
        (states_hbm.at[1 - side], states.at[1 - side]),
        (states_hbm.at[side], states.at[side]),
        (qkv_hbm, qkv_weight),
    )
    loads = [
        pltpu.make_async_copy(source, target, load_sem.at[number])
        for number, (source, target) in enumerate(sources)
    ]
    for load in loads:
        load.start()
    pl.semaphore_wait(barrier, 1)

    def project(rows):
        return (dot(rows, proj_weight[...]) + proj_bias_ref[...]).astype(BF16)

    def copy(own, slot, number):
        chunk = chunks_of(own, text_rows)[number]
        return crossing_copy(leaving, arrived, slot, chunk, send_sem, recv_sem, number)

    half = text_rows // 2
    loads[0].wait()
    loads[1].wait()
    for number in range(2):
        rows = pl.ds(number * half, half)
        leaving[rows, :] = project(states[1 - side, rows, :])
        for own in range(2):

            @pl.when(side == own)
            def _():
                copy(own, own, number).start()

    loads[2].wait()
    arrived[side] = project(states[side])
    loads[3].wait()

    def stores(first, count, number):
        rows = pl.ds(first, count)
        return [
            pltpu.make_async_copy(source.at[rows], target.at[rows], store_sem.at[number, place])
            for place, (source, target) in enumerate(
                ((joined, joined_hbm), (first_normed, first_hbm), (qkv, qkv_out_hbm))
            )
        ]

    def process(first, count, number):
        rows = pl.ds(first, count)
        if first < text_rows:
            block = arrived[1, rows, :].astype(F32)
        else:
            block = arrived[0, pl.ds(first - text_rows, count), :].astype(F32)
            row = first + lax.broadcasted_iota(jnp.int32, block.shape, 0)
            block = jnp.where(row == text_rows + PATCH_BIG, line_of(cls_ref), block)
            block = jnp.where(row > text_rows + PATCH_BIG, 0.0, block)
        joined[rows, :] = block
        scaled, _ = normalize(block)
        normed = (scaled * line_of(gain_ref) + line_of(shift_ref)).astype(BF16)
        first_normed[rows, :] = normed
        for part in range(3):
            columns = slice(part * width, (part + 1) * width)
            product = dot(normed, qkv_weight[:, columns])
            if part == 0:
                product = (product + line_of(bias_ref)[:, :width]) * SCALE
            elif part == 2:
                product = product + line_of(bias_ref)[:, width:]
            qkv[rows, columns] = product.astype(BF16)
        for store in stores(first, count, number):
            store.start()

    for own in range(2):

        @pl.when(side == own)
        def _():
            other = 1 - own
            kept = (0, text_rows) if own == 1 else (text_rows, ROWS - text_rows)
            order = [kept]
            for first, count in chunks_of(other, text_rows):
                order.append((first if other == 1 else text_rows + first, count))
            for number, (first, count) in enumerate(order):
                if number:
                    copy(other, other, number - 1).wait_recv()
                process(first, count, number)
            for number in range(2):
                copy(own, own, number).wait_send()
            for number, (first, count) in enumerate(order):
                for store in stores(first, count, number):
                    store.wait()


def entry(states, proj_weight, proj_bias, cls_row, gain, shift, qkv_weight, qkv_bias):
    text_rows, width = states.shape[1:]
    shapes = (((ROWS, width), F32), ((ROWS, width), BF16), ((ROWS, 3 * width), BF16))
    return pl.pallas_call(
        functools.partial(entry_kernel, text_rows),
        out_shape=tuple(jax.ShapeDtypeStruct(shape, kind) for shape, kind in shapes),
        in_specs=anywhere(2) + in_vmem(4) + anywhere() + in_vmem(),
        out_specs=tuple(anywhere(3)),
        scratch_shapes=[
            pltpu.VMEM((2, text_rows, width), BF16),
            pltpu.VMEM((text_rows, width), BF16),
            pltpu.VMEM((2, text_rows, width), BF16),
            pltpu.VMEM(proj_weight.shape, BF16),
            pltpu.VMEM(qkv_weight.shape, BF16),
        ]
        + [pltpu.VMEM(shape, kind) for shape, kind in shapes]
        + [
            pltpu.SemaphoreType.DMA((4,)),
            pltpu.SemaphoreType.DMA((3, 3)),
            pltpu.SemaphoreType.DMA((2,)),
            pltpu.SemaphoreType.DMA((2,)),
        ],
        compiler_params=pltpu.CompilerParams(
            collective_id=0, has_side_effects=True, vmem_limit_bytes=56 << 20
        ),
        name="entry",
    )(states, proj_weight, proj_bias, cls_row, gain, shift, qkv_weight, qkv_bias)


def attention_kernel(
    text_rows, group_ref, length_ref, qkv_hbm, out_hbm, total_hbm,
    blocks, outs, totals, keys_ref, load_sem, store_sem,
):
    pairs = total_hbm.shape[0]
    width = pairs * LANES

    def loads(index, slot):
        return [
            pltpu.make_async_copy(
                qkv_hbm.at[:, pl.ds(pl.multiple_of(part * width + index * LANES, LANES), LANES)],
                blocks.at[slot, part],
                load_sem.at[slot, part],
            )
            for part in range(3)
        ]

    def stores(index, slot):
        columns = pl.ds(pl.multiple_of(index * LANES, LANES), LANES)
        return [
            pltpu.make_async_copy(outs.at[slot], out_hbm.at[:, columns], store_sem.at[slot, 0]),
            pltpu.make_async_copy(totals.at[slot], total_hbm.at[index], store_sem.at[slot, 1]),
        ]

    for load in loads(0, 0):
        load.start()
    keys_ref[...] = key_lanes(group_ref[0, 0], length_ref[0, 0], text_rows)
    lane = lax.broadcasted_iota(jnp.int32, (ROWS, LANES), 1)
    plain = jnp.where(lane == 0, 1.0, 0.0).astype(BF16)

    @pl.loop(0, pairs)
    def pair(index):
        slot = lax.rem(index, 2)
        for load in loads(index, slot):
            load.wait()

        @pl.when(index + 1 < pairs)
        def _():
            for load in loads(index + 1, 1 - slot):
                load.start()

        queries = blocks[slot, 0]
        keys = jnp.concatenate([blocks[slot, 1], keys_ref[...]], axis=1)
        values = jnp.concatenate([blocks[slot, 2], keys_ref[...]], axis=1)
        scores = []
        for head in range(2):
            own = jnp.concatenate([head_part(queries, head), plain], axis=1)
            scores.append(dot(own, keys, NT))
        mixes, logs = [], []
        for head in range(2):
            row_max = jnp.max(scores[head], axis=1, keepdims=True)
            weights = jnp.exp(scores[head] - row_max).astype(BF16)
            mixed = dot(weights, values)
            row_total = mixed[:, LANES + 1 : LANES + 2]
            mixes.append(mixed[:, :LANES] / row_total)
            logs.append(row_max + jnp.log(row_total))

        @pl.when(index >= 2)
        def _():
            for store in stores(index - 2, slot):
                store.wait()

        outs[slot] = jnp.where(lane < HEAD_DIM, mixes[0], mixes[1]).astype(BF16)
        totals[slot] = jnp.where(lane < HEAD_DIM, logs[0], logs[1])
        for store in stores(index, slot):
            store.start()

    for index in (pairs - 2, pairs - 1):
        for store in stores(index, index % 2):
            store.wait()


def attention(text_rows, group, length, qkv):
    width = qkv.shape[1] // 3
    pairs = width // LANES
    return pl.pallas_call(
        functools.partial(attention_kernel, text_rows),
        out_shape=(
            jax.ShapeDtypeStruct((ROWS, width), BF16),
            jax.ShapeDtypeStruct((pairs, ROWS, LANES), F32),
        ),
        in_specs=in_smem(2) + anywhere(),
        out_specs=tuple(anywhere(2)),
        scratch_shapes=[
            pltpu.VMEM((2, 3, ROWS, LANES), BF16),
            pltpu.VMEM((2, ROWS, LANES), BF16),
            pltpu.VMEM((2, ROWS, LANES), F32),
            pltpu.VMEM((ROWS, LANES), BF16),
            pltpu.SemaphoreType.DMA((2, 3)),
            pltpu.SemaphoreType.DMA((2, 2)),
        ],
        compiler_params=pltpu.CompilerParams(vmem_limit_bytes=52 << 20),
        name="attention_forward",
    )(group, length, qkv)


class Reducer:
    def __init__(self, bits, early, units, refs):
        (
            self.grads, self.late, self.landed, self.crossing, self.crossed, self.held, self.sums,
            self.load_sem, self.send_sem, self.recv_sem,
        ) = refs
        self.bits, self.early, self.units = bits, early, units
        self.partners = [item_partner(bit) for bit in range(bits)]

    def greet(self):
        barrier = pltpu.get_barrier_semaphore()
        for partner, _ in self.partners:
            pl.semaphore_signal(barrier, inc=1, device_id=partner, device_id_type=MESH)

    def part(self, ref, first, side):
        return ref.at[first, side]

    def load(self, unit):
        slot = lax.rem(unit, 2)
        return pltpu.make_async_copy(
            self.part(self.grads, unit, self.partners[0][1]),
            self.held.at[slot],
            self.load_sem.at[slot],
        )

    def send(self, unit, step, late=False):
        partner = tower_partner()
        if step == self.bits:
            source, target = self.crossing.at[unit], self.crossed.at[unit]
        else:
            partner, low = self.partners[step]
            target = self.landed[step].at[lax.rem(unit, SLOTS[step])]
            if step:
                source = self.part(
                    self.landed[step - 1], lax.rem(unit, SLOTS[step - 1]), 1 - low
                )
            elif late:
                source = self.part(self.late, unit - self.early, 1 - low)
            else:
                source = self.part(self.grads, unit, 1 - low)
        return pltpu.make_async_remote_copy(
            src_ref=source,
            dst_ref=target,
            send_sem=self.send_sem.at[unit, step],
            recv_sem=self.recv_sem.at[unit, step],
            device_id=partner,
            device_id_type=MESH,
        )

    def add(self, mine, there, depth, last):
        @pl.loop(0, 1 << depth)
        def _(number):
            place = place_of(number, depth) if depth else ()
            if last is None:
                there[place] = mine[place] + there[place]
            else:
                self.crossing[last] = (
                    mine[...].astype(F32) + there[...].astype(F32)
                ).astype(BF16)

    def settle(self, unit, step, late=False):
        self.send(unit, step, late).wait()
        low = self.partners[step][1]
        if step:
            mine = self.part(self.landed[step - 1], lax.rem(unit, SLOTS[step - 1]), low)
        elif late:
            mine = self.part(self.late, unit - self.early, low)
        else:
            self.load(unit).wait()
            mine = self.held.at[lax.rem(unit, 2)]
        depth = self.bits - 1 - step
        there = self.landed[step].at[lax.rem(unit, SLOTS[step])]
        self.add(mine, there, depth, None if depth else unit)
        self.send(unit, step + 1).start()

    def finish(self, first, last):
        @pl.loop(first, last)
        def _(unit):
            self.send(unit, self.bits).wait()
            self.sums[unit] = self.crossing[unit].astype(F32) + self.crossed[unit].astype(F32)

    def begin(self, unit, late=False):
        if not late:
            self.load(unit).start()
        self.send(unit, 0, late).start()

    def either(self, act, unit, late):
        if isinstance(unit, int):
            act(late=unit >= self.early)
        elif not late:
            act(late=False)
        else:
            pl.when(unit < self.early)(functools.partial(act, late=False))
            pl.when(unit >= self.early)(functools.partial(act, late=True))

    def wave(self, number, late=False):
        fixed = isinstance(number, int)
        for step in reversed(range(self.bits)):
            unit = number - STARTS[step + 1]
            if fixed:
                if not 0 <= unit < self.units:
                    continue

            def go():
                if step:
                    self.settle(unit, step)
                else:
                    self.either(functools.partial(self.settle, unit, 0), unit, late)

            if fixed:
                go()
            else:
                pl.when(unit >= 0)(go)
        if not fixed or number < self.units:
            self.either(functools.partial(self.begin, number), number, late)


class LastReducer:
    def __init__(self, bits, orders, refs):
        (
            self.late, self.landed, self.crossing, self.crossed, self.sums, self.send_sem, self.recv_sem,
        ) = refs
        self.bits, self.orders = bits, orders
        self.partners = [item_partner(bit) for bit in range(bits)]

    def part(self, step, unit, mine):
        bit = self.orders[unit][step]
        partner, low = self.partners[bit]
        side = low if mine else 1 - low
        ref = self.landed[step - 1].at[unit] if step else self.late.at[unit]
        return ref.at[side], partner

    def send(self, unit, step):
        source, partner = self.part(step, unit, False)
        return pltpu.make_async_remote_copy(
            src_ref=source,
            dst_ref=self.landed[step].at[unit],
            send_sem=self.send_sem.at[unit, step],
            recv_sem=self.recv_sem.at[unit, step],
            device_id=partner,
            device_id_type=MESH,
        )

    def settle(self, unit, step):
        self.send(unit, step).wait()
        mine, _ = self.part(step, unit, True)
        there = self.landed[step].at[unit]
        depth = self.bits - 1 - step
        if depth:

            @pl.loop(0, 1 << depth)
            def _(number):
                place = place_of(number, depth)
                there[place] = mine[place] + there[place]

            self.send(unit, step + 1).start()
        else:
            self.crossing[unit] = (mine[...].astype(F32) + there[...].astype(F32)).astype(BF16)
            if unit == 0:
                self.cross().start()

    def cross(self):
        return pltpu.make_async_remote_copy(
            src_ref=self.crossing.at[0],
            dst_ref=self.crossed,
            send_sem=self.send_sem.at[0, self.bits],
            recv_sem=self.recv_sem.at[0, self.bits],
            device_id=tower_partner(),
            device_id_type=MESH,
        )

    def finish(self):
        self.cross().wait()
        total = self.crossing[1].astype(F32) + self.crossed[...].astype(F32)
        self.sums[self.sums.shape[0] - 1] = total


def layer_kernel(text_rows, bits, *refs):
    refs = list(refs)

    def take(count):
        taken = refs[:count]
        del refs[:count]
        return taken

    (
        group_ref, length_ref, out_bias_ref, gain2_ref, shift2_ref, up_bias_ref, down_bias_ref,
        gain1_ref,
    ) = take(8)
    (
        joined_hbm, attended_hbm, given_hbm, out_weight_hbm, up_weight_hbm, down_weight_hbm,
        qkv_hbm, total_hbm, first_hbm, qkv_weight_hbm, states_hbm, proj_hbm,
    ) = take(12)
    layer_hbm, state_grad_hbm, sums, line_out, grads_hbm, middle_hbm = take(6)
    keys_ref, grad_attended, returned, leaving, foreign, lines = take(6)
    load_sem, store_sem, pair_sem, send_sem, recv_sem = take(5)
    reducing = bits > 0
    width = joined_hbm.shape[1]
    extent = given_hbm.shape[0]
    hidden = up_weight_hbm.shape[1]
    parts = hidden // width
    pairs = width // LANES
    heads = pairs // 2
    share = width // GROUPS
    early = 2 * parts + 1
    whole = (2,) * bits if bits else (GROUPS,)
    unit_shape = whole + (share, width)
    text_end, image_end = text_rows, text_rows + PATCH_BIG
    side = lax.axis_index("tower")
    barrier = pltpu.get_barrier_semaphore()
    pl.semaphore_signal(barrier, inc=1, device_id=tower_partner(), device_id_type=MESH)
    state = {"late": None}
    if reducing:
        landed, last_landed = take(bits), take(bits)
        (
            crossing, crossed, last_crossing, last_crossed, held, held_sem, unit_send, unit_recv,
            last_send, last_recv, line_here, line_there, line_send, line_recv,
        ) = take(14)

        def reducer_of(late):
            return Reducer(
                bits, early, early + heads,
                (grads_hbm, late, landed, crossing, crossed, held, sums, held_sem, unit_send, unit_recv),
            )

        reducer_of(None).greet()

    def wave(number, late=False):
        if reducing:
            reducer_of(state["late"]).wave(number, late)

    def fill(target, block, order=tuple(range(bits))):
        block = block.astype(BF16).reshape(GROUPS, share, width)
        for number in range(GROUPS):
            place = place_of(number, bits)
            if bits:
                place = tuple(place[bit] for bit in order)
            target[place] = block[number]

    def local(source, target, sem):
        return pltpu.make_async_copy(source, target, sem)

    foreign_copy = pltpu.make_async_remote_copy(
        src_ref=states_hbm.at[1 - side],
        dst_ref=foreign,
        send_sem=send_sem.at[2],
        recv_sem=recv_sem.at[2],
        device_id=tower_partner(),
        device_id_type=MESH,
    )

    def middle_phase(
        out_weight, up_weight, down_weight, attended, given,
        wide, result, grad_second, normed, across, grad_low, up_stage, down_stage, out_stage,
    ):
        loads = [
            local(source, target, load_sem.at[number])
            for number, (source, target) in enumerate(
                (
                    (given_hbm, given), (out_weight_hbm, out_weight), (attended_hbm, attended),
                    (joined_hbm, grad_second), (up_weight_hbm, up_weight), (down_weight_hbm, down_weight),
                )
            )
        ]
        for load in loads:
            load.start()
        keys_ref[...] = key_lanes(group_ref[0, 0], length_ref[0, 0], text_rows)
        pl.semaphore_wait(barrier, bits + 1)
        foreign_copy.start()

        def store(unit):
            if isinstance(unit, int):
                source = out_stage if unit == 2 * parts else down_stage.at[unit - parts]
            else:
                source = up_stage
            return local(source, grads_hbm.at[unit], store_sem.at[unit])

        mask = live_rows((ROWS, 1), group_ref[0, 0], length_ref[0, 0], text_rows).astype(F32)
        loads[0].wait()
        wide[0:extent, :] = given[...].astype(F32)
        result[0:text_end, :] = wide[1 + PATCH_BIG : extent, :]
        result[text_end:image_end, :] = wide[1 : 1 + PATCH_BIG, :]
        result[image_end:extent, :] = wide[0:1, :]
        result[extent:ROWS, :] = jnp.zeros((ROWS - extent, width), F32)
        grad_result = result[...] * mask
        grad_low[...] = grad_result.astype(BF16)
        lines[8 + parts : 9 + parts, :] = column_sum(grad_result)
        for load in loads[1:4]:
            load.wait()
        middle = grad_second[...] + (dot(attended[...], out_weight[...]) + line_of(out_bias_ref))
        scaled, inverse = normalize(middle)
        second = scaled * line_of(gain2_ref) + line_of(shift2_ref)
        normed[...] = second.astype(BF16)
        across[...] = second.T.astype(BF16)
        wide[...] = scaled
        result[...] = middle + line_of(down_bias_ref)
        grad_second[...] = jnp.zeros_like(grad_second)
        for load in loads[4:]:
            load.wait()

        @pl.loop(0, parts)
        def tile(part):
            columns = pl.ds(pl.multiple_of(part * width, width), width)
            up, down = up_weight[:, columns], down_weight[columns, :]
            before = dot(normed[...], up) + up_bias_ref[columns].reshape(1, width)
            below = 0.5 + 0.5 * lax.erf(before * 0.7071067811865476)
            density = jnp.exp(-0.5 * before * before) * 0.3989422804014327
            activated = (before * below).astype(BF16)
            grad_hidden = dot(grad_low[...], down, NT) * (below + before * density)
            hidden_low = grad_hidden.astype(BF16)
            fill(up_stage, dot(across[...], hidden_low))
            store(part).start()
            result[...] += dot(activated, down)
            grad_second[...] += dot(hidden_low, up, NT)
            lines[pl.ds(8 + part, 1), :] = column_sum(hidden_low.astype(F32))
            down_grad = dot(activated, grad_low[...], TN).astype(BF16)
            rows = GROUPS // parts
            for group in range(rows):
                for piece in range(parts):
                    first = (group * parts + piece) * share
                    place = place_of(part * rows + group, bits)
                    down_stage[(piece,) + place] = down_grad[first : first + share]
            store(part).wait()
            wave(part)

        for piece in range(parts):
            store(parts + piece).start()
        result[...] = result[...] * mask
        second_grad = grad_second[...]
        scaled = wide[...]
        lines[6:7, :] = column_sum(second_grad * scaled)
        lines[7:8, :] = column_sum(second_grad)
        second_grad = second_grad * line_of(gain2_ref)
        grad_middle = grad_low[...].astype(F32) + inverse * (
            second_grad - row_mean(second_grad) - scaled * row_mean(second_grad * scaled)
        )
        grad_second[...] = grad_middle
        middle_store = local(grad_second, middle_hbm, load_sem.at[0])
        middle_store.start()
        for piece in range(parts):
            store(parts + piece).wait()
        wave(parts)
        grad_branch = grad_middle.astype(BF16)
        lines[5:6, :] = column_sum(grad_branch.astype(F32))
        fill(out_stage, dot(attended[...], grad_branch, TN))
        store(2 * parts).start()
        grad_attended[...] = dot(grad_branch, out_weight[...], NT).astype(BF16)
        wide[0:1, :] = result[image_end:extent, :]
        wide[1 : 1 + PATCH_BIG, :] = result[text_end:image_end, :]
        wide[1 + PATCH_BIG : extent, :] = result[0:text_end, :]
        given[...] = wide[0:extent, :].astype(BF16)
        layer_store = local(given, layer_hbm, load_sem.at[1])
        layer_store.start()
        wave(parts + 1)
        store(2 * parts).wait()
        middle_store.wait()
        layer_store.wait()

    pl.run_scoped(
        middle_phase,
        pltpu.VMEM((width, width), BF16),
        pltpu.VMEM((width, hidden), BF16),
        pltpu.VMEM((hidden, width), BF16),
        pltpu.VMEM((ROWS, width), BF16),
        pltpu.VMEM((extent, width), BF16),
        pltpu.VMEM((ROWS, width), F32),
        pltpu.VMEM((ROWS, width), F32),
        pltpu.VMEM((ROWS, width), F32),
        pltpu.VMEM((ROWS, width), BF16),
        pltpu.VMEM((width, ROWS), BF16),
        pltpu.VMEM((ROWS, width), BF16),
        pltpu.VMEM(unit_shape, BF16),
        pltpu.VMEM((parts,) + unit_shape, BF16),
        pltpu.VMEM(unit_shape, BF16),
    )

    def store_unit(late, unit, block, columns):
        for number in range(GROUPS):
            late[(unit,) + place_of(number, bits) + (slice(None), columns)] = block[number]

    def attention_phase(late, grad_qkv, first, across, blocks, totals):
        state["late"] = late

        def loads(index, slot):
            at = pl.multiple_of(index * LANES, LANES)
            sources = [
                qkv_hbm.at[:, pl.ds(at, LANES)],
                qkv_hbm.at[:, pl.ds(pl.multiple_of(width + at, LANES), LANES)],
                qkv_hbm.at[:, pl.ds(pl.multiple_of(2 * width + at, LANES), LANES)],
                attended_hbm.at[:, pl.ds(at, LANES)],
            ]
            copies = [
                local(source, blocks.at[slot, number], pair_sem.at[slot, number])
                for number, source in enumerate(sources)
            ]
            copies.append(
                local(total_hbm.at[index], totals.at[slot], pair_sem.at[slot, len(sources)])
            )
            return copies

        first_load = local(first_hbm, first, load_sem.at[1])
        for copy in loads(0, 0):
            copy.start()
        first_load.start()
        first_load.wait()
        across[...] = first[...].T

        @pl.loop(0, pairs)
        def pair(index):
            slot = lax.rem(index, 2)
            for copy in loads(index, slot):
                copy.wait()

            @pl.when(index + 1 < pairs)
            def _():
                for copy in loads(index + 1, 1 - slot):
                    copy.start()

            at = pl.multiple_of(index * LANES, LANES)
            key_at = pl.multiple_of(width + at, LANES)
            value_at = pl.multiple_of(2 * width + at, LANES)
            queries, keys, values = blocks[slot, 0], blocks[slot, 1], blocks[slot, 2]
            back = grad_attended[:, pl.ds(at, LANES)]
            product = back.astype(F32) * blocks[slot, 3].astype(F32)
            wide_keys = jnp.concatenate([keys, keys_ref[...]], axis=1)
            wide_values = jnp.concatenate([values, keys_ref[...]], axis=1)
            keys_across = keys.T
            query_grad, key_grad, value_grad = [], None, None
            for head in range(2):
                own_queries = head_part(queries, head)
                own_back = head_part(back, head)
                log_total = totals[slot, :, HEAD_DIM * head : HEAD_DIM * head + 1]
                inner = jnp.sum(head_part(product, head), axis=1, keepdims=True)
                left = jnp.concatenate([own_queries, query_lanes(1.0, log_total)], axis=1)
                right = jnp.concatenate([own_back, query_lanes(0.0, inner)], axis=1)
                weights = jnp.exp(dot(wide_keys, left, NT))
                score_grad = (weights * dot(wide_values, right, NT)).astype(BF16)
                value_part = dot(weights.astype(BF16), own_back)
                key_part = dot(score_grad, own_queries)
                value_grad = value_part if value_grad is None else value_grad + value_part
                key_grad = key_part if key_grad is None else key_grad + key_part
                query_grad.append(
                    dot(keys_across[HEAD_DIM * head : HEAD_DIM * (head + 1)], score_grad)
                )
            query_grad = (SCALE * jnp.concatenate(query_grad, axis=0).T).astype(BF16)
            key_grad, value_grad = key_grad.astype(BF16), value_grad.astype(BF16)
            grad_qkv[:, pl.ds(at, LANES)] = query_grad
            grad_qkv[:, pl.ds(key_at, LANES)] = key_grad
            grad_qkv[:, pl.ds(value_at, LANES)] = value_grad
            lines[3:4, pl.ds(at, LANES)] = column_sum(query_grad.astype(F32))
            lines[4:5, pl.ds(at, LANES)] = column_sum(value_grad.astype(F32))
            both = jnp.concatenate([query_grad, key_grad, value_grad], axis=1)
            weight_grad = dot(across[...], both).astype(BF16)
            weight_grad = weight_grad.reshape((GROUPS, share, 3 * LANES))
            for place in range(2):

                @pl.when(lax.rem(index, 2) == place)
                def _():
                    columns = slice(3 * LANES * place, 3 * LANES * (place + 1))
                    store_unit(late, index // 2, weight_grad, columns)

            wave(parts + 2 + index, late=True)

    def copy(own, slot, number):
        chunk = chunks_of(own, text_rows)[number]
        return crossing_copy(leaving, returned, slot, chunk, send_sem, recv_sem, number)

    def line_copy(number):
        partner = item_partner(number)[0] if number < bits else tower_partner()
        return pltpu.make_async_remote_copy(
            src_ref=line_here.at[number],
            dst_ref=line_there.at[number],
            send_sem=line_send.at[number],
            recv_sem=line_recv.at[number],
            device_id=partner,
            device_id_type=MESH,
        )

    def line_step(number):
        if not reducing:
            return
        line_copy(number).wait()
        total = line_here[number] + line_there[number]
        if number < bits:
            line_here[number + 1] = total
            line_copy(number + 1).start()
        else:
            line_out[...] = total

    def last_phase(late, grad_qkv, last_late, qkv_weight, joined, grad_middle, states, proj_weight, state_grad):
        loads = [
            local(source, target, load_sem.at[number])
            for number, (source, target) in enumerate(
                (
                    (qkv_weight_hbm, qkv_weight), (joined_hbm, joined), (middle_hbm, grad_middle),
                    (states_hbm.at[side], states), (proj_hbm, proj_weight),
                )
            )
        ]
        for load in loads:
            load.start()
        for load in loads[:3]:
            load.wait()
        lines[1:3, :] = jnp.zeros((2, width), F32)

        def rows_back(first, count):
            rows = pl.ds(first, count)
            grad_first = dot(grad_qkv[rows, :], qkv_weight[...], NT)
            scaled, inverse = normalize(joined[rows, :])
            lines[1:2, :] += column_sum(grad_first * scaled)
            lines[2:3, :] += column_sum(grad_first)
            grad_first = grad_first * line_of(gain1_ref)
            grad_joined = grad_middle[rows, :] + inverse * (
                grad_first - row_mean(grad_first) - scaled * row_mean(grad_first * scaled)
            )
            if first + count == ROWS:
                cls = text_rows + PATCH_BIG - first
                lines[0:1, :] = grad_joined[cls : cls + 1, :]
                row = lax.broadcasted_iota(jnp.int32, grad_joined.shape, 0)
                grad_joined = jnp.where(row < cls, grad_joined, 0.0)
            return grad_joined.astype(BF16)

        def on_each_side(act):
            for own in range(2):
                pl.when(side == own)(functools.partial(act, own))

        last = None
        if reducing:
            last = LastReducer(
                bits, LAST_ORDERS,
                (last_late, last_landed, last_crossing, last_crossed, sums, last_send, last_recv),
            )

        def settle(unit, step):
            if reducing:
                last.settle(unit, step)

        def leave(number, own):
            sent = 1 - own
            first, count = chunks_of(sent, text_rows)[number]
            start = first if sent == 1 else text_rows + first
            leaving[first : first + count, :] = rows_back(start, count)
            copy(sent, own, number).start()

        kept_rows = ROWS - text_rows

        def keep(own):
            if own == 1:
                returned[1] = rows_back(0, text_rows)
            else:
                returned[0, 0:kept_rows, :] = rows_back(text_rows, kept_rows)
                for home in range(2):
                    returned[home, kept_rows:text_rows, :] = jnp.zeros(
                        (text_rows - kept_rows, width), BF16
                    )

        def weight_grad(place, own):
            unit = own if place else 1 - own
            rows = pl.ds(0, kept_rows if unit == 0 else text_rows)
            grad = returned[own, rows, :] if place else leaving[rows, :]
            given = states[rows, :] if place else foreign[rows, :]
            order = LAST_ORDERS[place] if reducing else ()
            fill(last_late.at[place], dot(given, grad, TN), order)
            lines[13 + unit : 14 + unit, :] = column_sum(grad.astype(F32))

        units = early + heads
        on_each_side(functools.partial(leave, 0))
        wave(units)
        on_each_side(functools.partial(leave, 1))
        foreign_copy.wait()
        on_each_side(functools.partial(weight_grad, 0))
        if reducing:
            last.send(0, 0).start()
        on_each_side(keep)
        settle(0, 0)
        wave(units + 1)
        for load in loads[3:]:
            load.wait()
        on_each_side(functools.partial(weight_grad, 1))
        if reducing:
            last.send(1, 0).start()
            line_here[0] = lines[...]
            line_copy(0).start()
        state_grad[side] = dot(returned[side], proj_weight[...], NT).astype(BF16)
        grad_store = [
            local(state_grad.at[home], state_grad_hbm.at[home], load_sem.at[number])
            for number, home in enumerate((side, 1 - side))
        ]
        grad_store[0].start()
        settle(1, 0)
        line_step(0)
        wave(units + 2)
        line_step(1)
        settle(0, 1)
        wave(units + 3)
        settle(1, 1)
        line_step(2)

        def arrive(own):
            for number in range(2):
                copy(own, 1 - own, number).wait_recv()
                copy(1 - own, own, number).wait_send()

        on_each_side(arrive)
        state_grad[1 - side] = dot(returned[1 - side], proj_weight[...], NT).astype(BF16)
        grad_store[1].start()
        line_step(3)
        wave(units + 4)
        settle(0, 2)
        settle(1, 2)
        line_step(4)
        settle(0, 3)
        if reducing:
            reducer_of(late).finish(0, units)
        settle(1, 3)
        if reducing:
            last.finish()
        else:
            line_out[...] = lines[...]
            sums[0:heads] = late[...]
            sums[heads : heads + 2] = last_late[...]
        for store in grad_store:
            store.wait()

    def late_phase(late):
        def qkv_phase(grad_qkv):
            pl.run_scoped(
                functools.partial(attention_phase, late, grad_qkv),
                pltpu.VMEM((ROWS, width), BF16),
                pltpu.VMEM((width, ROWS), BF16),
                pltpu.VMEM((2, 4, ROWS, LANES), BF16),
                pltpu.VMEM((2, ROWS, LANES), F32),
            )
            pl.run_scoped(
                functools.partial(last_phase, late, grad_qkv),
                pltpu.VMEM((2,) + unit_shape, BF16),
                pltpu.VMEM((width, 3 * width), BF16),
                pltpu.VMEM((ROWS, width), F32),
                pltpu.VMEM((ROWS, width), F32),
                pltpu.VMEM((text_rows, width), BF16),
                pltpu.VMEM((width, width), BF16),
                pltpu.VMEM((2, text_rows, width), BF16),
            )

        pl.run_scoped(qkv_phase, pltpu.VMEM((ROWS, 3 * width), BF16))

    pl.run_scoped(late_phase, pltpu.VMEM((heads,) + unit_shape, BF16))


def layer(
    text_rows, bits, group, length, out_bias, gain2, shift2, up_bias, down_bias, gain1,
    joined, attended, given, out_weight, up_weight, down_weight, qkv, log_total, first_normed,
    qkv_weight, states, proj_weight,
):
    width, hidden = up_weight.shape
    parts = hidden // width
    share = width // GROUPS
    early, heads = 2 * parts + 1, width // LANES // 2
    units = early + heads
    whole = (2,) * bits if bits else (GROUPS,)
    line_shape = (VECTOR_ROWS, width)
    steps = bits + 1
    reducing = []
    if bits:
        for slots in (SLOTS, (2,) * bits):
            reducing += [
                pltpu.VMEM((slots[step],) + (2,) * (bits - 1 - step) + (share, width), BF16)
                for step in range(bits)
            ]
        reducing += [
            pltpu.VMEM((units, share, width), BF16),
            pltpu.VMEM((units, share, width), BF16),
            pltpu.VMEM((2, share, width), BF16),
            pltpu.VMEM((share, width), BF16),
            pltpu.VMEM((2,) + (2,) * (bits - 1) + (share, width), BF16),
            pltpu.SemaphoreType.DMA((2,)),
            pltpu.SemaphoreType.DMA((units, steps)),
            pltpu.SemaphoreType.DMA((units, steps)),
            pltpu.SemaphoreType.DMA((2, steps)),
            pltpu.SemaphoreType.DMA((2, steps)),
            pltpu.VMEM((steps,) + line_shape, F32),
            pltpu.VMEM((steps,) + line_shape, F32),
            pltpu.SemaphoreType.DMA((steps,)),
            pltpu.SemaphoreType.DMA((steps,)),
        ]
    sums = (units + 1, share, width) if bits else (heads + 2, GROUPS, share, width)
    outs = pl.pallas_call(
        functools.partial(layer_kernel, text_rows, bits),
        out_shape=(
            jax.ShapeDtypeStruct(given.shape, BF16),
            jax.ShapeDtypeStruct(states.shape, BF16),
            jax.ShapeDtypeStruct(sums, F32 if bits else BF16),
            jax.ShapeDtypeStruct(line_shape, F32),
            jax.ShapeDtypeStruct((early,) + whole + (share, width), BF16),
            jax.ShapeDtypeStruct((ROWS, width), F32),
        ),
        in_specs=in_smem(2) + in_vmem(6) + anywhere(12),
        out_specs=tuple(anywhere(2) + [pl.BlockSpec()] * 2 + anywhere(2)),
        scratch_shapes=[
            pltpu.VMEM((ROWS, LANES), BF16),
            pltpu.VMEM((ROWS, width), BF16),
            pltpu.VMEM((2, text_rows, width), BF16),
            pltpu.VMEM((text_rows, width), BF16),
            pltpu.VMEM((text_rows, width), BF16),
            pltpu.VMEM(line_shape, F32),
            pltpu.SemaphoreType.DMA((6,)),
            pltpu.SemaphoreType.DMA((early,)),
            pltpu.SemaphoreType.DMA((2, 5)),
            pltpu.SemaphoreType.DMA((3,)),
            pltpu.SemaphoreType.DMA((3,)),
        ]
        + reducing,
        compiler_params=pltpu.CompilerParams(
            collective_id=1, has_side_effects=True, vmem_limit_bytes=63 << 20
        ),
        name="layer",
    )(
        group, length, out_bias, gain2, shift2, up_bias, down_bias, gain1,
        joined, attended, given, out_weight, up_weight, down_weight, qkv, log_total, first_normed,
        qkv_weight, states, proj_weight,
    )
    return outs[:5]


def spread_kernel(layout, sums_ref, lines_ref, layer_hbm, state_hbm, layer_out, state_out, *outs):
    outs, (layer_here, state_here, sem) = outs[:-3], outs[-3:]
    passes = [
        [
            pltpu.make_async_copy(source, here, sem.at[number, 0]),
            pltpu.make_async_copy(here, target, sem.at[number, 1]),
        ]
        for number, (source, here, target) in enumerate(
            ((layer_hbm, layer_here, layer_out), (state_hbm, state_here, state_out))
        )
    ]
    for copy in passes:
        copy[0].start()
    for copy in passes:
        copy[0].wait()
        copy[1].start()
    me = lax.axis_index("items")
    rows, width = sums_ref.shape[1:]
    for (kind, first, count), out_ref in zip(layout, outs):
        if kind == "columns":
            for part in range(count):
                out_ref[:, part * width : (part + 1) * width] = sums_ref[first + part]
        elif kind == "heads":
            for part in range(count):
                for place in range(2):
                    for which in range(3):
                        source = (3 * place + which) * LANES
                        target = which * width + (2 * part + place) * LANES
                        out_ref[:, target : target + LANES] = sums_ref[
                            first + part, :, source : source + LANES
                        ]
        elif kind == "rows":
            for part in range(count):
                out_ref[part * rows : (part + 1) * rows, :] = sums_ref[first + part]
        else:
            line = jnp.concatenate(
                [lines_ref[first + part : first + part + 1, :] for part in range(count)], axis=1
            )
            if kind == "side":
                line = jnp.where(
                    lax.axis_index("tower") == 0,
                    lines_ref[first : first + 1, :],
                    lines_ref[first + 1 : first + 2, :],
                )
            share = out_ref.shape[1]
            line = jnp.broadcast_to(line, (8, line.shape[1]))
            line = pltpu.roll(line, lax.rem(line.shape[1] - me * share, line.shape[1]), 1)
            out_ref[...] = line[0:1, :share]
    for copy in passes:
        copy[1].wait()


def spread(layout, shapes, sums, lines, layer_out, state_grad):
    return pl.pallas_call(
        functools.partial(spread_kernel, layout),
        out_shape=(
            jax.ShapeDtypeStruct(layer_out.shape, BF16),
            jax.ShapeDtypeStruct(state_grad.shape, BF16),
        )
        + tuple(jax.ShapeDtypeStruct(shape, F32) for shape in shapes),
        in_specs=[pl.BlockSpec()] * 2 + anywhere(2),
        out_specs=tuple(anywhere(2) + [pl.BlockSpec()] * len(shapes)),
        scratch_shapes=[
            pltpu.VMEM(layer_out.shape, BF16),
            pltpu.VMEM(state_grad.shape, BF16),
            pltpu.SemaphoreType.DMA((2, 2)),
        ],
        compiler_params=pltpu.CompilerParams(vmem_limit_bytes=63 << 20),
        name="spread_shares",
    )(sums, lines, layer_out, state_grad)


def body(
    states,
    proj_weight,
    proj_bias,
    cls_row,
    norm1_gain,
    norm1_shift,
    qkv_weight,
    qv_bias,
    out_weight,
    out_bias,
    norm2_gain,
    norm2_shift,
    up_weight,
    up_bias,
    down_weight,
    down_bias,
    image_group,
    caption_len,
    out_grad,
):
    width = states.shape[-1]
    text_rows = states.shape[3]
    hidden = up_weight.shape[1]
    parts = hidden // width
    own_states = states.reshape(2, text_rows, width)
    joined, first_normed, qkv = entry(
        own_states, proj_weight[0], proj_bias, cls_row, norm1_gain, norm1_shift, qkv_weight, qv_bias,
    )
    attended, log_total = attention(text_rows, image_group, caption_len, qkv)
    items = lax.axis_size("items")
    share = width // items
    bits = items.bit_length() - 1
    if items != GROUPS or share % TILE_ROWS:
        bits = 0
    layer_out, state_grad, sums, lines, grads = layer(
        text_rows, bits, image_group, caption_len, out_bias, norm2_gain, norm2_shift, up_bias,
        down_bias, norm1_gain, joined, attended, out_grad[0, 0],
        out_weight, up_weight, down_weight, qkv, log_total, first_normed, qkv_weight, own_states,
        proj_weight[0],
    )
    if not bits:
        return (layer_out[None, None], state_grad.reshape(states.shape)) + plain_sums(
            grads, sums, lines, parts
        )
    heads = width // LANES // 2
    last = 2 * parts + 1 + heads
    layout = (
        ("rows", last, 1), ("side", 9 + parts, 1), ("line", 0, 1), ("line", 1, 1),
        ("line", 2, 1), ("heads", 2 * parts + 1, heads), ("line", 3, 2), ("rows", 2 * parts, 1),
        ("line", 5, 1), ("line", 6, 1), ("line", 7, 1), ("columns", 0, parts),
        ("line", 8, parts), ("rows", parts, parts), ("line", 8 + parts, 1),
    )
    shapes = []
    for kind, _, number in layout:
        if kind == "columns":
            shapes.append((share, number * width))
        elif kind == "heads":
            shapes.append((share, 3 * width))
        elif kind == "rows":
            shapes.append((number * share, width))
        else:
            shapes.append((1, number * share))
    layer_out, state_grad, *shares = spread(layout, shapes, sums, lines, layer_out, state_grad)
    layer_out, state_grad = layer_out[None, None], state_grad.reshape(states.shape)
    shares = [
        piece.reshape(-1) if kind in ("line", "side") else piece
        for piece, (kind, _, _) in zip(shares, layout)
    ]
    return (layer_out, state_grad, shares[0][None], shares[1][None]) + tuple(shares[2:])


def plain_sums(grads, later, lines, parts):
    def over_items(part):
        return lax.psum_scatter(part.astype(F32), "items", scatter_dimension=0, tiled=True)

    def over_both(part):
        return lax.psum(over_items(part).astype(BF16), "tower").astype(F32)

    def over_sides(first, second):
        first, second = over_both(first), over_both(second)
        return jnp.where(lax.axis_index("tower") == 0, first, second)[None]

    width = lines.shape[1]
    heads = later.shape[0] - 2
    up_grad = grads[:parts].transpose(1, 2, 0, 3).reshape(width, parts * width)
    down_grad = grads[parts : 2 * parts].transpose(1, 0, 2, 3).reshape(parts * width, width)
    out_grad = grads[2 * parts].reshape(width, width)
    qkv_grad = later[:heads].reshape(heads, width, 2, 3, LANES).transpose(1, 3, 0, 2, 4)
    qkv_grad = qkv_grad.reshape(width, 3 * width)
    sides = [later[heads + place].reshape(width, width) for place in range(2)]
    image_first = lax.axis_index("tower") == 1
    sides = (
        jnp.where(image_first, sides[0], sides[1]),
        jnp.where(image_first, sides[1], sides[0]),
    )
    return (
        over_sides(*sides),
        over_sides(lines[9 + parts], lines[10 + parts]),
        over_both(lines[0]),
        over_both(lines[1]),
        over_both(lines[2]),
        over_both(qkv_grad),
        over_both(lines[3:5].reshape(-1)),
        over_both(out_grad),
        over_both(lines[5]),
        over_both(lines[6]),
        over_both(lines[7]),
        over_both(up_grad),
        over_both(lines[8 : 8 + parts].reshape(-1)),
        over_both(down_grad),
        over_both(lines[8 + parts]),
    )


def solution(mesh):
    in_specs = (
        P("tower", None, "items", None, None),
        P("tower", None, None),
        P("tower", None),
        P(),
        P(),
        P(),
        P(),
        P(),
        P(),
        P(),
        P(),
        P(),
        P(),
        P(),
        P(),
        P(),
        P("tower", "items"),
        P("tower", "items"),
        P("tower", "items", None, None),
    )
    out_specs = (
        P("tower", "items", None, None),
        P("tower", None, "items", None, None),
        P("tower", "items", None),
        P("tower", "items"),
        P("items"),
        P("items"),
        P("items"),
        P("items", None),
        P("items"),
        P("items", None),
        P("items"),
        P("items"),
        P("items"),
        P("items", None),
        P("items"),
        P("items", None),
        P("items"),
    )
    return jax.shard_map(body, mesh=mesh, in_specs=in_specs, out_specs=out_specs, check_vma=False)
```

```python
import functools

import jax
import jax.numpy as jnp
from jax import lax
from jax.experimental import pallas as pl
from jax.experimental.pallas import tpu as pltpu
from jax.sharding import PartitionSpec as P

HEADS = 12
HEAD_DIM = 64
PATCH_SMALL = 197
PATCH_BIG = 325
EPSILON = 1e-06
MASKED = -1000000000.0
SCALE = 0.125
ROWS = 896
LANES = 128
TILE_ROWS = 16
GROUPS = 16
STARTS = (0, 1, 3, 4, 5)
SLOTS = (5, 6, 4, 3)
VECTOR_ROWS = 16
HALF_ORDERS = ((0, 1, 2, 3), (0, 2, 3, 1))

F32 = jnp.float32
BF16 = jnp.bfloat16
NN = (((1,), (0,)), ((), ()))
NT = (((1,), (1,)), ((), ()))
TN = (((0,), (0,)), ((), ()))
MESH = pl.DeviceIdType.MESH


def dot(left, right, numbers=NN):
    return lax.dot_general(left, right, numbers, preferred_element_type=F32)


def live_rows(shape, group, length, text_rows):
    row = lax.broadcasted_iota(jnp.int32, shape, 0)
    patches = PATCH_SMALL + (PATCH_BIG - PATCH_SMALL) * group
    image = (row >= text_rows) & (row < text_rows + patches)
    return (row < length) | image | (row == text_rows + PATCH_BIG)


def key_lanes(group, length, text_rows):
    lane = lax.broadcasted_iota(jnp.int32, (ROWS, LANES), 1)
    bias = jnp.where(live_rows((ROWS, LANES), group, length, text_rows), 0.0, MASKED)
    return jnp.where(lane == 0, bias, jnp.where(lane < 4, 1.0, 0.0)).astype(BF16)


def query_lanes(first, column):
    lane = lax.broadcasted_iota(jnp.int32, (ROWS, LANES), 1)
    upper = column.astype(BF16).astype(F32)
    rest = column - upper
    inner = rest.astype(BF16).astype(F32)
    lower = rest - inner
    lanes = jnp.where(lane == 0, first, 0.0)
    lanes = jnp.where(lane == 1, -upper, lanes)
    lanes = jnp.where(lane == 2, -inner, lanes)
    return jnp.where(lane == 3, -lower, lanes).astype(BF16)


def head_part(block, head):
    lane = lax.broadcasted_iota(jnp.int32, block.shape, 1)
    keep = lane < HEAD_DIM if head == 0 else lane >= HEAD_DIM
    return jnp.where(keep, block, jnp.zeros_like(block))


def column_sum(block):
    return jnp.sum(block, axis=0, keepdims=True)


def line_of(ref):
    return ref[...].reshape(1, ref.shape[0])


def row_mean(block):
    return jnp.mean(block, axis=1, keepdims=True)


def normalize(block):
    centered = block - row_mean(block)
    inverse = lax.rsqrt(row_mean(centered * centered) + EPSILON)
    return centered * inverse, inverse


def in_vmem(count=1):
    return [pl.BlockSpec(memory_space=pltpu.VMEM)] * count


def in_smem(count=1):
    return [pl.BlockSpec(memory_space=pltpu.SMEM)] * count


def anywhere(count=1):
    return [pl.BlockSpec(memory_space=pl.ANY)] * count


def tower_partner():
    return {"tower": 1 - lax.axis_index("tower")}


def item_partner(bit):
    me = lax.axis_index("items")
    low = lax.rem(me // (1 << bit), 2)
    return {"items": me + (1 - 2 * low) * (1 << bit)}, low


def chunks_of(side, text_rows):
    half = text_rows // 2
    if side == 1:
        return (0, half), (half, half)
    return (0, half), (half, ROWS - text_rows - half)


def crossing_copy(source, target, slot, chunk, send_sem, recv_sem, number):
    first, count = chunk
    return pltpu.make_async_remote_copy(
        src_ref=source.at[pl.ds(first, count)],
        dst_ref=target.at[slot, pl.ds(first, count)],
        send_sem=send_sem.at[number],
        recv_sem=recv_sem.at[number],
        device_id=tower_partner(),
        device_id_type=MESH,
    )


def place_of(number, bits):
    if not bits:
        return (number,)
    if isinstance(number, int):
        return tuple((number >> bit) & 1 for bit in range(bits))
    return tuple(lax.rem(number // (1 << bit), 2) for bit in range(bits))


def entry_kernel(
    text_rows, states_hbm, proj_hbm, proj_bias_ref, cls_ref, gain_ref, shift_ref, qkv_hbm, bias_ref,
    joined_hbm, first_hbm, qkv_out_hbm,
    arrived, leaving, states, proj_weight, qkv_weight, joined, first_normed, qkv,
    load_sem, store_sem, send_sem, recv_sem,
):
    side = lax.axis_index("tower")
    width = joined.shape[1]
    barrier = pltpu.get_barrier_semaphore()
    pl.semaphore_signal(barrier, inc=1, device_id=tower_partner(), device_id_type=MESH)
    sources = (
        (proj_hbm, proj_weight),
        (states_hbm.at[1 - side], states.at[1 - side]),
        (states_hbm.at[side], states.at[side]),
        (qkv_hbm, qkv_weight),
    )
    loads = [
        pltpu.make_async_copy(source, target, load_sem.at[number])
        for number, (source, target) in enumerate(sources)
    ]
    for load in loads:
        load.start()
    pl.semaphore_wait(barrier, 1)

    def project(rows):
        return (dot(rows, proj_weight[...]) + proj_bias_ref[...]).astype(BF16)

    def copy(own, slot, number):
        chunk = chunks_of(own, text_rows)[number]
        return crossing_copy(leaving, arrived, slot, chunk, send_sem, recv_sem, number)

    half = text_rows // 2
    loads[0].wait()
    loads[1].wait()
    for number in range(2):
        rows = pl.ds(number * half, half)
        leaving[rows, :] = project(states[1 - side, rows, :])
        for own in range(2):

            @pl.when(side == own)
            def _():
                copy(own, own, number).start()

    loads[2].wait()
    arrived[side] = project(states[side])
    loads[3].wait()

    def stores(first, count, number):
        rows = pl.ds(first, count)
        return [
            pltpu.make_async_copy(source.at[rows], target.at[rows], store_sem.at[number, place])
            for place, (source, target) in enumerate(
                ((joined, joined_hbm), (first_normed, first_hbm), (qkv, qkv_out_hbm))
            )
        ]

    def process(first, count, number):
        rows = pl.ds(first, count)
        if first < text_rows:
            block = arrived[1, rows, :].astype(F32)
        else:
            block = arrived[0, pl.ds(first - text_rows, count), :].astype(F32)
            row = first + lax.broadcasted_iota(jnp.int32, block.shape, 0)
            block = jnp.where(row == text_rows + PATCH_BIG, line_of(cls_ref), block)
            block = jnp.where(row > text_rows + PATCH_BIG, 0.0, block)
        joined[rows, :] = block
        scaled, _ = normalize(block)
        normed = (scaled * line_of(gain_ref) + line_of(shift_ref)).astype(BF16)
        first_normed[rows, :] = normed
        for part in range(3):
            columns = slice(part * width, (part + 1) * width)
            product = dot(normed, qkv_weight[:, columns])
            if part == 0:
                product = (product + line_of(bias_ref)[:, :width]) * SCALE
            elif part == 2:
                product = product + line_of(bias_ref)[:, width:]
            qkv[rows, columns] = product.astype(BF16)
        for store in stores(first, count, number):
            store.start()

    for own in range(2):

        @pl.when(side == own)
        def _():
            other = 1 - own
            kept = (0, text_rows) if own == 1 else (text_rows, ROWS - text_rows)
            order = [kept]
            for first, count in chunks_of(other, text_rows):
                order.append((first if other == 1 else text_rows + first, count))
            for number, (first, count) in enumerate(order):
                if number:
                    copy(other, other, number - 1).wait_recv()
                process(first, count, number)
            for number in range(2):
                copy(own, own, number).wait_send()
            for number, (first, count) in enumerate(order):
                for store in stores(first, count, number):
                    store.wait()


def entry(states, proj_weight, proj_bias, cls_row, gain, shift, qkv_weight, qkv_bias):
    text_rows, width = states.shape[1:]
    shapes = (((ROWS, width), F32), ((ROWS, width), BF16), ((ROWS, 3 * width), BF16))
    return pl.pallas_call(
        functools.partial(entry_kernel, text_rows),
        out_shape=tuple(jax.ShapeDtypeStruct(shape, kind) for shape, kind in shapes),
        in_specs=anywhere(2) + in_vmem(4) + anywhere() + in_vmem(),
        out_specs=tuple(anywhere(3)),
        scratch_shapes=[
            pltpu.VMEM((2, text_rows, width), BF16),
            pltpu.VMEM((text_rows, width), BF16),
            pltpu.VMEM((2, text_rows, width), BF16),
            pltpu.VMEM(proj_weight.shape, BF16),
            pltpu.VMEM(qkv_weight.shape, BF16),
        ]
        + [pltpu.VMEM(shape, kind) for shape, kind in shapes]
        + [
            pltpu.SemaphoreType.DMA((4,)),
            pltpu.SemaphoreType.DMA((3, 3)),
            pltpu.SemaphoreType.DMA((2,)),
            pltpu.SemaphoreType.DMA((2,)),
        ],
        compiler_params=pltpu.CompilerParams(
            collective_id=0, has_side_effects=True, vmem_limit_bytes=56 << 20
        ),
        name="entry",
    )(states, proj_weight, proj_bias, cls_row, gain, shift, qkv_weight, qkv_bias)


def attention_kernel(
    text_rows, group_ref, length_ref, qkv_hbm, out_hbm, total_hbm,
    blocks, outs, totals, keys_ref, load_sem, store_sem,
):
    pairs = total_hbm.shape[0]
    width = pairs * LANES

    def loads(index, slot):
        return [
            pltpu.make_async_copy(
                qkv_hbm.at[:, pl.ds(pl.multiple_of(part * width + index * LANES, LANES), LANES)],
                blocks.at[slot, part],
                load_sem.at[slot, part],
            )
            for part in range(3)
        ]

    def stores(index, slot):
        columns = pl.ds(pl.multiple_of(index * LANES, LANES), LANES)
        return [
            pltpu.make_async_copy(outs.at[slot], out_hbm.at[:, columns], store_sem.at[slot, 0]),
            pltpu.make_async_copy(totals.at[slot], total_hbm.at[index], store_sem.at[slot, 1]),
        ]

    for load in loads(0, 0):
        load.start()
    keys_ref[...] = key_lanes(group_ref[0, 0], length_ref[0, 0], text_rows)
    lane = lax.broadcasted_iota(jnp.int32, (ROWS, LANES), 1)
    plain = jnp.where(lane == 0, 1.0, 0.0).astype(BF16)

    @pl.loop(0, pairs)
    def pair(index):
        slot = lax.rem(index, 2)
        for load in loads(index, slot):
            load.wait()

        @pl.when(index + 1 < pairs)
        def _():
            for load in loads(index + 1, 1 - slot):
                load.start()

        queries = blocks[slot, 0]
        keys = jnp.concatenate([blocks[slot, 1], keys_ref[...]], axis=1)
        values = jnp.concatenate([blocks[slot, 2], keys_ref[...]], axis=1)
        scores = []
        for head in range(2):
            own = jnp.concatenate([head_part(queries, head), plain], axis=1)
            scores.append(dot(own, keys, NT))
        mixes, logs = [], []
        for head in range(2):
            row_max = jnp.max(scores[head], axis=1, keepdims=True)
            weights = jnp.exp(scores[head] - row_max).astype(BF16)
            mixed = dot(weights, values)
            row_total = mixed[:, LANES + 1 : LANES + 2]
            mixes.append(mixed[:, :LANES] / row_total)
            logs.append(row_max + jnp.log(row_total))

        @pl.when(index >= 2)
        def _():
            for store in stores(index - 2, slot):
                store.wait()

        outs[slot] = jnp.where(lane < HEAD_DIM, mixes[0], mixes[1]).astype(BF16)
        totals[slot] = jnp.where(lane < HEAD_DIM, logs[0], logs[1])
        for store in stores(index, slot):
            store.start()

    for index in (pairs - 2, pairs - 1):
        for store in stores(index, index % 2):
            store.wait()


def attention(text_rows, group, length, qkv):
    width = qkv.shape[1] // 3
    pairs = width // LANES
    return pl.pallas_call(
        functools.partial(attention_kernel, text_rows),
        out_shape=(
            jax.ShapeDtypeStruct((ROWS, width), BF16),
            jax.ShapeDtypeStruct((pairs, ROWS, LANES), F32),
        ),
        in_specs=in_smem(2) + anywhere(),
        out_specs=tuple(anywhere(2)),
        scratch_shapes=[
            pltpu.VMEM((2, 3, ROWS, LANES), BF16),
            pltpu.VMEM((2, ROWS, LANES), BF16),
            pltpu.VMEM((2, ROWS, LANES), F32),
            pltpu.VMEM((ROWS, LANES), BF16),
            pltpu.SemaphoreType.DMA((2, 3)),
            pltpu.SemaphoreType.DMA((2, 2)),
        ],
        compiler_params=pltpu.CompilerParams(vmem_limit_bytes=52 << 20),
        name="attention_forward",
    )(group, length, qkv)


class Reducer:
    def __init__(self, bits, early, units, refs):
        (
            self.grads, self.late, self.landed, self.crossing, self.crossed, self.held, self.sums,
            self.load_sem, self.send_sem, self.recv_sem,
        ) = refs
        self.bits, self.early, self.units = bits, early, units
        self.partners = [item_partner(bit) for bit in range(bits)]

    def greet(self):
        barrier = pltpu.get_barrier_semaphore()
        for partner, _ in self.partners:
            pl.semaphore_signal(barrier, inc=1, device_id=partner, device_id_type=MESH)

    def part(self, ref, first, side):
        return ref.at[first, side]

    def load(self, unit):
        slot = lax.rem(unit, 2)
        return pltpu.make_async_copy(
            self.part(self.grads, unit, self.partners[0][1]),
            self.held.at[slot],
            self.load_sem.at[slot],
        )

    def send(self, unit, step, late=False):
        partner = tower_partner()
        if step == self.bits:
            source, target = self.crossing.at[unit], self.crossed.at[unit]
        else:
            partner, low = self.partners[step]
            target = self.landed[step].at[lax.rem(unit, SLOTS[step])]
            if step:
                source = self.part(
                    self.landed[step - 1], lax.rem(unit, SLOTS[step - 1]), 1 - low
                )
            elif late:
                source = self.part(self.late, unit - self.early, 1 - low)
            else:
                source = self.part(self.grads, unit, 1 - low)
        return pltpu.make_async_remote_copy(
            src_ref=source,
            dst_ref=target,
            send_sem=self.send_sem.at[unit, step],
            recv_sem=self.recv_sem.at[unit, step],
            device_id=partner,
            device_id_type=MESH,
        )

    def add(self, mine, there, depth, last):
        @pl.loop(0, 1 << depth)
        def _(number):
            place = place_of(number, depth) if depth else ()
            if last is None:
                there[place] = mine[place] + there[place]
            else:
                self.crossing[last] = (
                    mine[...].astype(F32) + there[...].astype(F32)
                ).astype(BF16)

    def settle(self, unit, step, late=False):
        self.send(unit, step, late).wait()
        low = self.partners[step][1]
        if step:
            mine = self.part(self.landed[step - 1], lax.rem(unit, SLOTS[step - 1]), low)
        elif late:
            mine = self.part(self.late, unit - self.early, low)
        else:
            self.load(unit).wait()
            mine = self.held.at[lax.rem(unit, 2)]
        depth = self.bits - 1 - step
        there = self.landed[step].at[lax.rem(unit, SLOTS[step])]
        self.add(mine, there, depth, None if depth else unit)
        self.send(unit, step + 1).start()

    def finish(self, first, last):
        @pl.loop(first, last)
        def _(unit):
            self.send(unit, self.bits).wait()
            self.sums[unit] = self.crossing[unit].astype(F32) + self.crossed[unit].astype(F32)

    def begin(self, unit, late=False):
        if not late:
            self.load(unit).start()
        self.send(unit, 0, late).start()

    def either(self, act, unit, late):
        if isinstance(unit, int):
            act(late=unit >= self.early)
        elif not late:
            act(late=False)
        else:
            pl.when(unit < self.early)(functools.partial(act, late=False))
            pl.when(unit >= self.early)(functools.partial(act, late=True))

    def wave(self, number, late=False):
        fixed = isinstance(number, int)
        for step in reversed(range(self.bits)):
            unit = number - STARTS[step + 1]
            if fixed:
                if not 0 <= unit < self.units:
                    continue

            def go():
                if step:
                    self.settle(unit, step)
                else:
                    self.either(functools.partial(self.settle, unit, 0), unit, late)

            if fixed:
                go()
            else:
                pl.when(unit >= 0)(go)
        if not fixed or number < self.units:
            self.either(functools.partial(self.begin, number), number, late)


class LastReducer:
    def __init__(self, bits, orders, refs):
        (
            self.late, self.landed, self.crossing, self.crossed, self.sums, self.send_sem, self.recv_sem,
        ) = refs
        self.bits, self.orders = bits, orders
        self.partners = [item_partner(bit) for bit in range(bits)]

    def part(self, unit, half, step, mine):
        partner, low = self.partners[self.orders[half][step]]
        ref = self.landed[step - 1] if step else self.late
        return ref.at[unit, half, low if mine else 1 - low], partner

    def send(self, unit, half, step):
        source, partner = self.part(unit, half, step, False)
        return pltpu.make_async_remote_copy(
            src_ref=source,
            dst_ref=self.landed[step].at[unit, half],
            send_sem=self.send_sem.at[unit, half, step],
            recv_sem=self.recv_sem.at[unit, half, step],
            device_id=partner,
            device_id_type=MESH,
        )

    def begin(self, unit):
        for half in range(2):
            self.send(unit, half, 0).start()

    def settle(self, unit, step):
        for half in range(2):
            self.send(unit, half, step).wait()
            mine, _ = self.part(unit, half, step, True)
            there = self.landed[step].at[unit, half]
            depth = self.bits - 1 - step
            if depth:

                @pl.loop(0, 1 << depth)
                def _(number):
                    place = place_of(number, depth)
                    there[place] = mine[place] + there[place]

                self.send(unit, half, step + 1).start()
            else:
                width = there.shape[1]
                total = (mine[...].astype(F32) + there[...].astype(F32)).astype(BF16)
                self.crossing[unit, :, half * width : (half + 1) * width] = total
        if step == self.bits - 1 and unit == 0:
            self.cross().start()

    def cross(self):
        return pltpu.make_async_remote_copy(
            src_ref=self.crossing.at[0],
            dst_ref=self.crossed,
            send_sem=self.send_sem.at[0, 0, self.bits],
            recv_sem=self.recv_sem.at[0, 0, self.bits],
            device_id=tower_partner(),
            device_id_type=MESH,
        )

    def finish(self):
        self.cross().wait()
        total = self.crossing[1].astype(F32) + self.crossed[...].astype(F32)
        self.sums[self.sums.shape[0] - 1] = total


def layer_kernel(text_rows, bits, *refs):
    refs = list(refs)

    def take(count):
        taken = refs[:count]
        del refs[:count]
        return taken

    (
        group_ref, length_ref, out_bias_ref, gain2_ref, shift2_ref, up_bias_ref, down_bias_ref,
        gain1_ref,
    ) = take(8)
    (
        joined_hbm, attended_hbm, given_hbm, out_weight_hbm, up_weight_hbm, down_weight_hbm,
        qkv_hbm, total_hbm, first_hbm, qkv_weight_hbm, states_hbm, proj_hbm,
    ) = take(12)
    layer_hbm, state_grad_hbm, sums, line_out, grads_hbm, middle_hbm = take(6)
    keys_ref, grad_attended, returned, leaving, foreign, lines = take(6)
    load_sem, store_sem, pair_sem, send_sem, recv_sem = take(5)
    reducing = bits > 0
    width = joined_hbm.shape[1]
    extent = given_hbm.shape[0]
    hidden = up_weight_hbm.shape[1]
    parts = hidden // width
    pairs = width // LANES
    heads = pairs // 2
    share = width // GROUPS
    early = 2 * parts + 1
    whole = (2,) * bits if bits else (GROUPS,)
    unit_shape = whole + (share, width)
    last_shape = (2, 2) + whole + (share, width // 2) if bits else (2,) + unit_shape
    text_end, image_end = text_rows, text_rows + PATCH_BIG
    side = lax.axis_index("tower")
    barrier = pltpu.get_barrier_semaphore()
    pl.semaphore_signal(barrier, inc=1, device_id=tower_partner(), device_id_type=MESH)
    state = {"late": None}
    if reducing:
        landed, last_landed = take(bits), take(bits)
        (
            crossing, crossed, last_crossing, last_crossed, held, held_sem, unit_send, unit_recv,
            last_send, last_recv, line_here, line_there, line_send, line_recv,
        ) = take(14)

        def reducer_of(late):
            return Reducer(
                bits, early, early + heads,
                (grads_hbm, late, landed, crossing, crossed, held, sums, held_sem, unit_send, unit_recv),
            )

        reducer_of(None).greet()

    def wave(number, late=False):
        if reducing:
            reducer_of(state["late"]).wave(number, late)

    def fill(target, block, order=tuple(range(bits))):
        block = block.astype(BF16).reshape(GROUPS, share, block.shape[1])
        for number in range(GROUPS):
            place = place_of(number, bits)
            if bits:
                place = tuple(place[bit] for bit in order)
            target[place] = block[number]

    def local(source, target, sem):
        return pltpu.make_async_copy(source, target, sem)

    foreign_copy = pltpu.make_async_remote_copy(
        src_ref=states_hbm.at[1 - side],
        dst_ref=foreign,
        send_sem=send_sem.at[2],
        recv_sem=recv_sem.at[2],
        device_id=tower_partner(),
        device_id_type=MESH,
    )

    def middle_phase(
        out_weight, up_weight, down_weight, attended, given,
        wide, result, grad_second, normed, across, grad_low, up_stage, down_stage, out_stage,
    ):
        loads = [
            local(source, target, load_sem.at[number])
            for number, (source, target) in enumerate(
                (
                    (given_hbm, given), (out_weight_hbm, out_weight), (attended_hbm, attended),
                    (joined_hbm, grad_second), (up_weight_hbm, up_weight), (down_weight_hbm, down_weight),
                )
            )
        ]
        for load in loads:
            load.start()
        keys_ref[...] = key_lanes(group_ref[0, 0], length_ref[0, 0], text_rows)
        pl.semaphore_wait(barrier, bits + 1)
        foreign_copy.start()

        def store(unit):
            if isinstance(unit, int):
                source = out_stage if unit == 2 * parts else down_stage.at[unit - parts]
            else:
                source = up_stage
            return local(source, grads_hbm.at[unit], store_sem.at[unit])

        mask = live_rows((ROWS, 1), group_ref[0, 0], length_ref[0, 0], text_rows).astype(F32)
        loads[0].wait()
        wide[0:extent, :] = given[...].astype(F32)
        result[0:text_end, :] = wide[1 + PATCH_BIG : extent, :]
        result[text_end:image_end, :] = wide[1 : 1 + PATCH_BIG, :]
        result[image_end:extent, :] = wide[0:1, :]
        result[extent:ROWS, :] = jnp.zeros((ROWS - extent, width), F32)
        grad_result = result[...] * mask
        grad_low[...] = grad_result.astype(BF16)
        lines[8 + parts : 9 + parts, :] = column_sum(grad_result)
        for load in loads[1:4]:
            load.wait()
        middle = grad_second[...] + (dot(attended[...], out_weight[...]) + line_of(out_bias_ref))
        scaled, inverse = normalize(middle)
        second = scaled * line_of(gain2_ref) + line_of(shift2_ref)
        normed[...] = second.astype(BF16)
        across[...] = second.T.astype(BF16)
        wide[...] = scaled
        result[...] = middle + line_of(down_bias_ref)
        grad_second[...] = jnp.zeros_like(grad_second)
        for load in loads[4:]:
            load.wait()

        @pl.loop(0, parts)
        def tile(part):
            columns = pl.ds(pl.multiple_of(part * width, width), width)
            up, down = up_weight[:, columns], down_weight[columns, :]
            before = dot(normed[...], up) + up_bias_ref[columns].reshape(1, width)
            below = 0.5 + 0.5 * lax.erf(before * 0.7071067811865476)
            density = jnp.exp(-0.5 * before * before) * 0.3989422804014327
            activated = (before * below).astype(BF16)
            grad_hidden = dot(grad_low[...], down, NT) * (below + before * density)
            hidden_low = grad_hidden.astype(BF16)
            fill(up_stage, dot(across[...], hidden_low))
            store(part).start()
            result[...] += dot(activated, down)
            grad_second[...] += dot(hidden_low, up, NT)
            lines[pl.ds(8 + part, 1), :] = column_sum(hidden_low.astype(F32))
            down_grad = dot(activated, grad_low[...], TN).astype(BF16)
            rows = GROUPS // parts
            for group in range(rows):
                for piece in range(parts):
                    first = (group * parts + piece) * share
                    place = place_of(part * rows + group, bits)
                    down_stage[(piece,) + place] = down_grad[first : first + share]
            store(part).wait()
            wave(part)

        for piece in range(parts):
            store(parts + piece).start()
        result[...] = result[...] * mask
        second_grad = grad_second[...]
        scaled = wide[...]
        lines[6:7, :] = column_sum(second_grad * scaled)
        lines[7:8, :] = column_sum(second_grad)
        second_grad = second_grad * line_of(gain2_ref)
        grad_middle = grad_low[...].astype(F32) + inverse * (
            second_grad - row_mean(second_grad) - scaled * row_mean(second_grad * scaled)
        )
        grad_second[...] = grad_middle
        middle_store = local(grad_second, middle_hbm, load_sem.at[0])
        middle_store.start()
        for piece in range(parts):
            store(parts + piece).wait()
        wave(parts)
        grad_branch = grad_middle.astype(BF16)
        lines[5:6, :] = column_sum(grad_branch.astype(F32))
        fill(out_stage, dot(attended[...], grad_branch, TN))
        store(2 * parts).start()
        grad_attended[...] = dot(grad_branch, out_weight[...], NT).astype(BF16)
        wide[0:1, :] = result[image_end:extent, :]
        wide[1 : 1 + PATCH_BIG, :] = result[text_end:image_end, :]
        wide[1 + PATCH_BIG : extent, :] = result[0:text_end, :]
        given[...] = wide[0:extent, :].astype(BF16)
        layer_store = local(given, layer_hbm, load_sem.at[1])
        layer_store.start()
        wave(parts + 1)
        store(2 * parts).wait()
        middle_store.wait()
        layer_store.wait()

    pl.run_scoped(
        middle_phase,
        pltpu.VMEM((width, width), BF16),
        pltpu.VMEM((width, hidden), BF16),
        pltpu.VMEM((hidden, width), BF16),
        pltpu.VMEM((ROWS, width), BF16),
        pltpu.VMEM((extent, width), BF16),
        pltpu.VMEM((ROWS, width), F32),
        pltpu.VMEM((ROWS, width), F32),
        pltpu.VMEM((ROWS, width), F32),
        pltpu.VMEM((ROWS, width), BF16),
        pltpu.VMEM((width, ROWS), BF16),
        pltpu.VMEM((ROWS, width), BF16),
        pltpu.VMEM(unit_shape, BF16),
        pltpu.VMEM((parts,) + unit_shape, BF16),
        pltpu.VMEM(unit_shape, BF16),
    )

    def store_unit(late, unit, block, columns):
        for number in range(GROUPS):
            late[(unit,) + place_of(number, bits) + (slice(None), columns)] = block[number]

    def attention_phase(late, grad_qkv, last_loads, first, across, blocks, totals):
        state["late"] = late

        def loads(index, slot):
            at = pl.multiple_of(index * LANES, LANES)
            sources = [
                qkv_hbm.at[:, pl.ds(at, LANES)],
                qkv_hbm.at[:, pl.ds(pl.multiple_of(width + at, LANES), LANES)],
                qkv_hbm.at[:, pl.ds(pl.multiple_of(2 * width + at, LANES), LANES)],
                attended_hbm.at[:, pl.ds(at, LANES)],
            ]
            copies = [
                local(source, blocks.at[slot, number], pair_sem.at[slot, number])
                for number, source in enumerate(sources)
            ]
            copies.append(
                local(total_hbm.at[index], totals.at[slot], pair_sem.at[slot, len(sources)])
            )
            return copies

        first_load = local(first_hbm, first, load_sem.at[1])
        for copy in loads(0, 0):
            copy.start()
        first_load.start()
        for load in last_loads:
            load.start()
        first_load.wait()
        across[...] = first[...].T

        @pl.loop(0, pairs)
        def pair(index):
            slot = lax.rem(index, 2)
            for copy in loads(index, slot):
                copy.wait()

            @pl.when(index + 1 < pairs)
            def _():
                for copy in loads(index + 1, 1 - slot):
                    copy.start()

            at = pl.multiple_of(index * LANES, LANES)
            key_at = pl.multiple_of(width + at, LANES)
            value_at = pl.multiple_of(2 * width + at, LANES)
            queries, keys, values = blocks[slot, 0], blocks[slot, 1], blocks[slot, 2]
            back = grad_attended[:, pl.ds(at, LANES)]
            product = back.astype(F32) * blocks[slot, 3].astype(F32)
            wide_keys = jnp.concatenate([keys, keys_ref[...]], axis=1)
            wide_values = jnp.concatenate([values, keys_ref[...]], axis=1)
            keys_across = keys.T
            query_grad, key_grad, value_grad = [], None, None
            for head in range(2):
                own_queries = head_part(queries, head)
                own_back = head_part(back, head)
                log_total = totals[slot, :, HEAD_DIM * head : HEAD_DIM * head + 1]
                inner = jnp.sum(head_part(product, head), axis=1, keepdims=True)
                left = jnp.concatenate([own_queries, query_lanes(1.0, log_total)], axis=1)
                right = jnp.concatenate([own_back, query_lanes(0.0, inner)], axis=1)
                weights = jnp.exp(dot(wide_keys, left, NT))
                score_grad = (weights * dot(wide_values, right, NT)).astype(BF16)
                value_part = dot(weights.astype(BF16), own_back)
                key_part = dot(score_grad, own_queries)
                value_grad = value_part if value_grad is None else value_grad + value_part
                key_grad = key_part if key_grad is None else key_grad + key_part
                query_grad.append(
                    dot(keys_across[HEAD_DIM * head : HEAD_DIM * (head + 1)], score_grad)
                )
            query_grad = (SCALE * jnp.concatenate(query_grad, axis=0).T).astype(BF16)
            key_grad, value_grad = key_grad.astype(BF16), value_grad.astype(BF16)
            grad_qkv[:, pl.ds(at, LANES)] = query_grad
            grad_qkv[:, pl.ds(key_at, LANES)] = key_grad
            grad_qkv[:, pl.ds(value_at, LANES)] = value_grad
            lines[3:4, pl.ds(at, LANES)] = column_sum(query_grad.astype(F32))
            lines[4:5, pl.ds(at, LANES)] = column_sum(value_grad.astype(F32))
            both = jnp.concatenate([query_grad, key_grad, value_grad], axis=1)
            weight_grad = dot(across[...], both).astype(BF16)
            weight_grad = weight_grad.reshape((GROUPS, share, 3 * LANES))
            for place in range(2):

                @pl.when(lax.rem(index, 2) == place)
                def _():
                    columns = slice(3 * LANES * place, 3 * LANES * (place + 1))
                    store_unit(late, index // 2, weight_grad, columns)

            wave(parts + 2 + index, late=True)

    def copy(own, slot, number):
        chunk = chunks_of(own, text_rows)[number]
        return crossing_copy(leaving, returned, slot, chunk, send_sem, recv_sem, number)

    def line_copy(number):
        partner = item_partner(number)[0] if number < bits else tower_partner()
        return pltpu.make_async_remote_copy(
            src_ref=line_here.at[number],
            dst_ref=line_there.at[number],
            send_sem=line_send.at[number],
            recv_sem=line_recv.at[number],
            device_id=partner,
            device_id_type=MESH,
        )

    def line_step(number):
        if not reducing:
            return
        line_copy(number).wait()
        total = line_here[number] + line_there[number]
        if number < bits:
            line_here[number + 1] = total
            line_copy(number + 1).start()
        else:
            line_out[...] = total

    def last_phase(
        late, grad_qkv, loads, qkv_weight, joined, grad_middle, states, proj_weight, last_late, state_grad
    ):
        for load in loads[:3]:
            load.wait()
        lines[1:3, :] = jnp.zeros((2, width), F32)

        def rows_back(first, count):
            rows = pl.ds(first, count)
            grad_first = dot(grad_qkv[rows, :], qkv_weight[...], NT)
            scaled, inverse = normalize(joined[rows, :])
            lines[1:2, :] += column_sum(grad_first * scaled)
            lines[2:3, :] += column_sum(grad_first)
            grad_first = grad_first * line_of(gain1_ref)
            grad_joined = grad_middle[rows, :] + inverse * (
                grad_first - row_mean(grad_first) - scaled * row_mean(grad_first * scaled)
            )
            if first + count == ROWS:
                cls = text_rows + PATCH_BIG - first
                lines[0:1, :] = grad_joined[cls : cls + 1, :]
                row = lax.broadcasted_iota(jnp.int32, grad_joined.shape, 0)
                grad_joined = jnp.where(row < cls, grad_joined, 0.0)
            return grad_joined.astype(BF16)

        def on_each_side(act):
            for own in range(2):
                pl.when(side == own)(functools.partial(act, own))

        last = None
        if reducing:
            last = LastReducer(
                bits, HALF_ORDERS,
                (last_late, last_landed, last_crossing, last_crossed, sums, last_send, last_recv),
            )

        def settle(unit, step):
            if reducing:
                last.settle(unit, step)

        def leave(number, own):
            sent = 1 - own
            first, count = chunks_of(sent, text_rows)[number]
            start = first if sent == 1 else text_rows + first
            leaving[first : first + count, :] = rows_back(start, count)
            copy(sent, own, number).start()

        kept_rows = ROWS - text_rows

        def keep(own):
            if own == 1:
                returned[1] = rows_back(0, text_rows)
            else:
                returned[0, 0:kept_rows, :] = rows_back(text_rows, kept_rows)
                for home in range(2):
                    returned[home, kept_rows:text_rows, :] = jnp.zeros(
                        (text_rows - kept_rows, width), BF16
                    )

        def weight_grad(place, own):
            unit = own if place else 1 - own
            rows = pl.ds(0, kept_rows if unit == 0 else text_rows)
            grad = returned[own, rows, :] if place else leaving[rows, :]
            given = states[rows, :] if place else foreign[rows, :]
            block = dot(given, grad, TN)
            if not reducing:
                fill(last_late.at[place], block)
            else:
                middle = width // 2
                for half, order in enumerate(HALF_ORDERS):
                    columns = block[:, half * middle : (half + 1) * middle]
                    fill(last_late.at[place, half], columns, order)
            lines[13 + unit : 14 + unit, :] = column_sum(grad.astype(F32))

        units = early + heads
        on_each_side(functools.partial(leave, 0))
        wave(units)
        on_each_side(functools.partial(leave, 1))
        foreign_copy.wait()
        on_each_side(functools.partial(weight_grad, 0))
        if reducing:
            last.begin(0)
        on_each_side(keep)
        settle(0, 0)
        wave(units + 1)
        for load in loads[3:]:
            load.wait()
        on_each_side(functools.partial(weight_grad, 1))
        if reducing:
            last.begin(1)
            line_here[0] = lines[...]
            line_copy(0).start()
        state_grad[side] = dot(returned[side], proj_weight[...], NT).astype(BF16)
        grad_store = [
            local(state_grad.at[home], state_grad_hbm.at[home], load_sem.at[number])
            for number, home in enumerate((side, 1 - side))
        ]
        grad_store[0].start()
        settle(1, 0)
        line_step(0)
        wave(units + 2)
        settle(0, 1)
        line_step(1)
        wave(units + 3)
        settle(1, 1)
        line_step(2)

        def arrive(own):
            for number in range(2):
                copy(own, 1 - own, number).wait_recv()
                copy(1 - own, own, number).wait_send()

        on_each_side(arrive)
        state_grad[1 - side] = dot(returned[1 - side], proj_weight[...], NT).astype(BF16)
        grad_store[1].start()
        settle(0, 2)
        line_step(3)
        settle(1, 2)
        wave(units + 4)
        settle(0, 3)
        line_step(4)
        if reducing:
            reducer_of(late).finish(0, units)
        settle(1, 3)
        if reducing:
            last.finish()
        else:
            line_out[...] = lines[...]
            sums[0:heads] = late[...]
            sums[heads : heads + 2] = last_late[...]
        for store in grad_store:
            store.wait()

    def late_phase(late, grad_qkv, qkv_weight, joined, grad_middle, states, proj_weight):
        loads = [
            local(source, target, load_sem.at[6 + number])
            for number, (source, target) in enumerate(
                (
                    (qkv_weight_hbm, qkv_weight), (joined_hbm, joined), (middle_hbm, grad_middle),
                    (states_hbm.at[side], states), (proj_hbm, proj_weight),
                )
            )
        ]
        pl.run_scoped(
            functools.partial(attention_phase, late, grad_qkv, loads),
            pltpu.VMEM((ROWS, width), BF16),
            pltpu.VMEM((width, ROWS), BF16),
            pltpu.VMEM((2, 4, ROWS, LANES), BF16),
            pltpu.VMEM((2, ROWS, LANES), F32),
        )
        pl.run_scoped(
            functools.partial(
                last_phase, late, grad_qkv, loads, qkv_weight, joined, grad_middle, states, proj_weight
            ),
            pltpu.VMEM(last_shape, BF16),
            pltpu.VMEM((2, text_rows, width), BF16),
        )

    pl.run_scoped(
        late_phase,
        pltpu.VMEM((heads,) + unit_shape, BF16),
        pltpu.VMEM((ROWS, 3 * width), BF16),
        pltpu.VMEM((width, 3 * width), BF16),
        pltpu.VMEM((ROWS, width), F32),
        pltpu.VMEM((ROWS, width), F32),
        pltpu.VMEM((text_rows, width), BF16),
        pltpu.VMEM((width, width), BF16),
    )


def layer(
    text_rows, bits, group, length, out_bias, gain2, shift2, up_bias, down_bias, gain1,
    joined, attended, given, out_weight, up_weight, down_weight, qkv, log_total, first_normed,
    qkv_weight, states, proj_weight,
):
    width, hidden = up_weight.shape
    parts = hidden // width
    share = width // GROUPS
    early, heads = 2 * parts + 1, width // LANES // 2
    units = early + heads
    whole = (2,) * bits if bits else (GROUPS,)
    line_shape = (VECTOR_ROWS, width)
    steps = bits + 1
    reducing = []
    if bits:
        for slots, cut in ([(slot,) for slot in SLOTS], 1), ([(2, 2)] * bits, 2):
            reducing += [
                pltpu.VMEM(slots[step] + (2,) * (bits - 1 - step) + (share, width // cut), BF16)
                for step in range(bits)
            ]
        reducing += [
            pltpu.VMEM((units, share, width), BF16),
            pltpu.VMEM((units, share, width), BF16),
            pltpu.VMEM((2, share, width), BF16),
            pltpu.VMEM((share, width), BF16),
            pltpu.VMEM((2,) + (2,) * (bits - 1) + (share, width), BF16),
            pltpu.SemaphoreType.DMA((2,)),
            pltpu.SemaphoreType.DMA((units, steps)),
            pltpu.SemaphoreType.DMA((units, steps)),
            pltpu.SemaphoreType.DMA((2, 2, steps)),
            pltpu.SemaphoreType.DMA((2, 2, steps)),
            pltpu.VMEM((steps,) + line_shape, F32),
            pltpu.VMEM((steps,) + line_shape, F32),
            pltpu.SemaphoreType.DMA((steps,)),
            pltpu.SemaphoreType.DMA((steps,)),
        ]
    sums = (units + 1, share, width) if bits else (heads + 2, GROUPS, share, width)
    outs = pl.pallas_call(
        functools.partial(layer_kernel, text_rows, bits),
        out_shape=(
            jax.ShapeDtypeStruct(given.shape, BF16),
            jax.ShapeDtypeStruct(states.shape, BF16),
            jax.ShapeDtypeStruct(sums, F32 if bits else BF16),
            jax.ShapeDtypeStruct(line_shape, F32),
            jax.ShapeDtypeStruct((early,) + whole + (share, width), BF16),
            jax.ShapeDtypeStruct((ROWS, width), F32),
        ),
        in_specs=in_smem(2) + in_vmem(6) + anywhere(12),
        out_specs=tuple(anywhere(2) + [pl.BlockSpec()] * 2 + anywhere(2)),
        scratch_shapes=[
            pltpu.VMEM((ROWS, LANES), BF16),
            pltpu.VMEM((ROWS, width), BF16),
            pltpu.VMEM((2, text_rows, width), BF16),
            pltpu.VMEM((text_rows, width), BF16),
            pltpu.VMEM((text_rows, width), BF16),
            pltpu.VMEM(line_shape, F32),
            pltpu.SemaphoreType.DMA((11,)),
            pltpu.SemaphoreType.DMA((early,)),
            pltpu.SemaphoreType.DMA((2, 5)),
            pltpu.SemaphoreType.DMA((3,)),
            pltpu.SemaphoreType.DMA((3,)),
        ]
        + reducing,
        compiler_params=pltpu.CompilerParams(
            collective_id=1, has_side_effects=True, vmem_limit_bytes=63 << 20
        ),
        name="layer",
    )(
        group, length, out_bias, gain2, shift2, up_bias, down_bias, gain1,
        joined, attended, given, out_weight, up_weight, down_weight, qkv, log_total, first_normed,
        qkv_weight, states, proj_weight,
    )
    return outs[:5]


def spread_kernel(layout, sums_ref, lines_ref, layer_hbm, state_hbm, layer_out, state_out, *outs):
    outs, (layer_here, state_here, sem) = outs[:-3], outs[-3:]
    passes = [
        [
            pltpu.make_async_copy(source, here, sem.at[number, 0]),
            pltpu.make_async_copy(here, target, sem.at[number, 1]),
        ]
        for number, (source, here, target) in enumerate(
            ((layer_hbm, layer_here, layer_out), (state_hbm, state_here, state_out))
        )
    ]
    for copy in passes:
        copy[0].start()
    for copy in passes:
        copy[0].wait()
        copy[1].start()
    me = lax.axis_index("items")
    rows, width = sums_ref.shape[1:]
    for (kind, first, count), out_ref in zip(layout, outs):
        if kind == "columns":
            for part in range(count):
                out_ref[:, part * width : (part + 1) * width] = sums_ref[first + part]
        elif kind == "heads":
            for part in range(count):
                for place in range(2):
                    for which in range(3):
                        source = (3 * place + which) * LANES
                        target = which * width + (2 * part + place) * LANES
                        out_ref[:, target : target + LANES] = sums_ref[
                            first + part, :, source : source + LANES
                        ]
        elif kind == "rows":
            for part in range(count):
                out_ref[part * rows : (part + 1) * rows, :] = sums_ref[first + part]
        else:
            line = jnp.concatenate(
                [lines_ref[first + part : first + part + 1, :] for part in range(count)], axis=1
            )
            if kind == "side":
                line = jnp.where(
                    lax.axis_index("tower") == 0,
                    lines_ref[first : first + 1, :],
                    lines_ref[first + 1 : first + 2, :],
                )
            share = out_ref.shape[1]
            line = jnp.broadcast_to(line, (8, line.shape[1]))
            line = pltpu.roll(line, lax.rem(line.shape[1] - me * share, line.shape[1]), 1)
            out_ref[...] = line[0:1, :share]
    for copy in passes:
        copy[1].wait()


def spread(layout, shapes, sums, lines, layer_out, state_grad):
    return pl.pallas_call(
        functools.partial(spread_kernel, layout),
        out_shape=(
            jax.ShapeDtypeStruct(layer_out.shape, BF16),
            jax.ShapeDtypeStruct(state_grad.shape, BF16),
        )
        + tuple(jax.ShapeDtypeStruct(shape, F32) for shape in shapes),
        in_specs=[pl.BlockSpec()] * 2 + anywhere(2),
        out_specs=tuple(anywhere(2) + [pl.BlockSpec()] * len(shapes)),
        scratch_shapes=[
            pltpu.VMEM(layer_out.shape, BF16),
            pltpu.VMEM(state_grad.shape, BF16),
            pltpu.SemaphoreType.DMA((2, 2)),
        ],
        compiler_params=pltpu.CompilerParams(vmem_limit_bytes=63 << 20),
        name="spread_shares",
    )(sums, lines, layer_out, state_grad)


def body(
    states,
    proj_weight,
    proj_bias,
    cls_row,
    norm1_gain,
    norm1_shift,
    qkv_weight,
    qv_bias,
    out_weight,
    out_bias,
    norm2_gain,
    norm2_shift,
    up_weight,
    up_bias,
    down_weight,
    down_bias,
    image_group,
    caption_len,
    out_grad,
):
    width = states.shape[-1]
    text_rows = states.shape[3]
    hidden = up_weight.shape[1]
    parts = hidden // width
    own_states = states.reshape(2, text_rows, width)
    joined, first_normed, qkv = entry(
        own_states, proj_weight[0], proj_bias, cls_row, norm1_gain, norm1_shift, qkv_weight, qv_bias,
    )
    attended, log_total = attention(text_rows, image_group, caption_len, qkv)
    items = lax.axis_size("items")
    share = width // items
    bits = items.bit_length() - 1
    if items != GROUPS or share % TILE_ROWS:
        bits = 0
    layer_out, state_grad, sums, lines, grads = layer(
        text_rows, bits, image_group, caption_len, out_bias, norm2_gain, norm2_shift, up_bias,
        down_bias, norm1_gain, joined, attended, out_grad[0, 0],
        out_weight, up_weight, down_weight, qkv, log_total, first_normed, qkv_weight, own_states,
        proj_weight[0],
    )
    if not bits:
        return (layer_out[None, None], state_grad.reshape(states.shape)) + plain_sums(
            grads, sums, lines, parts
        )
    heads = width // LANES // 2
    last = 2 * parts + 1 + heads
    layout = (
        ("rows", last, 1), ("side", 9 + parts, 1), ("line", 0, 1), ("line", 1, 1),
        ("line", 2, 1), ("heads", 2 * parts + 1, heads), ("line", 3, 2), ("rows", 2 * parts, 1),
        ("line", 5, 1), ("line", 6, 1), ("line", 7, 1), ("columns", 0, parts),
        ("line", 8, parts), ("rows", parts, parts), ("line", 8 + parts, 1),
    )
    shapes = []
    for kind, _, number in layout:
        if kind == "columns":
            shapes.append((share, number * width))
        elif kind == "heads":
            shapes.append((share, 3 * width))
        elif kind == "rows":
            shapes.append((number * share, width))
        else:
            shapes.append((1, number * share))
    layer_out, state_grad, *shares = spread(layout, shapes, sums, lines, layer_out, state_grad)
    layer_out, state_grad = layer_out[None, None], state_grad.reshape(states.shape)
    shares = [
        piece.reshape(-1) if kind in ("line", "side") else piece
        for piece, (kind, _, _) in zip(shares, layout)
    ]
    return (layer_out, state_grad, shares[0][None], shares[1][None]) + tuple(shares[2:])


def plain_sums(grads, later, lines, parts):
    def over_items(part):
        return lax.psum_scatter(part.astype(F32), "items", scatter_dimension=0, tiled=True)

    def over_both(part):
        return lax.psum(over_items(part).astype(BF16), "tower").astype(F32)

    def over_sides(first, second):
        first, second = over_both(first), over_both(second)
        return jnp.where(lax.axis_index("tower") == 0, first, second)[None]

    width = lines.shape[1]
    heads = later.shape[0] - 2
    up_grad = grads[:parts].transpose(1, 2, 0, 3).reshape(width, parts * width)
    down_grad = grads[parts : 2 * parts].transpose(1, 0, 2, 3).reshape(parts * width, width)
    out_grad = grads[2 * parts].reshape(width, width)
    qkv_grad = later[:heads].reshape(heads, width, 2, 3, LANES).transpose(1, 3, 0, 2, 4)
    qkv_grad = qkv_grad.reshape(width, 3 * width)
    sides = [later[heads + place].reshape(width, width) for place in range(2)]
    image_first = lax.axis_index("tower") == 1
    sides = (
        jnp.where(image_first, sides[0], sides[1]),
        jnp.where(image_first, sides[1], sides[0]),
    )
    return (
        over_sides(*sides),
        over_sides(lines[9 + parts], lines[10 + parts]),
        over_both(lines[0]),
        over_both(lines[1]),
        over_both(lines[2]),
        over_both(qkv_grad),
        over_both(lines[3:5].reshape(-1)),
        over_both(out_grad),
        over_both(lines[5]),
        over_both(lines[6]),
        over_both(lines[7]),
        over_both(up_grad),
        over_both(lines[8 : 8 + parts].reshape(-1)),
        over_both(down_grad),
        over_both(lines[8 + parts]),
    )


def solution(mesh):
    in_specs = (
        P("tower", None, "items", None, None),
        P("tower", None, None),
        P("tower", None),
        P(),
        P(),
        P(),
        P(),
        P(),
        P(),
        P(),
        P(),
        P(),
        P(),
        P(),
        P(),
        P(),
        P("tower", "items"),
        P("tower", "items"),
        P("tower", "items", None, None),
    )
    out_specs = (
        P("tower", "items", None, None),
        P("tower", None, "items", None, None),
        P("tower", "items", None),
        P("tower", "items"),
        P("items"),
        P("items"),
        P("items"),
        P("items", None),
        P("items"),
        P("items", None),
        P("items"),
        P("items"),
        P("items"),
        P("items", None),
        P("items"),
        P("items", None),
        P("items"),
    )
    return jax.shard_map(body, mesh=mesh, in_specs=in_specs, out_specs=out_specs, check_vma=False)
```

```python
import functools

import jax
import jax.numpy as jnp
from jax import lax
from jax.experimental import pallas as pl
from jax.experimental.pallas import tpu as pltpu
from jax.sharding import PartitionSpec as P

HEADS = 12
HEAD_DIM = 64
PATCH_SMALL = 197
PATCH_BIG = 325
EPSILON = 1e-06
MASKED = -1000000000.0
SCALE = 0.125
ROWS = 896
LANES = 128
TILE_ROWS = 16
GROUPS = 16
STARTS = (0, 1, 3, 4, 5)
SLOTS = (5, 6, 4, 3)
VECTOR_ROWS = 16
HALF_ORDERS = ((0, 1, 2, 3), (0, 2, 3, 1))

F32 = jnp.float32
BF16 = jnp.bfloat16
NN = (((1,), (0,)), ((), ()))
NT = (((1,), (1,)), ((), ()))
TN = (((0,), (0,)), ((), ()))
MESH = pl.DeviceIdType.MESH


def dot(left, right, numbers=NN):
    return lax.dot_general(left, right, numbers, preferred_element_type=F32)


def live_rows(shape, group, length, text_rows):
    row = lax.broadcasted_iota(jnp.int32, shape, 0)
    patches = PATCH_SMALL + (PATCH_BIG - PATCH_SMALL) * group
    image = (row >= text_rows) & (row < text_rows + patches)
    return (row < length) | image | (row == text_rows + PATCH_BIG)


def key_lanes(group, length, text_rows):
    lane = lax.broadcasted_iota(jnp.int32, (ROWS, LANES), 1)
    bias = jnp.where(live_rows((ROWS, LANES), group, length, text_rows), 0.0, MASKED)
    return jnp.where(lane == 0, bias, jnp.where(lane < 4, 1.0, 0.0)).astype(BF16)


def query_lanes(first, column):
    lane = lax.broadcasted_iota(jnp.int32, (ROWS, LANES), 1)
    upper = column.astype(BF16).astype(F32)
    rest = column - upper
    inner = rest.astype(BF16).astype(F32)
    lower = rest - inner
    lanes = jnp.where(lane == 0, first, 0.0)
    lanes = jnp.where(lane == 1, -upper, lanes)
    lanes = jnp.where(lane == 2, -inner, lanes)
    return jnp.where(lane == 3, -lower, lanes).astype(BF16)


def head_part(block, head):
    lane = lax.broadcasted_iota(jnp.int32, block.shape, 1)
    keep = lane < HEAD_DIM if head == 0 else lane >= HEAD_DIM
    return jnp.where(keep, block, jnp.zeros_like(block))


def column_sum(block):
    return jnp.sum(block, axis=0, keepdims=True)


def line_of(ref):
    return ref[...].reshape(1, ref.shape[0])


def row_mean(block):
    return jnp.mean(block, axis=1, keepdims=True)


def normalize(block):
    centered = block - row_mean(block)
    inverse = lax.rsqrt(row_mean(centered * centered) + EPSILON)
    return centered * inverse, inverse


def in_vmem(count=1):
    return [pl.BlockSpec(memory_space=pltpu.VMEM)] * count


def in_smem(count=1):
    return [pl.BlockSpec(memory_space=pltpu.SMEM)] * count


def anywhere(count=1):
    return [pl.BlockSpec(memory_space=pl.ANY)] * count


def tower_partner():
    return {"tower": 1 - lax.axis_index("tower")}


def item_partner(bit):
    me = lax.axis_index("items")
    low = lax.rem(me // (1 << bit), 2)
    return {"items": me + (1 - 2 * low) * (1 << bit)}, low


def chunks_of(side, text_rows):
    half = text_rows // 2
    if side == 1:
        return (0, half), (half, half)
    return (0, half), (half, ROWS - text_rows - half)


def crossing_copy(source, target, slot, chunk, send_sem, recv_sem, number):
    first, count = chunk
    return pltpu.make_async_remote_copy(
        src_ref=source.at[pl.ds(first, count)],
        dst_ref=target.at[slot, pl.ds(first, count)],
        send_sem=send_sem.at[number],
        recv_sem=recv_sem.at[number],
        device_id=tower_partner(),
        device_id_type=MESH,
    )


def place_of(number, bits):
    if not bits:
        return (number,)
    if isinstance(number, int):
        return tuple((number >> bit) & 1 for bit in range(bits))
    return tuple(lax.rem(number // (1 << bit), 2) for bit in range(bits))


def entry_kernel(
    text_rows, group_ref, length_ref,
    states_hbm, proj_hbm, proj_bias_ref, cls_ref, gain_ref, shift_ref, qkv_hbm, bias_ref,
    given_hbm, down_hbm,
    joined_hbm, first_hbm, qkv_out_hbm, grad_low_hbm, grad_active_hbm,
    arrived, leaving, states, proj_weight, qkv_weight, joined, first_normed, qkv,
    given, down_weight, wide, shifted, grad_low, grad_active, back_sem,
    load_sem, store_sem, send_sem, recv_sem,
):
    side = lax.axis_index("tower")
    width = joined.shape[1]
    barrier = pltpu.get_barrier_semaphore()
    pl.semaphore_signal(barrier, inc=1, device_id=tower_partner(), device_id_type=MESH)
    sources = (
        (proj_hbm, proj_weight),
        (states_hbm.at[1 - side], states.at[1 - side]),
        (states_hbm.at[side], states.at[side]),
        (qkv_hbm, qkv_weight),
        (given_hbm, given),
        (down_hbm, down_weight),
    )
    loads = [
        pltpu.make_async_copy(source, target, load_sem.at[number])
        for number, (source, target) in enumerate(sources)
    ]
    for load in loads:
        load.start()
    pl.semaphore_wait(barrier, 1)

    def project(rows):
        return (dot(rows, proj_weight[...]) + proj_bias_ref[...]).astype(BF16)

    def copy(own, slot, number):
        chunk = chunks_of(own, text_rows)[number]
        return crossing_copy(leaving, arrived, slot, chunk, send_sem, recv_sem, number)

    half = text_rows // 2
    loads[0].wait()
    loads[1].wait()
    for number in range(2):
        rows = pl.ds(number * half, half)
        leaving[rows, :] = project(states[1 - side, rows, :])
        for own in range(2):

            @pl.when(side == own)
            def _():
                copy(own, own, number).start()

    loads[2].wait()
    arrived[side] = project(states[side])
    loads[3].wait()

    def stores(first, count, number):
        rows = pl.ds(first, count)
        return [
            pltpu.make_async_copy(source.at[rows], target.at[rows], store_sem.at[number, place])
            for place, (source, target) in enumerate(
                ((joined, joined_hbm), (first_normed, first_hbm), (qkv, qkv_out_hbm))
            )
        ]

    def process(first, count, number):
        rows = pl.ds(first, count)
        if first < text_rows:
            block = arrived[1, rows, :].astype(F32)
        else:
            block = arrived[0, pl.ds(first - text_rows, count), :].astype(F32)
            row = first + lax.broadcasted_iota(jnp.int32, block.shape, 0)
            block = jnp.where(row == text_rows + PATCH_BIG, line_of(cls_ref), block)
            block = jnp.where(row > text_rows + PATCH_BIG, 0.0, block)
        joined[rows, :] = block
        scaled, _ = normalize(block)
        normed = (scaled * line_of(gain_ref) + line_of(shift_ref)).astype(BF16)
        first_normed[rows, :] = normed
        for part in range(3):
            columns = slice(part * width, (part + 1) * width)
            product = dot(normed, qkv_weight[:, columns])
            if part == 0:
                product = (product + line_of(bias_ref)[:, :width]) * SCALE
            elif part == 2:
                product = product + line_of(bias_ref)[:, width:]
            qkv[rows, columns] = product.astype(BF16)
        for store in stores(first, count, number):
            store.start()

    def order_of(own):
        other = 1 - own
        order = [(0, text_rows) if own == 1 else (text_rows, ROWS - text_rows)]
        for first, count in chunks_of(other, text_rows):
            order.append((first if other == 1 else text_rows + first, count))
        return order

    for own in range(2):
        pl.when(side == own)(functools.partial(process, *order_of(own)[0], 0))

    extent = given.shape[0]
    parts = grad_active.shape[0]
    mask = live_rows((ROWS, 1), group_ref[0, 0], length_ref[0, 0], text_rows).astype(F32)
    loads[4].wait()
    wide[0:extent, :] = given[...].astype(F32)
    shifted[0:text_rows, :] = wide[1 + PATCH_BIG : extent, :]
    shifted[text_rows : text_rows + PATCH_BIG, :] = wide[1 : 1 + PATCH_BIG, :]
    shifted[text_rows + PATCH_BIG : extent, :] = wide[0:1, :]
    shifted[extent:ROWS, :] = jnp.zeros((ROWS - extent, width), F32)
    grad_low[...] = (shifted[...] * mask).astype(BF16)
    back_stores = [pltpu.make_async_copy(grad_low, grad_low_hbm, back_sem.at[parts])]
    back_stores[0].start()
    loads[5].wait()
    for part in range(parts):
        down = down_weight[part * width : (part + 1) * width, :]
        grad_active[part] = dot(grad_low[...], down, NT).astype(BF16)
        back_stores.append(
            pltpu.make_async_copy(grad_active.at[part], grad_active_hbm.at[part], back_sem.at[part])
        )
        back_stores[-1].start()

    for own in range(2):

        @pl.when(side == own)
        def _():
            other = 1 - own
            for number, (first, count) in enumerate(order_of(own)):
                if number:
                    copy(other, other, number - 1).wait_recv()
                    process(first, count, number)
            for number in range(2):
                copy(own, own, number).wait_send()
            for number, (first, count) in enumerate(order_of(own)):
                for store in stores(first, count, number):
                    store.wait()

    for store in back_stores:
        store.wait()


def entry(
    group, length, states, proj_weight, proj_bias, cls_row, gain, shift, qkv_weight, qkv_bias, given,
    down_weight,
):
    text_rows, width = states.shape[1:]
    parts = down_weight.shape[0] // width
    shapes = (((ROWS, width), F32), ((ROWS, width), BF16), ((ROWS, 3 * width), BF16))
    back_shapes = (((ROWS, width), BF16), ((parts, ROWS, width), BF16))
    return pl.pallas_call(
        functools.partial(entry_kernel, text_rows),
        out_shape=tuple(jax.ShapeDtypeStruct(shape, kind) for shape, kind in shapes + back_shapes),
        in_specs=in_smem(2) + anywhere(2) + in_vmem(4) + anywhere() + in_vmem() + anywhere(2),
        out_specs=tuple(anywhere(5)),
        scratch_shapes=[
            pltpu.VMEM((2, text_rows, width), BF16),
            pltpu.VMEM((text_rows, width), BF16),
            pltpu.VMEM((2, text_rows, width), BF16),
            pltpu.VMEM(proj_weight.shape, BF16),
            pltpu.VMEM(qkv_weight.shape, BF16),
        ]
        + [pltpu.VMEM(shape, kind) for shape, kind in shapes]
        + [
            pltpu.VMEM(given.shape, BF16),
            pltpu.VMEM(down_weight.shape, BF16),
            pltpu.VMEM((ROWS, width), F32),
            pltpu.VMEM((ROWS, width), F32),
        ]
        + [pltpu.VMEM(shape, kind) for shape, kind in back_shapes]
        + [
            pltpu.SemaphoreType.DMA((parts + 1,)),
            pltpu.SemaphoreType.DMA((6,)),
            pltpu.SemaphoreType.DMA((3, 3)),
            pltpu.SemaphoreType.DMA((2,)),
            pltpu.SemaphoreType.DMA((2,)),
        ],
        compiler_params=pltpu.CompilerParams(
            collective_id=0, has_side_effects=True, vmem_limit_bytes=56 << 20
        ),
        name="entry",
    )(
        group, length, states, proj_weight, proj_bias, cls_row, gain, shift, qkv_weight, qkv_bias, given,
        down_weight,
    )


def attention_kernel(
    text_rows, group_ref, length_ref, qkv_hbm, out_hbm, total_hbm,
    blocks, outs, totals, keys_ref, load_sem, store_sem,
):
    pairs = total_hbm.shape[0]
    width = pairs * LANES

    def loads(index, slot):
        return [
            pltpu.make_async_copy(
                qkv_hbm.at[:, pl.ds(pl.multiple_of(part * width + index * LANES, LANES), LANES)],
                blocks.at[slot, part],
                load_sem.at[slot, part],
            )
            for part in range(3)
        ]

    def stores(index, slot):
        columns = pl.ds(pl.multiple_of(index * LANES, LANES), LANES)
        return [
            pltpu.make_async_copy(outs.at[slot], out_hbm.at[:, columns], store_sem.at[slot, 0]),
            pltpu.make_async_copy(totals.at[slot], total_hbm.at[index], store_sem.at[slot, 1]),
        ]

    for load in loads(0, 0):
        load.start()
    keys_ref[...] = key_lanes(group_ref[0, 0], length_ref[0, 0], text_rows)
    lane = lax.broadcasted_iota(jnp.int32, (ROWS, LANES), 1)
    plain = jnp.where(lane == 0, 1.0, 0.0).astype(BF16)

    @pl.loop(0, pairs)
    def pair(index):
        slot = lax.rem(index, 2)
        for load in loads(index, slot):
            load.wait()

        @pl.when(index + 1 < pairs)
        def _():
            for load in loads(index + 1, 1 - slot):
                load.start()

        queries = blocks[slot, 0]
        keys = jnp.concatenate([blocks[slot, 1], keys_ref[...]], axis=1)
        values = jnp.concatenate([blocks[slot, 2], keys_ref[...]], axis=1)
        scores = []
        for head in range(2):
            own = jnp.concatenate([head_part(queries, head), plain], axis=1)
            scores.append(dot(own, keys, NT))
        mixes, logs = [], []
        for head in range(2):
            row_max = jnp.max(scores[head], axis=1, keepdims=True)
            weights = jnp.exp(scores[head] - row_max).astype(BF16)
            mixed = dot(weights, values)
            row_total = mixed[:, LANES + 1 : LANES + 2]
            mixes.append(mixed[:, :LANES] / row_total)
            logs.append(row_max + jnp.log(row_total))

        @pl.when(index >= 2)
        def _():
            for store in stores(index - 2, slot):
                store.wait()

        outs[slot] = jnp.where(lane < HEAD_DIM, mixes[0], mixes[1]).astype(BF16)
        totals[slot] = jnp.where(lane < HEAD_DIM, logs[0], logs[1])
        for store in stores(index, slot):
            store.start()

    for index in (pairs - 2, pairs - 1):
        for store in stores(index, index % 2):
            store.wait()


def attention(text_rows, group, length, qkv):
    width = qkv.shape[1] // 3
    pairs = width // LANES
    return pl.pallas_call(
        functools.partial(attention_kernel, text_rows),
        out_shape=(
            jax.ShapeDtypeStruct((ROWS, width), BF16),
            jax.ShapeDtypeStruct((pairs, ROWS, LANES), F32),
        ),
        in_specs=in_smem(2) + anywhere(),
        out_specs=tuple(anywhere(2)),
        scratch_shapes=[
            pltpu.VMEM((2, 3, ROWS, LANES), BF16),
            pltpu.VMEM((2, ROWS, LANES), BF16),
            pltpu.VMEM((2, ROWS, LANES), F32),
            pltpu.VMEM((ROWS, LANES), BF16),
            pltpu.SemaphoreType.DMA((2, 3)),
            pltpu.SemaphoreType.DMA((2, 2)),
        ],
        compiler_params=pltpu.CompilerParams(vmem_limit_bytes=52 << 20),
        name="attention_forward",
    )(group, length, qkv)


class Reducer:
    def __init__(self, bits, early, units, refs):
        (
            self.grads, self.late, self.landed, self.crossing, self.crossed, self.held, self.sums,
            self.load_sem, self.send_sem, self.recv_sem,
        ) = refs
        self.bits, self.early, self.units = bits, early, units
        self.partners = [item_partner(bit) for bit in range(bits)]

    def greet(self):
        barrier = pltpu.get_barrier_semaphore()
        for partner, _ in self.partners:
            pl.semaphore_signal(barrier, inc=1, device_id=partner, device_id_type=MESH)

    def part(self, ref, first, side):
        return ref.at[first, side]

    def load(self, unit):
        slot = lax.rem(unit, 2)
        return pltpu.make_async_copy(
            self.part(self.grads, unit, self.partners[0][1]),
            self.held.at[slot],
            self.load_sem.at[slot],
        )

    def send(self, unit, step, late=False):
        partner = tower_partner()
        if step == self.bits:
            source, target = self.crossing.at[unit], self.crossed.at[unit]
        else:
            partner, low = self.partners[step]
            target = self.landed[step].at[lax.rem(unit, SLOTS[step])]
            if step:
                source = self.part(
                    self.landed[step - 1], lax.rem(unit, SLOTS[step - 1]), 1 - low
                )
            elif late:
                source = self.part(self.late, unit - self.early, 1 - low)
            else:
                source = self.part(self.grads, unit, 1 - low)
        return pltpu.make_async_remote_copy(
            src_ref=source,
            dst_ref=target,
            send_sem=self.send_sem.at[unit, step],
            recv_sem=self.recv_sem.at[unit, step],
            device_id=partner,
            device_id_type=MESH,
        )

    def add(self, mine, there, depth, last):
        @pl.loop(0, 1 << depth)
        def _(number):
            place = place_of(number, depth) if depth else ()
            if last is None:
                there[place] = mine[place] + there[place]
            else:
                self.crossing[last] = (
                    mine[...].astype(F32) + there[...].astype(F32)
                ).astype(BF16)

    def settle(self, unit, step, late=False):
        self.send(unit, step, late).wait()
        low = self.partners[step][1]
        if step:
            mine = self.part(self.landed[step - 1], lax.rem(unit, SLOTS[step - 1]), low)
        elif late:
            mine = self.part(self.late, unit - self.early, low)
        else:
            self.load(unit).wait()
            mine = self.held.at[lax.rem(unit, 2)]
        depth = self.bits - 1 - step
        there = self.landed[step].at[lax.rem(unit, SLOTS[step])]
        self.add(mine, there, depth, None if depth else unit)
        self.send(unit, step + 1).start()

    def finish(self, first, last):
        @pl.loop(first, last)
        def _(unit):
            self.send(unit, self.bits).wait()
            self.sums[unit] = self.crossing[unit].astype(F32) + self.crossed[unit].astype(F32)

    def begin(self, unit, late=False):
        if not late:
            self.load(unit).start()
        self.send(unit, 0, late).start()

    def either(self, act, unit, late):
        if isinstance(unit, int):
            act(late=unit >= self.early)
        elif not late:
            act(late=False)
        else:
            pl.when(unit < self.early)(functools.partial(act, late=False))
            pl.when(unit >= self.early)(functools.partial(act, late=True))

    def wave(self, number, late=False):
        fixed = isinstance(number, int)
        for step in reversed(range(self.bits)):
            unit = number - STARTS[step + 1]
            if fixed:
                if not 0 <= unit < self.units:
                    continue

            def go():
                if step:
                    self.settle(unit, step)
                else:
                    self.either(functools.partial(self.settle, unit, 0), unit, late)

            if fixed:
                go()
            else:
                pl.when(unit >= 0)(go)
        if not fixed or number < self.units:
            self.either(functools.partial(self.begin, number), number, late)


class LastReducer:
    def __init__(self, bits, orders, refs):
        (
            self.late, self.landed, self.crossing, self.crossed, self.sums, self.send_sem, self.recv_sem,
        ) = refs
        self.bits, self.orders = bits, orders
        self.partners = [item_partner(bit) for bit in range(bits)]

    def part(self, unit, half, step, mine):
        partner, low = self.partners[self.orders[half][step]]
        ref = self.landed[step - 1] if step else self.late
        return ref.at[unit, half, low if mine else 1 - low], partner

    def send(self, unit, half, step):
        source, partner = self.part(unit, half, step, False)
        return pltpu.make_async_remote_copy(
            src_ref=source,
            dst_ref=self.landed[step].at[unit, half],
            send_sem=self.send_sem.at[unit, half, step],
            recv_sem=self.recv_sem.at[unit, half, step],
            device_id=partner,
            device_id_type=MESH,
        )

    def begin(self, unit):
        for half in range(2):
            self.send(unit, half, 0).start()

    def settle(self, unit, step):
        for half in range(2):
            self.send(unit, half, step).wait()
            mine, _ = self.part(unit, half, step, True)
            there = self.landed[step].at[unit, half]
            depth = self.bits - 1 - step
            if depth:

                @pl.loop(0, 1 << depth)
                def _(number):
                    place = place_of(number, depth)
                    there[place] = mine[place] + there[place]

                self.send(unit, half, step + 1).start()
            else:
                width = there.shape[1]
                total = (mine[...].astype(F32) + there[...].astype(F32)).astype(BF16)
                self.crossing[unit, :, half * width : (half + 1) * width] = total
        if step == self.bits - 1 and unit == 0:
            self.cross().start()

    def cross(self):
        return pltpu.make_async_remote_copy(
            src_ref=self.crossing.at[0],
            dst_ref=self.crossed,
            send_sem=self.send_sem.at[0, 0, self.bits],
            recv_sem=self.recv_sem.at[0, 0, self.bits],
            device_id=tower_partner(),
            device_id_type=MESH,
        )

    def finish(self):
        self.cross().wait()
        total = self.crossing[1].astype(F32) + self.crossed[...].astype(F32)
        self.sums[self.sums.shape[0] - 1] = total


def layer_kernel(text_rows, extent, bits, *refs):
    refs = list(refs)

    def take(count):
        taken = refs[:count]
        del refs[:count]
        return taken

    (
        group_ref, length_ref, out_bias_ref, gain2_ref, shift2_ref, up_bias_ref, down_bias_ref,
        gain1_ref,
    ) = take(8)
    (
        joined_hbm, attended_hbm, grad_low_hbm, grad_active_hbm, out_weight_hbm, up_weight_hbm,
        down_weight_hbm, qkv_hbm, total_hbm, first_hbm, qkv_weight_hbm, states_hbm, proj_hbm,
    ) = take(13)
    layer_hbm, state_grad_hbm, sums, line_out, grads_hbm, middle_hbm = take(6)
    padded = layer_hbm.shape[0]
    grad_attended, returned, foreign, lines = take(4)
    load_sem, store_sem, pair_sem, send_sem, recv_sem = take(5)
    reducing = bits > 0
    width = joined_hbm.shape[1]
    hidden = up_weight_hbm.shape[1]
    parts = hidden // width
    pairs = width // LANES
    heads = pairs // 2
    share = width // GROUPS
    early = 2 * parts + 1
    whole = (2,) * bits if bits else (GROUPS,)
    unit_shape = whole + (share, width)
    last_shape = (2, 2) + whole + (share, width // 2) if bits else (2,) + unit_shape
    text_end, image_end = text_rows, text_rows + PATCH_BIG
    side = lax.axis_index("tower")
    barrier = pltpu.get_barrier_semaphore()
    pl.semaphore_signal(barrier, inc=1, device_id=tower_partner(), device_id_type=MESH)
    state = {"late": None}
    if reducing:
        landed, last_landed = take(bits), take(bits)
        (
            crossing, crossed, last_crossing, last_crossed, held, held_sem, unit_send, unit_recv,
            last_send, last_recv, line_here, line_there, line_send, line_recv,
        ) = take(14)

        def reducer_of(late):
            return Reducer(
                bits, early, early + heads,
                (grads_hbm, late, landed, crossing, crossed, held, sums, held_sem, unit_send, unit_recv),
            )

        reducer_of(None).greet()

    def wave(number, late=False):
        if reducing:
            reducer_of(state["late"]).wave(number, late)

    def fill(target, block, order=tuple(range(bits))):
        block = block.astype(BF16).reshape(GROUPS, share, block.shape[1])
        for number in range(GROUPS):
            place = place_of(number, bits)
            if bits:
                place = tuple(place[bit] for bit in order)
            target[place] = block[number]

    def local(source, target, sem):
        return pltpu.make_async_copy(source, target, sem)

    foreign_copy = pltpu.make_async_remote_copy(
        src_ref=states_hbm.at[1 - side],
        dst_ref=foreign,
        send_sem=send_sem.at[2],
        recv_sem=recv_sem.at[2],
        device_id=tower_partner(),
        device_id_type=MESH,
    )

    def middle_phase(
        out_weight, up_weight, down_weight, attended,
        wide, result, grad_second, normed, across, grad_low, up_stage, down_stage,
    ):
        loads = [
            local(source, target, load_sem.at[number])
            for number, (source, target) in enumerate(
                (
                    (grad_low_hbm, grad_low), (out_weight_hbm, out_weight), (attended_hbm, attended),
                    (joined_hbm, grad_second), (up_weight_hbm, up_weight), (down_weight_hbm, down_weight),
                )
            )
        ]
        for load in loads:
            load.start()

        active = grad_attended

        def load_active(part):
            return local(grad_active_hbm.at[part], active, load_sem.at[6])

        load_active(0).start()
        pl.semaphore_wait(barrier, bits + 1)
        foreign_copy.start()

        def store(unit):
            if isinstance(unit, int):
                source = up_stage if unit == 2 * parts else down_stage.at[unit - parts]
            else:
                source = up_stage
            return local(source, grads_hbm.at[unit], store_sem.at[unit])

        mask = live_rows((ROWS, 1), group_ref[0, 0], length_ref[0, 0], text_rows).astype(F32)
        loads[0].wait()
        lines[8 + parts : 9 + parts, :] = column_sum(grad_low[...].astype(F32))
        for load in loads[1:4]:
            load.wait()
        middle = grad_second[...] + (dot(attended[...], out_weight[...]) + line_of(out_bias_ref))
        scaled, inverse = normalize(middle)
        second = scaled * line_of(gain2_ref) + line_of(shift2_ref)
        normed[...] = second.astype(BF16)
        across[...] = second.T.astype(BF16)
        wide[...] = scaled
        result[...] = middle + line_of(down_bias_ref)
        grad_second[...] = jnp.zeros_like(grad_second)
        for load in loads[4:]:
            load.wait()

        @pl.loop(0, parts)
        def tile(part):
            columns = pl.ds(pl.multiple_of(part * width, width), width)
            up, down = up_weight[:, columns], down_weight[columns, :]
            before = dot(normed[...], up) + up_bias_ref[columns].reshape(1, width)
            below = 0.5 + 0.5 * lax.erf(before * 0.7071067811865476)
            density = jnp.exp(-0.5 * before * before) * 0.3989422804014327
            activated = (before * below).astype(BF16)
            load_active(part).wait()
            grad_hidden = active[...].astype(F32) * (below + before * density)
            pl.when(part + 1 < parts)(lambda: load_active(part + 1).start())
            hidden_low = grad_hidden.astype(BF16)
            fill(up_stage, dot(across[...], hidden_low))
            store(part).start()
            result[...] += dot(activated, down)
            grad_second[...] += dot(hidden_low, up, NT)
            lines[pl.ds(8 + part, 1), :] = column_sum(hidden_low.astype(F32))
            down_grad = dot(activated, grad_low[...], TN).astype(BF16)
            rows = GROUPS // parts
            for group in range(rows):
                for piece in range(parts):
                    first = (group * parts + piece) * share
                    place = place_of(part * rows + group, bits)
                    down_stage[(piece,) + place] = down_grad[first : first + share]
            store(part).wait()
            wave(part)

        for piece in range(parts):
            store(parts + piece).start()
        result[...] = result[...] * mask
        second_grad = grad_second[...]
        scaled = wide[...]
        lines[6:7, :] = column_sum(second_grad * scaled)
        lines[7:8, :] = column_sum(second_grad)
        second_grad = second_grad * line_of(gain2_ref)
        grad_middle = grad_low[...].astype(F32) + inverse * (
            second_grad - row_mean(second_grad) - scaled * row_mean(second_grad * scaled)
        )
        grad_second[...] = grad_middle
        middle_store = local(grad_second, middle_hbm, load_sem.at[0])
        middle_store.start()
        for piece in range(parts):
            store(parts + piece).wait()
        wave(parts)
        grad_branch = grad_middle.astype(BF16)
        lines[5:6, :] = column_sum(grad_branch.astype(F32))
        fill(up_stage, dot(attended[...], grad_branch, TN))
        store(2 * parts).start()
        grad_attended[...] = dot(grad_branch, out_weight[...], NT).astype(BF16)
        wide[0:1, :] = result[image_end:extent, :]
        wide[1 : 1 + PATCH_BIG, :] = result[text_end:image_end, :]
        wide[1 + PATCH_BIG : extent, :] = result[0:text_end, :]
        wide[extent:padded, :] = jnp.zeros((padded - extent, width), F32)
        attended[0:padded, :] = wide[0:padded, :].astype(BF16)
        layer_store = local(attended.at[0:padded], layer_hbm, load_sem.at[1])
        layer_store.start()
        wave(parts + 1)
        store(2 * parts).wait()
        middle_store.wait()
        layer_store.wait()

    pl.run_scoped(
        middle_phase,
        pltpu.VMEM((width, width), BF16),
        pltpu.VMEM((width, hidden), BF16),
        pltpu.VMEM((hidden, width), BF16),
        pltpu.VMEM((ROWS, width), BF16),
        pltpu.VMEM((ROWS, width), F32),
        pltpu.VMEM((ROWS, width), F32),
        pltpu.VMEM((ROWS, width), F32),
        pltpu.VMEM((ROWS, width), BF16),
        pltpu.VMEM((width, ROWS), BF16),
        pltpu.VMEM((ROWS, width), BF16),
        pltpu.VMEM(unit_shape, BF16),
        pltpu.VMEM((parts,) + unit_shape, BF16),
    )

    def store_unit(late, unit, block, columns):
        for number in range(GROUPS):
            late[(unit,) + place_of(number, bits) + (slice(None), columns)] = block[number]

    def attention_phase(late, grad_qkv, last_loads, first, across, blocks, totals, keys_ref):
        state["late"] = late

        def loads(index, slot):
            at = pl.multiple_of(index * LANES, LANES)
            sources = [
                qkv_hbm.at[:, pl.ds(at, LANES)],
                qkv_hbm.at[:, pl.ds(pl.multiple_of(width + at, LANES), LANES)],
                qkv_hbm.at[:, pl.ds(pl.multiple_of(2 * width + at, LANES), LANES)],
                attended_hbm.at[:, pl.ds(at, LANES)],
            ]
            copies = [
                local(source, blocks.at[slot, number], pair_sem.at[slot, number])
                for number, source in enumerate(sources)
            ]
            copies.append(
                local(total_hbm.at[index], totals.at[slot], pair_sem.at[slot, len(sources)])
            )
            return copies

        first_load = local(first_hbm, first, load_sem.at[1])
        for copy in loads(0, 0):
            copy.start()
        first_load.start()
        for load in last_loads:
            load.start()
        keys_ref[...] = key_lanes(group_ref[0, 0], length_ref[0, 0], text_rows)
        first_load.wait()
        across[...] = first[...].T

        @pl.loop(0, pairs)
        def pair(index):
            slot = lax.rem(index, 2)
            for copy in loads(index, slot):
                copy.wait()

            @pl.when(index + 1 < pairs)
            def _():
                for copy in loads(index + 1, 1 - slot):
                    copy.start()

            at = pl.multiple_of(index * LANES, LANES)
            key_at = pl.multiple_of(width + at, LANES)
            value_at = pl.multiple_of(2 * width + at, LANES)
            queries, keys, values = blocks[slot, 0], blocks[slot, 1], blocks[slot, 2]
            back = grad_attended[:, pl.ds(at, LANES)]
            product = back.astype(F32) * blocks[slot, 3].astype(F32)
            wide_keys = jnp.concatenate([keys, keys_ref[...]], axis=1)
            wide_values = jnp.concatenate([values, keys_ref[...]], axis=1)
            keys_across = keys.T
            query_grad, key_grad, value_grad = [], None, None
            for head in range(2):
                own_queries = head_part(queries, head)
                own_back = head_part(back, head)
                log_total = totals[slot, :, HEAD_DIM * head : HEAD_DIM * head + 1]
                inner = jnp.sum(head_part(product, head), axis=1, keepdims=True)
                left = jnp.concatenate([own_queries, query_lanes(1.0, log_total)], axis=1)
                right = jnp.concatenate([own_back, query_lanes(0.0, inner)], axis=1)
                weights = jnp.exp(dot(wide_keys, left, NT))
                score_grad = (weights * dot(wide_values, right, NT)).astype(BF16)
                value_part = dot(weights.astype(BF16), own_back)
                key_part = dot(score_grad, own_queries)
                value_grad = value_part if value_grad is None else value_grad + value_part
                key_grad = key_part if key_grad is None else key_grad + key_part
                query_grad.append(
                    dot(keys_across[HEAD_DIM * head : HEAD_DIM * (head + 1)], score_grad)
                )
            query_grad = (SCALE * jnp.concatenate(query_grad, axis=0).T).astype(BF16)
            key_grad, value_grad = key_grad.astype(BF16), value_grad.astype(BF16)
            grad_qkv[:, pl.ds(at, LANES)] = query_grad
            grad_qkv[:, pl.ds(key_at, LANES)] = key_grad
            grad_qkv[:, pl.ds(value_at, LANES)] = value_grad
            lines[3:4, pl.ds(at, LANES)] = column_sum(query_grad.astype(F32))
            lines[4:5, pl.ds(at, LANES)] = column_sum(value_grad.astype(F32))
            both = jnp.concatenate([query_grad, key_grad, value_grad], axis=1)
            weight_grad = dot(across[...], both).astype(BF16)
            weight_grad = weight_grad.reshape((GROUPS, share, 3 * LANES))
            for place in range(2):

                @pl.when(lax.rem(index, 2) == place)
                def _():
                    columns = slice(3 * LANES * place, 3 * LANES * (place + 1))
                    store_unit(late, index // 2, weight_grad, columns)

            wave(parts + 2 + index, late=True)

    def line_copy(number):
        partner = item_partner(number)[0] if number < bits else tower_partner()
        return pltpu.make_async_remote_copy(
            src_ref=line_here.at[number],
            dst_ref=line_there.at[number],
            send_sem=line_send.at[number],
            recv_sem=line_recv.at[number],
            device_id=partner,
            device_id_type=MESH,
        )

    def line_step(number):
        if not reducing:
            return
        line_copy(number).wait()
        total = line_here[number] + line_there[number]
        if number < bits:
            line_here[number + 1] = total
            line_copy(number + 1).start()
        else:
            line_out[...] = total

    def last_phase(
        late, grad_qkv, loads, qkv_weight, joined, grad_middle, states, proj_weight,
        last_late, state_grad, leaving,
    ):
        def copy(own, slot, number):
            chunk = chunks_of(own, text_rows)[number]
            return crossing_copy(leaving, returned, slot, chunk, send_sem, recv_sem, number)

        for load in loads[:3]:
            load.wait()
        lines[1:3, :] = jnp.zeros((2, width), F32)

        def rows_back(first, count):
            rows = pl.ds(first, count)
            grad_first = dot(grad_qkv[rows, :], qkv_weight[...], NT)
            scaled, inverse = normalize(joined[rows, :])
            lines[1:2, :] += column_sum(grad_first * scaled)
            lines[2:3, :] += column_sum(grad_first)
            grad_first = grad_first * line_of(gain1_ref)
            grad_joined = grad_middle[rows, :] + inverse * (
                grad_first - row_mean(grad_first) - scaled * row_mean(grad_first * scaled)
            )
            if first + count == ROWS:
                cls = text_rows + PATCH_BIG - first
                lines[0:1, :] = grad_joined[cls : cls + 1, :]
                row = lax.broadcasted_iota(jnp.int32, grad_joined.shape, 0)
                grad_joined = jnp.where(row < cls, grad_joined, 0.0)
            return grad_joined.astype(BF16)

        def on_each_side(act):
            for own in range(2):
                pl.when(side == own)(functools.partial(act, own))

        last = None
        if reducing:
            last = LastReducer(
                bits, HALF_ORDERS,
                (last_late, last_landed, last_crossing, last_crossed, sums, last_send, last_recv),
            )

        def settle(unit, step):
            if reducing:
                last.settle(unit, step)

        def leave(number, own):
            sent = 1 - own
            first, count = chunks_of(sent, text_rows)[number]
            start = first if sent == 1 else text_rows + first
            leaving[first : first + count, :] = rows_back(start, count)
            copy(sent, own, number).start()

        kept_rows = ROWS - text_rows

        def keep(own):
            if own == 1:
                returned[1] = rows_back(0, text_rows)
            else:
                returned[0, 0:kept_rows, :] = rows_back(text_rows, kept_rows)
                for home in range(2):
                    returned[home, kept_rows:text_rows, :] = jnp.zeros(
                        (text_rows - kept_rows, width), BF16
                    )

        def weight_grad(place, own):
            unit = own if place else 1 - own
            rows = pl.ds(0, kept_rows if unit == 0 else text_rows)
            grad = returned[own, rows, :] if place else leaving[rows, :]
            given = states[rows, :] if place else foreign[rows, :]
            block = dot(given, grad, TN)
            if not reducing:
                fill(last_late.at[place], block)
            else:
                middle = width // 2
                for half, order in enumerate(HALF_ORDERS):
                    columns = block[:, half * middle : (half + 1) * middle]
                    fill(last_late.at[place, half], columns, order)
            lines[13 + unit : 14 + unit, :] = column_sum(grad.astype(F32))

        units = early + heads
        on_each_side(functools.partial(leave, 0))
        wave(units)
        on_each_side(functools.partial(leave, 1))
        foreign_copy.wait()
        on_each_side(functools.partial(weight_grad, 0))
        if reducing:
            last.begin(0)
        on_each_side(keep)
        settle(0, 0)
        wave(units + 1)
        for load in loads[3:]:
            load.wait()
        on_each_side(functools.partial(weight_grad, 1))
        if reducing:
            last.begin(1)
            line_here[0] = lines[...]
            line_copy(0).start()
        state_grad[side] = dot(returned[side], proj_weight[...], NT).astype(BF16)
        grad_store = [
            local(state_grad.at[home], state_grad_hbm.at[home], load_sem.at[number])
            for number, home in enumerate((side, 1 - side))
        ]
        grad_store[0].start()
        settle(1, 0)
        line_step(0)
        wave(units + 2)
        settle(0, 1)
        line_step(1)
        wave(units + 3)
        settle(1, 1)
        line_step(2)

        def arrive(own):
            for number in range(2):
                copy(own, 1 - own, number).wait_recv()
                copy(1 - own, own, number).wait_send()

        on_each_side(arrive)
        state_grad[1 - side] = dot(returned[1 - side], proj_weight[...], NT).astype(BF16)
        grad_store[1].start()
        settle(0, 2)
        line_step(3)
        settle(1, 2)
        wave(units + 4)
        settle(0, 3)
        line_step(4)
        if reducing:
            reducer_of(late).finish(0, units)
        settle(1, 3)
        if reducing:
            last.finish()
        else:
            line_out[...] = lines[...]
            sums[0:heads] = late[...]
            sums[heads : heads + 2] = last_late[...]
        for store in grad_store:
            store.wait()

    def late_phase(late, grad_qkv, qkv_weight, joined, grad_middle, states, proj_weight):
        loads = [
            local(source, target, load_sem.at[6 + number])
            for number, (source, target) in enumerate(
                (
                    (qkv_weight_hbm, qkv_weight), (joined_hbm, joined), (middle_hbm, grad_middle),
                    (states_hbm.at[side], states), (proj_hbm, proj_weight),
                )
            )
        ]
        pl.run_scoped(
            functools.partial(attention_phase, late, grad_qkv, loads),
            pltpu.VMEM((ROWS, width), BF16),
            pltpu.VMEM((width, ROWS), BF16),
            pltpu.VMEM((2, 4, ROWS, LANES), BF16),
            pltpu.VMEM((2, ROWS, LANES), F32),
            pltpu.VMEM((ROWS, LANES), BF16),
        )
        pl.run_scoped(
            functools.partial(
                last_phase, late, grad_qkv, loads, qkv_weight, joined, grad_middle, states, proj_weight
            ),
            pltpu.VMEM(last_shape, BF16),
            pltpu.VMEM((2, text_rows, width), BF16),
            pltpu.VMEM((text_rows, width), BF16),
        )

    pl.run_scoped(
        late_phase,
        pltpu.VMEM((heads,) + unit_shape, BF16),
        pltpu.VMEM((ROWS, 3 * width), BF16),
        pltpu.VMEM((width, 3 * width), BF16),
        pltpu.VMEM((ROWS, width), F32),
        pltpu.VMEM((ROWS, width), F32),
        pltpu.VMEM((text_rows, width), BF16),
        pltpu.VMEM((width, width), BF16),
    )


def layer(
    text_rows, bits, group, length, out_bias, gain2, shift2, up_bias, down_bias, gain1,
    joined, attended, out_shape, grad_low, grad_active, out_weight, up_weight, down_weight, qkv,
    log_total, first_normed, qkv_weight, states, proj_weight,
):
    width, hidden = up_weight.shape
    parts = hidden // width
    share = width // GROUPS
    early, heads = 2 * parts + 1, width // LANES // 2
    units = early + heads
    whole = (2,) * bits if bits else (GROUPS,)
    line_shape = (VECTOR_ROWS, width)
    steps = bits + 1
    reducing = []
    if bits:
        for slots, cut in ([(slot,) for slot in SLOTS], 1), ([(2, 2)] * bits, 2):
            reducing += [
                pltpu.VMEM(slots[step] + (2,) * (bits - 1 - step) + (share, width // cut), BF16)
                for step in range(bits)
            ]
        reducing += [
            pltpu.VMEM((units, share, width), BF16),
            pltpu.VMEM((units, share, width), BF16),
            pltpu.VMEM((2, share, width), BF16),
            pltpu.VMEM((share, width), BF16),
            pltpu.VMEM((2,) + (2,) * (bits - 1) + (share, width), BF16),
            pltpu.SemaphoreType.DMA((2,)),
            pltpu.SemaphoreType.DMA((units, steps)),
            pltpu.SemaphoreType.DMA((units, steps)),
            pltpu.SemaphoreType.DMA((2, 2, steps)),
            pltpu.SemaphoreType.DMA((2, 2, steps)),
            pltpu.VMEM((steps,) + line_shape, F32),
            pltpu.VMEM((steps,) + line_shape, F32),
            pltpu.SemaphoreType.DMA((steps,)),
            pltpu.SemaphoreType.DMA((steps,)),
        ]
    sums = (units + 1, share, width) if bits else (heads + 2, GROUPS, share, width)
    outs = pl.pallas_call(
        functools.partial(layer_kernel, text_rows, out_shape[0], bits),
        out_shape=(
            jax.ShapeDtypeStruct((pl.cdiv(out_shape[0], TILE_ROWS) * TILE_ROWS, width), BF16),
            jax.ShapeDtypeStruct(states.shape, BF16),
            jax.ShapeDtypeStruct(sums, F32 if bits else BF16),
            jax.ShapeDtypeStruct(line_shape, F32),
            jax.ShapeDtypeStruct((early,) + whole + (share, width), BF16),
            jax.ShapeDtypeStruct((ROWS, width), F32),
        ),
        in_specs=in_smem(2) + in_vmem(6) + anywhere(13),
        out_specs=tuple(anywhere(2) + [pl.BlockSpec()] * 2 + anywhere(2)),
        scratch_shapes=[
            pltpu.VMEM((ROWS, width), BF16),
            pltpu.VMEM((2, text_rows, width), BF16),
            pltpu.VMEM((text_rows, width), BF16),
            pltpu.VMEM(line_shape, F32),
            pltpu.SemaphoreType.DMA((11,)),
            pltpu.SemaphoreType.DMA((early,)),
            pltpu.SemaphoreType.DMA((2, 5)),
            pltpu.SemaphoreType.DMA((3,)),
            pltpu.SemaphoreType.DMA((3,)),
        ]
        + reducing,
        compiler_params=pltpu.CompilerParams(
            collective_id=1, has_side_effects=True, vmem_limit_bytes=127 << 19
        ),
        name="layer",
    )(
        group, length, out_bias, gain2, shift2, up_bias, down_bias, gain1,
        joined, attended, grad_low, grad_active, out_weight, up_weight, down_weight, qkv, log_total,
        first_normed, qkv_weight, states, proj_weight,
    )
    return outs[:5]


def spread_kernel(layout, sums_ref, lines_ref, layer_hbm, state_hbm, layer_out, state_out, *outs):
    outs, (layer_here, layer_low, state_here, sem) = outs[:-4], outs[-4:]
    passes = [
        [
            pltpu.make_async_copy(source, here, sem.at[number, 0]),
            pltpu.make_async_copy(low, target, sem.at[number, 1]),
        ]
        for number, (source, here, low, target) in enumerate(
            (
                (state_hbm, state_here, state_here, state_out),
                (layer_hbm, layer_here, layer_low, layer_out),
            )
        )
    ]
    for copy in passes:
        copy[0].start()
    for number, copy in enumerate(passes):
        copy[0].wait()
        if number == 1:
            layer_low[...] = layer_here[0 : layer_low.shape[0], :]
        copy[1].start()
    me = lax.axis_index("items")
    rows, width = sums_ref.shape[1:]
    for (kind, first, count), out_ref in zip(layout, outs):
        if kind == "columns":
            for part in range(count):
                out_ref[:, part * width : (part + 1) * width] = sums_ref[first + part]
        elif kind == "heads":
            for part in range(count):
                for place in range(2):
                    for which in range(3):
                        source = (3 * place + which) * LANES
                        target = which * width + (2 * part + place) * LANES
                        out_ref[:, target : target + LANES] = sums_ref[
                            first + part, :, source : source + LANES
                        ]
        elif kind == "rows":
            for part in range(count):
                out_ref[part * rows : (part + 1) * rows, :] = sums_ref[first + part]
        else:
            line = jnp.concatenate(
                [lines_ref[first + part : first + part + 1, :] for part in range(count)], axis=1
            )
            if kind == "side":
                line = jnp.where(
                    lax.axis_index("tower") == 0,
                    lines_ref[first : first + 1, :],
                    lines_ref[first + 1 : first + 2, :],
                )
            share = out_ref.shape[1]
            line = jnp.broadcast_to(line, (8, line.shape[1]))
            line = pltpu.roll(line, lax.rem(line.shape[1] - me * share, line.shape[1]), 1)
            out_ref[...] = line[0:1, :share]
    for copy in passes:
        copy[1].wait()


def spread(layout, shapes, sums, lines, layer_out, state_grad, extent):
    return pl.pallas_call(
        functools.partial(spread_kernel, layout),
        out_shape=(
            jax.ShapeDtypeStruct((extent, layer_out.shape[1]), BF16),
            jax.ShapeDtypeStruct(state_grad.shape, BF16),
        )
        + tuple(jax.ShapeDtypeStruct(shape, F32) for shape in shapes),
        in_specs=[pl.BlockSpec()] * 2 + anywhere(2),
        out_specs=tuple(anywhere(2) + [pl.BlockSpec()] * len(shapes)),
        scratch_shapes=[
            pltpu.VMEM(layer_out.shape, BF16),
            pltpu.VMEM((extent, layer_out.shape[1]), BF16),
            pltpu.VMEM(state_grad.shape, BF16),
            pltpu.SemaphoreType.DMA((2, 2)),
        ],
        compiler_params=pltpu.CompilerParams(vmem_limit_bytes=63 << 20),
        name="spread_shares",
    )(sums, lines, layer_out, state_grad)


def body(
    states,
    proj_weight,
    proj_bias,
    cls_row,
    norm1_gain,
    norm1_shift,
    qkv_weight,
    qv_bias,
    out_weight,
    out_bias,
    norm2_gain,
    norm2_shift,
    up_weight,
    up_bias,
    down_weight,
    down_bias,
    image_group,
    caption_len,
    out_grad,
):
    width = states.shape[-1]
    text_rows = states.shape[3]
    hidden = up_weight.shape[1]
    parts = hidden // width
    own_states = states.reshape(2, text_rows, width)
    given = out_grad[0, 0]
    joined, first_normed, qkv, grad_low, grad_active = entry(
        image_group, caption_len, own_states, proj_weight[0], proj_bias, cls_row, norm1_gain, norm1_shift, qkv_weight, qv_bias,
        given, down_weight,
    )
    attended, log_total = attention(text_rows, image_group, caption_len, qkv)
    items = lax.axis_size("items")
    share = width // items
    bits = items.bit_length() - 1
    if items != GROUPS or share % TILE_ROWS:
        bits = 0
    layer_out, state_grad, sums, lines, grads = layer(
        text_rows, bits, image_group, caption_len, out_bias, norm2_gain, norm2_shift, up_bias,
        down_bias, norm1_gain, joined, attended, given.shape, grad_low, grad_active,
        out_weight, up_weight, down_weight, qkv, log_total, first_normed, qkv_weight, own_states,
        proj_weight[0],
    )
    if not bits:
        return (layer_out[None, None, : given.shape[0]], state_grad.reshape(states.shape)) + plain_sums(
            grads, sums, lines, parts
        )
    heads = width // LANES // 2
    last = 2 * parts + 1 + heads
    layout = (
        ("rows", last, 1), ("side", 9 + parts, 1), ("line", 0, 1), ("line", 1, 1),
        ("line", 2, 1), ("heads", 2 * parts + 1, heads), ("line", 3, 2), ("rows", 2 * parts, 1),
        ("line", 5, 1), ("line", 6, 1), ("line", 7, 1), ("columns", 0, parts),
        ("line", 8, parts), ("rows", parts, parts), ("line", 8 + parts, 1),
    )
    shapes = []
    for kind, _, number in layout:
        if kind == "columns":
            shapes.append((share, number * width))
        elif kind == "heads":
            shapes.append((share, 3 * width))
        elif kind == "rows":
            shapes.append((number * share, width))
        else:
            shapes.append((1, number * share))
    layer_out, state_grad, *shares = spread(
        layout, shapes, sums, lines, layer_out, state_grad, given.shape[0]
    )
    layer_out, state_grad = layer_out[None, None], state_grad.reshape(states.shape)
    shares = [
        piece.reshape(-1) if kind in ("line", "side") else piece
        for piece, (kind, _, _) in zip(shares, layout)
    ]
    return (layer_out, state_grad, shares[0][None], shares[1][None]) + tuple(shares[2:])


def plain_sums(grads, later, lines, parts):
    def over_items(part):
        return lax.psum_scatter(part.astype(F32), "items", scatter_dimension=0, tiled=True)

    def over_both(part):
        return lax.psum(over_items(part).astype(BF16), "tower").astype(F32)

    def over_sides(first, second):
        first, second = over_both(first), over_both(second)
        return jnp.where(lax.axis_index("tower") == 0, first, second)[None]

    width = lines.shape[1]
    heads = later.shape[0] - 2
    up_grad = grads[:parts].transpose(1, 2, 0, 3).reshape(width, parts * width)
    down_grad = grads[parts : 2 * parts].transpose(1, 0, 2, 3).reshape(parts * width, width)
    out_grad = grads[2 * parts].reshape(width, width)
    qkv_grad = later[:heads].reshape(heads, width, 2, 3, LANES).transpose(1, 3, 0, 2, 4)
    qkv_grad = qkv_grad.reshape(width, 3 * width)
    sides = [later[heads + place].reshape(width, width) for place in range(2)]
    image_first = lax.axis_index("tower") == 1
    sides = (
        jnp.where(image_first, sides[0], sides[1]),
        jnp.where(image_first, sides[1], sides[0]),
    )
    return (
        over_sides(*sides),
        over_sides(lines[9 + parts], lines[10 + parts]),
        over_both(lines[0]),
        over_both(lines[1]),
        over_both(lines[2]),
        over_both(qkv_grad),
        over_both(lines[3:5].reshape(-1)),
        over_both(out_grad),
        over_both(lines[5]),
        over_both(lines[6]),
        over_both(lines[7]),
        over_both(up_grad),
        over_both(lines[8 : 8 + parts].reshape(-1)),
        over_both(down_grad),
        over_both(lines[8 + parts]),
    )


def solution(mesh):
    in_specs = (
        P("tower", None, "items", None, None),
        P("tower", None, None),
        P("tower", None),
        P(),
        P(),
        P(),
        P(),
        P(),
        P(),
        P(),
        P(),
        P(),
        P(),
        P(),
        P(),
        P(),
        P("tower", "items"),
        P("tower", "items"),
        P("tower", "items", None, None),
    )
    out_specs = (
        P("tower", "items", None, None),
        P("tower", None, "items", None, None),
        P("tower", "items", None),
        P("tower", "items"),
        P("items"),
        P("items"),
        P("items"),
        P("items", None),
        P("items"),
        P("items", None),
        P("items"),
        P("items"),
        P("items"),
        P("items", None),
        P("items"),
        P("items", None),
        P("items"),
    )
    return jax.shard_map(body, mesh=mesh, in_specs=in_specs, out_specs=out_specs, check_vma=False)
```

```python
import functools

import jax
import jax.numpy as jnp
from jax import lax
from jax.experimental import pallas as pl
from jax.experimental.pallas import tpu as pltpu
from jax.sharding import PartitionSpec as P

HEADS = 12
HEAD_DIM = 64
PATCH_SMALL = 197
PATCH_BIG = 325
EPSILON = 1e-06
MASKED = -1000000000.0
SCALE = 0.125
ROWS = 896
LANES = 128
TILE_ROWS = 16
GROUPS = 16
STARTS = (0, 1, 3, 4, 5)
SLOTS = (5, 6, 4, 3)
VECTOR_ROWS = 16
HALF_ORDERS = ((0, 1, 2, 3), (0, 2, 3, 1))

F32 = jnp.float32
BF16 = jnp.bfloat16
NN = (((1,), (0,)), ((), ()))
NT = (((1,), (1,)), ((), ()))
TN = (((0,), (0,)), ((), ()))
MESH = pl.DeviceIdType.MESH


def dot(left, right, numbers=NN):
    return lax.dot_general(left, right, numbers, preferred_element_type=F32)


def live_rows(shape, group, length, text_rows):
    row = lax.broadcasted_iota(jnp.int32, shape, 0)
    patches = PATCH_SMALL + (PATCH_BIG - PATCH_SMALL) * group
    image = (row >= text_rows) & (row < text_rows + patches)
    return (row < length) | image | (row == text_rows + PATCH_BIG)


def key_lanes(group, length, text_rows):
    lane = lax.broadcasted_iota(jnp.int32, (ROWS, LANES), 1)
    bias = jnp.where(live_rows((ROWS, LANES), group, length, text_rows), 0.0, MASKED)
    return jnp.where(lane == 0, bias, jnp.where(lane < 4, 1.0, 0.0)).astype(BF16)


def query_lanes(first, column):
    lane = lax.broadcasted_iota(jnp.int32, (ROWS, LANES), 1)
    upper = column.astype(BF16).astype(F32)
    rest = column - upper
    inner = rest.astype(BF16).astype(F32)
    lower = rest - inner
    lanes = jnp.where(lane == 0, first, 0.0)
    lanes = jnp.where(lane == 1, -upper, lanes)
    lanes = jnp.where(lane == 2, -inner, lanes)
    return jnp.where(lane == 3, -lower, lanes).astype(BF16)


def head_part(block, head):
    lane = lax.broadcasted_iota(jnp.int32, block.shape, 1)
    keep = lane < HEAD_DIM if head == 0 else lane >= HEAD_DIM
    return jnp.where(keep, block, jnp.zeros_like(block))


def column_sum(block):
    return jnp.sum(block, axis=0, keepdims=True)


def line_of(ref):
    return ref[...].reshape(1, ref.shape[0])


def row_mean(block):
    return jnp.mean(block, axis=1, keepdims=True)


def normalize(block):
    centered = block - row_mean(block)
    inverse = lax.rsqrt(row_mean(centered * centered) + EPSILON)
    return centered * inverse, inverse


def in_vmem(count=1):
    return [pl.BlockSpec(memory_space=pltpu.VMEM)] * count


def in_smem(count=1):
    return [pl.BlockSpec(memory_space=pltpu.SMEM)] * count


def anywhere(count=1):
    return [pl.BlockSpec(memory_space=pl.ANY)] * count


def tower_partner():
    return {"tower": 1 - lax.axis_index("tower")}


def item_partner(bit):
    me = lax.axis_index("items")
    low = lax.rem(me // (1 << bit), 2)
    return {"items": me + (1 - 2 * low) * (1 << bit)}, low


def chunks_of(side, text_rows):
    half = text_rows // 2
    if side == 1:
        return (0, half), (half, half)
    return (0, half), (half, ROWS - text_rows - half)


def crossing_copy(source, target, slot, chunk, send_sem, recv_sem, number):
    first, count = chunk
    return pltpu.make_async_remote_copy(
        src_ref=source.at[pl.ds(first, count)],
        dst_ref=target.at[slot, pl.ds(first, count)],
        send_sem=send_sem.at[number],
        recv_sem=recv_sem.at[number],
        device_id=tower_partner(),
        device_id_type=MESH,
    )


def place_of(number, bits):
    if not bits:
        return (number,)
    if isinstance(number, int):
        return tuple((number >> bit) & 1 for bit in range(bits))
    return tuple(lax.rem(number // (1 << bit), 2) for bit in range(bits))


def entry_kernel(
    text_rows, group_ref, length_ref,
    states_hbm, proj_hbm, proj_bias_ref, cls_ref, gain_ref, shift_ref, qkv_hbm, bias_ref,
    given_hbm, down_hbm,
    joined_hbm, first_hbm, qkv_out_hbm, grad_low_hbm, grad_active_hbm,
    arrived, leaving, states, proj_weight, qkv_weight, joined, first_normed, qkv,
    given, down_weight, wide, shifted, grad_low, grad_active, back_sem,
    load_sem, store_sem, send_sem, recv_sem,
):
    side = lax.axis_index("tower")
    width = joined.shape[1]
    barrier = pltpu.get_barrier_semaphore()
    pl.semaphore_signal(barrier, inc=1, device_id=tower_partner(), device_id_type=MESH)
    sources = (
        (proj_hbm, proj_weight),
        (states_hbm.at[1 - side], states.at[1 - side]),
        (states_hbm.at[side], states.at[side]),
        (qkv_hbm, qkv_weight),
        (given_hbm, given),
        (down_hbm, down_weight),
    )
    loads = [
        pltpu.make_async_copy(source, target, load_sem.at[number])
        for number, (source, target) in enumerate(sources)
    ]
    for load in loads:
        load.start()
    pl.semaphore_wait(barrier, 1)

    def project(rows):
        return (dot(rows, proj_weight[...]) + proj_bias_ref[...]).astype(BF16)

    def copy(own, slot, number):
        chunk = chunks_of(own, text_rows)[number]
        return crossing_copy(leaving, arrived, slot, chunk, send_sem, recv_sem, number)

    half = text_rows // 2
    loads[0].wait()
    loads[1].wait()
    for number in range(2):
        rows = pl.ds(number * half, half)
        leaving[rows, :] = project(states[1 - side, rows, :])
        for own in range(2):

            @pl.when(side == own)
            def _():
                copy(own, own, number).start()

    loads[2].wait()
    arrived[side] = project(states[side])
    loads[3].wait()

    def stores(first, count, number):
        rows = pl.ds(first, count)
        return [
            pltpu.make_async_copy(source.at[rows], target.at[rows], store_sem.at[number, place])
            for place, (source, target) in enumerate(
                ((joined, joined_hbm), (first_normed, first_hbm), (qkv, qkv_out_hbm))
            )
        ]

    def process(first, count, number):
        rows = pl.ds(first, count)
        if first < text_rows:
            block = arrived[1, rows, :].astype(F32)
        else:
            block = arrived[0, pl.ds(first - text_rows, count), :].astype(F32)
            row = first + lax.broadcasted_iota(jnp.int32, block.shape, 0)
            block = jnp.where(row == text_rows + PATCH_BIG, line_of(cls_ref), block)
            block = jnp.where(row > text_rows + PATCH_BIG, 0.0, block)
        joined[rows, :] = block
        scaled, _ = normalize(block)
        normed = (scaled * line_of(gain_ref) + line_of(shift_ref)).astype(BF16)
        first_normed[rows, :] = normed
        for part in range(3):
            columns = slice(part * width, (part + 1) * width)
            product = dot(normed, qkv_weight[:, columns])
            if part == 0:
                product = (product + line_of(bias_ref)[:, :width]) * SCALE
            elif part == 2:
                product = product + line_of(bias_ref)[:, width:]
            qkv[rows, columns] = product.astype(BF16)
        for store in stores(first, count, number):
            store.start()

    def order_of(own):
        other = 1 - own
        order = [(0, text_rows) if own == 1 else (text_rows, ROWS - text_rows)]
        for first, count in chunks_of(other, text_rows):
            order.append((first if other == 1 else text_rows + first, count))
        return order

    for own in range(2):
        pl.when(side == own)(functools.partial(process, *order_of(own)[0], 0))

    extent = given.shape[0]
    parts = grad_active.shape[0]
    mask = live_rows((ROWS, 1), group_ref[0, 0], length_ref[0, 0], text_rows).astype(F32)
    loads[4].wait()
    wide[0:extent, :] = given[...].astype(F32)
    shifted[0:text_rows, :] = wide[1 + PATCH_BIG : extent, :]
    shifted[text_rows : text_rows + PATCH_BIG, :] = wide[1 : 1 + PATCH_BIG, :]
    shifted[text_rows + PATCH_BIG : extent, :] = wide[0:1, :]
    shifted[extent:ROWS, :] = jnp.zeros((ROWS - extent, width), F32)
    grad_low[...] = (shifted[...] * mask).astype(BF16)
    back_stores = [pltpu.make_async_copy(grad_low, grad_low_hbm, back_sem.at[parts])]
    back_stores[0].start()
    loads[5].wait()
    for part in range(parts):
        down = down_weight[part * width : (part + 1) * width, :]
        grad_active[part] = dot(grad_low[...], down, NT).astype(BF16)
        back_stores.append(
            pltpu.make_async_copy(grad_active.at[part], grad_active_hbm.at[part], back_sem.at[part])
        )
        back_stores[-1].start()

    for own in range(2):

        @pl.when(side == own)
        def _():
            other = 1 - own
            for number, (first, count) in enumerate(order_of(own)):
                if number:
                    copy(other, other, number - 1).wait_recv()
                    process(first, count, number)
            for number in range(2):
                copy(own, own, number).wait_send()
            for number, (first, count) in enumerate(order_of(own)):
                for store in stores(first, count, number):
                    store.wait()

    for store in back_stores:
        store.wait()


def entry(
    group, length, states, proj_weight, proj_bias, cls_row, gain, shift, qkv_weight, qkv_bias, given,
    down_weight,
):
    text_rows, width = states.shape[1:]
    parts = down_weight.shape[0] // width
    shapes = (((ROWS, width), F32), ((ROWS, width), BF16), ((ROWS, 3 * width), BF16))
    back_shapes = (((ROWS, width), BF16), ((parts, ROWS, width), BF16))
    return pl.pallas_call(
        functools.partial(entry_kernel, text_rows),
        out_shape=tuple(jax.ShapeDtypeStruct(shape, kind) for shape, kind in shapes + back_shapes),
        in_specs=in_smem(2) + anywhere(2) + in_vmem(4) + anywhere() + in_vmem() + anywhere(2),
        out_specs=tuple(anywhere(5)),
        scratch_shapes=[
            pltpu.VMEM((2, text_rows, width), BF16),
            pltpu.VMEM((text_rows, width), BF16),
            pltpu.VMEM((2, text_rows, width), BF16),
            pltpu.VMEM(proj_weight.shape, BF16),
            pltpu.VMEM(qkv_weight.shape, BF16),
        ]
        + [pltpu.VMEM(shape, kind) for shape, kind in shapes]
        + [
            pltpu.VMEM(given.shape, BF16),
            pltpu.VMEM(down_weight.shape, BF16),
            pltpu.VMEM((ROWS, width), F32),
            pltpu.VMEM((ROWS, width), F32),
        ]
        + [pltpu.VMEM(shape, kind) for shape, kind in back_shapes]
        + [
            pltpu.SemaphoreType.DMA((parts + 1,)),
            pltpu.SemaphoreType.DMA((6,)),
            pltpu.SemaphoreType.DMA((3, 3)),
            pltpu.SemaphoreType.DMA((2,)),
            pltpu.SemaphoreType.DMA((2,)),
        ],
        compiler_params=pltpu.CompilerParams(
            collective_id=0, has_side_effects=True, vmem_limit_bytes=56 << 20
        ),
        name="entry",
    )(
        group, length, states, proj_weight, proj_bias, cls_row, gain, shift, qkv_weight, qkv_bias, given,
        down_weight,
    )


def attention_kernel(
    text_rows, group_ref, length_ref, qkv_hbm, out_hbm, total_hbm,
    blocks, outs, totals, keys_ref, load_sem, store_sem,
):
    pairs = total_hbm.shape[0]
    width = pairs * LANES

    def loads(index, slot):
        return [
            pltpu.make_async_copy(
                qkv_hbm.at[:, pl.ds(pl.multiple_of(part * width + index * LANES, LANES), LANES)],
                blocks.at[slot, part],
                load_sem.at[slot, part],
            )
            for part in range(3)
        ]

    def stores(index, slot):
        columns = pl.ds(pl.multiple_of(index * LANES, LANES), LANES)
        return [
            pltpu.make_async_copy(outs.at[slot], out_hbm.at[:, columns], store_sem.at[slot, 0]),
            pltpu.make_async_copy(totals.at[slot], total_hbm.at[index], store_sem.at[slot, 1]),
        ]

    for load in loads(0, 0):
        load.start()
    keys_ref[...] = key_lanes(group_ref[0, 0], length_ref[0, 0], text_rows)
    lane = lax.broadcasted_iota(jnp.int32, (ROWS, LANES), 1)
    plain = jnp.where(lane == 0, 1.0, 0.0).astype(BF16)

    @pl.loop(0, pairs)
    def pair(index):
        slot = lax.rem(index, 2)
        for load in loads(index, slot):
            load.wait()

        @pl.when(index + 1 < pairs)
        def _():
            for load in loads(index + 1, 1 - slot):
                load.start()

        queries = blocks[slot, 0]
        keys = jnp.concatenate([blocks[slot, 1], keys_ref[...]], axis=1)
        values = jnp.concatenate([blocks[slot, 2], keys_ref[...]], axis=1)
        scores = []
        for head in range(2):
            own = jnp.concatenate([head_part(queries, head), plain], axis=1)
            scores.append(dot(own, keys, NT))
        mixes, logs = [], []
        for head in range(2):
            row_max = jnp.max(scores[head], axis=1, keepdims=True)
            weights = jnp.exp(scores[head] - row_max).astype(BF16)
            mixed = dot(weights, values)
            row_total = mixed[:, LANES + 1 : LANES + 2]
            mixes.append(mixed[:, :LANES] / row_total)
            logs.append(row_max + jnp.log(row_total))

        @pl.when(index >= 2)
        def _():
            for store in stores(index - 2, slot):
                store.wait()

        outs[slot] = jnp.where(lane < HEAD_DIM, mixes[0], mixes[1]).astype(BF16)
        totals[slot] = jnp.where(lane < HEAD_DIM, logs[0], logs[1])
        for store in stores(index, slot):
            store.start()

    for index in (pairs - 2, pairs - 1):
        for store in stores(index, index % 2):
            store.wait()


def attention(text_rows, group, length, qkv):
    width = qkv.shape[1] // 3
    pairs = width // LANES
    return pl.pallas_call(
        functools.partial(attention_kernel, text_rows),
        out_shape=(
            jax.ShapeDtypeStruct((ROWS, width), BF16),
            jax.ShapeDtypeStruct((pairs, ROWS, LANES), F32),
        ),
        in_specs=in_smem(2) + anywhere(),
        out_specs=tuple(anywhere(2)),
        scratch_shapes=[
            pltpu.VMEM((2, 3, ROWS, LANES), BF16),
            pltpu.VMEM((2, ROWS, LANES), BF16),
            pltpu.VMEM((2, ROWS, LANES), F32),
            pltpu.VMEM((ROWS, LANES), BF16),
            pltpu.SemaphoreType.DMA((2, 3)),
            pltpu.SemaphoreType.DMA((2, 2)),
        ],
        compiler_params=pltpu.CompilerParams(vmem_limit_bytes=52 << 20),
        name="attention_forward",
    )(group, length, qkv)


class Reducer:
    def __init__(self, bits, early, units, refs):
        (
            self.grads, self.late, self.landed, self.crossing, self.crossed, self.held, self.sums,
            self.load_sem, self.send_sem, self.recv_sem,
        ) = refs
        self.bits, self.early, self.units = bits, early, units
        self.partners = [item_partner(bit) for bit in range(bits)]

    def greet(self):
        barrier = pltpu.get_barrier_semaphore()
        for partner, _ in self.partners:
            pl.semaphore_signal(barrier, inc=1, device_id=partner, device_id_type=MESH)

    def part(self, ref, first, side):
        return ref.at[first, side]

    def load(self, unit):
        slot = lax.rem(unit, 2)
        return pltpu.make_async_copy(
            self.part(self.grads, unit, self.partners[0][1]),
            self.held.at[slot],
            self.load_sem.at[slot],
        )

    def send(self, unit, step, late=False):
        partner = tower_partner()
        if step == self.bits:
            source, target = self.crossing.at[unit], self.crossed.at[unit]
        else:
            partner, low = self.partners[step]
            target = self.landed[step].at[lax.rem(unit, SLOTS[step])]
            if step:
                source = self.part(
                    self.landed[step - 1], lax.rem(unit, SLOTS[step - 1]), 1 - low
                )
            elif late:
                source = self.part(self.late, unit - self.early, 1 - low)
            else:
                source = self.part(self.grads, unit, 1 - low)
        return pltpu.make_async_remote_copy(
            src_ref=source,
            dst_ref=target,
            send_sem=self.send_sem.at[unit, step],
            recv_sem=self.recv_sem.at[unit, step],
            device_id=partner,
            device_id_type=MESH,
        )

    def add(self, mine, there, depth, last):
        @pl.loop(0, 1 << depth)
        def _(number):
            place = place_of(number, depth) if depth else ()
            if last is None:
                there[place] = mine[place] + there[place]
            else:
                self.crossing[last] = (
                    mine[...].astype(F32) + there[...].astype(F32)
                ).astype(BF16)

    def settle(self, unit, step, late=False):
        self.send(unit, step, late).wait()
        low = self.partners[step][1]
        if step:
            mine = self.part(self.landed[step - 1], lax.rem(unit, SLOTS[step - 1]), low)
        elif late:
            mine = self.part(self.late, unit - self.early, low)
        else:
            self.load(unit).wait()
            mine = self.held.at[lax.rem(unit, 2)]
        depth = self.bits - 1 - step
        there = self.landed[step].at[lax.rem(unit, SLOTS[step])]
        self.add(mine, there, depth, None if depth else unit)
        self.send(unit, step + 1).start()

    def finish(self, first, last):
        @pl.loop(first, last)
        def _(unit):
            self.send(unit, self.bits).wait()
            self.sums[unit] = self.crossing[unit].astype(F32) + self.crossed[unit].astype(F32)

    def begin(self, unit, late=False):
        if not late:
            self.load(unit).start()
        self.send(unit, 0, late).start()

    def either(self, act, unit, late):
        if isinstance(unit, int):
            act(late=unit >= self.early)
        elif not late:
            act(late=False)
        else:
            pl.when(unit < self.early)(functools.partial(act, late=False))
            pl.when(unit >= self.early)(functools.partial(act, late=True))

    def wave(self, number, late=False):
        fixed = isinstance(number, int)
        for step in reversed(range(self.bits)):
            unit = number - STARTS[step + 1]
            if fixed:
                if not 0 <= unit < self.units:
                    continue

            def go():
                if step:
                    self.settle(unit, step)
                else:
                    self.either(functools.partial(self.settle, unit, 0), unit, late)

            if fixed:
                go()
            else:
                pl.when(unit >= 0)(go)
        if not fixed or number < self.units:
            self.either(functools.partial(self.begin, number), number, late)


class LastReducer:
    def __init__(self, bits, orders, refs):
        (
            self.late, self.landed, self.crossing, self.crossed, self.sums, self.send_sem, self.recv_sem,
        ) = refs
        self.bits, self.orders = bits, orders
        self.partners = [item_partner(bit) for bit in range(bits)]

    def part(self, unit, half, step, mine):
        partner, low = self.partners[self.orders[half][step]]
        ref = self.landed[step - 1] if step else self.late
        return ref.at[unit, half, low if mine else 1 - low], partner

    def send(self, unit, half, step):
        source, partner = self.part(unit, half, step, False)
        return pltpu.make_async_remote_copy(
            src_ref=source,
            dst_ref=self.landed[step].at[unit, half],
            send_sem=self.send_sem.at[unit, half, step],
            recv_sem=self.recv_sem.at[unit, half, step],
            device_id=partner,
            device_id_type=MESH,
        )

    def begin(self, unit):
        for half in range(2):
            self.send(unit, half, 0).start()

    def settle(self, unit, step):
        for half in range(2):
            self.send(unit, half, step).wait()
            mine, _ = self.part(unit, half, step, True)
            there = self.landed[step].at[unit, half]
            depth = self.bits - 1 - step
            if depth:

                @pl.loop(0, 1 << depth)
                def _(number):
                    place = place_of(number, depth)
                    there[place] = mine[place] + there[place]

                self.send(unit, half, step + 1).start()
            else:
                width = there.shape[1]
                total = (mine[...].astype(F32) + there[...].astype(F32)).astype(BF16)
                self.crossing[unit, :, half * width : (half + 1) * width] = total
        if step == self.bits - 1 and unit == 0:
            self.cross().start()

    def cross(self):
        return pltpu.make_async_remote_copy(
            src_ref=self.crossing.at[0],
            dst_ref=self.crossed,
            send_sem=self.send_sem.at[0, 0, self.bits],
            recv_sem=self.recv_sem.at[0, 0, self.bits],
            device_id=tower_partner(),
            device_id_type=MESH,
        )

    def finish(self):
        self.cross().wait()
        total = self.crossing[1].astype(F32) + self.crossed[...].astype(F32)
        self.sums[self.sums.shape[0] - 1] = total


def layer_kernel(text_rows, extent, bits, *refs):
    refs = list(refs)

    def take(count):
        taken = refs[:count]
        del refs[:count]
        return taken

    (
        group_ref, length_ref, out_bias_ref, gain2_ref, shift2_ref, up_bias_ref, down_bias_ref,
        gain1_ref,
    ) = take(8)
    (
        joined_hbm, attended_hbm, grad_low_hbm, grad_active_hbm, out_weight_hbm, up_weight_hbm,
        down_weight_hbm, qkv_hbm, total_hbm, first_hbm, qkv_weight_hbm, states_hbm, proj_hbm,
    ) = take(13)
    layer_hbm, state_grad_hbm, sums, line_out, grads_hbm, middle_hbm = take(6)
    padded = layer_hbm.shape[0]
    grad_attended, returned, foreign, lines = take(4)
    load_sem, store_sem, pair_sem, send_sem, recv_sem = take(5)
    reducing = bits > 0
    width = joined_hbm.shape[1]
    hidden = up_weight_hbm.shape[1]
    parts = hidden // width
    pairs = width // LANES
    heads = pairs // 2
    share = width // GROUPS
    early = 2 * parts + 1
    whole = (2,) * bits if bits else (GROUPS,)
    unit_shape = whole + (share, width)
    last_shape = (2, 2) + whole + (share, width // 2) if bits else (2,) + unit_shape
    text_end, image_end = text_rows, text_rows + PATCH_BIG
    side = lax.axis_index("tower")
    barrier = pltpu.get_barrier_semaphore()
    pl.semaphore_signal(barrier, inc=1, device_id=tower_partner(), device_id_type=MESH)
    state = {"late": None}
    if reducing:
        landed, last_landed = take(bits), take(bits)
        (
            crossing, crossed, last_crossing, last_crossed, held, held_sem, unit_send, unit_recv,
            last_send, last_recv, line_here, line_there, line_send, line_recv,
        ) = take(14)

        def reducer_of(late):
            return Reducer(
                bits, early, early + heads,
                (grads_hbm, late, landed, crossing, crossed, held, sums, held_sem, unit_send, unit_recv),
            )

        reducer_of(None).greet()

    def wave(number, late=False):
        if reducing:
            reducer_of(state["late"]).wave(number, late)

    def fill(target, block, order=tuple(range(bits))):
        block = block.astype(BF16).reshape(GROUPS, share, block.shape[1])
        for number in range(GROUPS):
            place = place_of(number, bits)
            if bits:
                place = tuple(place[bit] for bit in order)
            target[place] = block[number]

    def local(source, target, sem):
        return pltpu.make_async_copy(source, target, sem)

    foreign_copy = pltpu.make_async_remote_copy(
        src_ref=states_hbm.at[1 - side],
        dst_ref=foreign,
        send_sem=send_sem.at[2],
        recv_sem=recv_sem.at[2],
        device_id=tower_partner(),
        device_id_type=MESH,
    )

    def middle_phase(
        out_weight, up_weight, down_weight, attended,
        wide, result, grad_second, normed, across, grad_low, up_stage, down_stage,
    ):
        loads = [
            local(source, target, load_sem.at[number])
            for number, (source, target) in enumerate(
                (
                    (grad_low_hbm, grad_low), (out_weight_hbm, out_weight), (attended_hbm, attended),
                    (joined_hbm, grad_second), (up_weight_hbm, up_weight), (down_weight_hbm, down_weight),
                )
            )
        ]
        for load in loads:
            load.start()

        active = grad_attended

        def load_active(part):
            return local(grad_active_hbm.at[part], active, load_sem.at[6])

        load_active(0).start()
        pl.semaphore_wait(barrier, bits + 1)
        foreign_copy.start()

        def store(unit):
            if isinstance(unit, int):
                source = up_stage if unit == 2 * parts else down_stage.at[unit - parts]
            else:
                source = up_stage
            return local(source, grads_hbm.at[unit], store_sem.at[unit])

        mask = live_rows((ROWS, 1), group_ref[0, 0], length_ref[0, 0], text_rows).astype(F32)
        loads[0].wait()
        lines[8 + parts : 9 + parts, :] = column_sum(grad_low[...].astype(F32))
        for load in loads[1:4]:
            load.wait()
        middle = grad_second[...] + (dot(attended[...], out_weight[...]) + line_of(out_bias_ref))
        scaled, inverse = normalize(middle)
        second = scaled * line_of(gain2_ref) + line_of(shift2_ref)
        normed[...] = second.astype(BF16)
        across[...] = normed[...].T
        wide[...] = scaled
        result[...] = middle + line_of(down_bias_ref)
        grad_second[...] = jnp.zeros_like(grad_second)
        for load in loads[4:]:
            load.wait()

        @pl.loop(0, parts)
        def tile(part):
            columns = pl.ds(pl.multiple_of(part * width, width), width)
            up, down = up_weight[:, columns], down_weight[columns, :]
            before = dot(normed[...], up) + up_bias_ref[columns].reshape(1, width)
            below = 0.5 + 0.5 * lax.erf(before * 0.7071067811865476)
            density = jnp.exp(-0.5 * before * before) * 0.3989422804014327
            activated = (before * below).astype(BF16)
            load_active(part).wait()
            grad_hidden = active[...].astype(F32) * (below + before * density)
            pl.when(part + 1 < parts)(lambda: load_active(part + 1).start())
            hidden_low = grad_hidden.astype(BF16)
            fill(up_stage, dot(across[...], hidden_low))
            store(part).start()
            result[...] += dot(activated, down)
            grad_second[...] += dot(hidden_low, up, NT)
            lines[pl.ds(8 + part, 1), :] = column_sum(hidden_low.astype(F32))
            down_grad = dot(activated, grad_low[...], TN).astype(BF16)
            rows = GROUPS // parts
            for group in range(rows):
                for piece in range(parts):
                    first = (group * parts + piece) * share
                    place = place_of(part * rows + group, bits)
                    down_stage[(piece,) + place] = down_grad[first : first + share]
            store(part).wait()
            wave(part)

        for piece in range(parts):
            store(parts + piece).start()
        result[...] = result[...] * mask
        second_grad = grad_second[...]
        scaled = wide[...]
        lines[6:7, :] = column_sum(second_grad * scaled)
        lines[7:8, :] = column_sum(second_grad)
        second_grad = second_grad * line_of(gain2_ref)
        grad_middle = grad_low[...].astype(F32) + inverse * (
            second_grad - row_mean(second_grad) - scaled * row_mean(second_grad * scaled)
        )
        grad_second[...] = grad_middle
        middle_store = local(grad_second, middle_hbm, load_sem.at[0])
        middle_store.start()
        for piece in range(parts):
            store(parts + piece).wait()
        wave(parts)
        grad_branch = grad_middle.astype(BF16)
        lines[5:6, :] = column_sum(grad_branch.astype(F32))
        fill(up_stage, dot(attended[...], grad_branch, TN))
        store(2 * parts).start()
        grad_attended[...] = dot(grad_branch, out_weight[...], NT).astype(BF16)
        wide[0:1, :] = result[image_end:extent, :]
        wide[1 : 1 + PATCH_BIG, :] = result[text_end:image_end, :]
        wide[1 + PATCH_BIG : extent, :] = result[0:text_end, :]
        wide[extent:padded, :] = jnp.zeros((padded - extent, width), F32)
        attended[0:padded, :] = wide[0:padded, :].astype(BF16)
        layer_store = local(attended.at[0:padded], layer_hbm, load_sem.at[1])
        layer_store.start()
        wave(parts + 1)
        store(2 * parts).wait()
        middle_store.wait()
        layer_store.wait()

    pl.run_scoped(
        middle_phase,
        pltpu.VMEM((width, width), BF16),
        pltpu.VMEM((width, hidden), BF16),
        pltpu.VMEM((hidden, width), BF16),
        pltpu.VMEM((ROWS, width), BF16),
        pltpu.VMEM((ROWS, width), F32),
        pltpu.VMEM((ROWS, width), F32),
        pltpu.VMEM((ROWS, width), F32),
        pltpu.VMEM((ROWS, width), BF16),
        pltpu.VMEM((width, ROWS), BF16),
        pltpu.VMEM((ROWS, width), BF16),
        pltpu.VMEM(unit_shape, BF16),
        pltpu.VMEM((parts,) + unit_shape, BF16),
    )

    def store_unit(late, unit, block, columns):
        for number in range(GROUPS):
            late[(unit,) + place_of(number, bits) + (slice(None), columns)] = block[number]

    def attention_phase(late, grad_qkv, last_loads, first, across, blocks, totals, keys_ref):
        state["late"] = late

        def loads(index, slot):
            at = pl.multiple_of(index * LANES, LANES)
            sources = [
                qkv_hbm.at[:, pl.ds(at, LANES)],
                qkv_hbm.at[:, pl.ds(pl.multiple_of(width + at, LANES), LANES)],
                qkv_hbm.at[:, pl.ds(pl.multiple_of(2 * width + at, LANES), LANES)],
                attended_hbm.at[:, pl.ds(at, LANES)],
            ]
            copies = [
                local(source, blocks.at[slot, number], pair_sem.at[slot, number])
                for number, source in enumerate(sources)
            ]
            copies.append(
                local(total_hbm.at[index], totals.at[slot], pair_sem.at[slot, len(sources)])
            )
            return copies

        first_load = local(first_hbm, first, load_sem.at[1])
        for copy in loads(0, 0):
            copy.start()
        first_load.start()
        for load in last_loads:
            load.start()
        keys_ref[...] = key_lanes(group_ref[0, 0], length_ref[0, 0], text_rows)
        first_load.wait()
        across[...] = first[...].T

        @pl.loop(0, pairs)
        def pair(index):
            slot = lax.rem(index, 2)
            for copy in loads(index, slot):
                copy.wait()

            @pl.when(index + 1 < pairs)
            def _():
                for copy in loads(index + 1, 1 - slot):
                    copy.start()

            at = pl.multiple_of(index * LANES, LANES)
            key_at = pl.multiple_of(width + at, LANES)
            value_at = pl.multiple_of(2 * width + at, LANES)
            queries, keys, values = blocks[slot, 0], blocks[slot, 1], blocks[slot, 2]
            back = grad_attended[:, pl.ds(at, LANES)]
            product = back.astype(F32) * blocks[slot, 3].astype(F32)
            wide_keys = jnp.concatenate([keys, keys_ref[...]], axis=1)
            wide_values = jnp.concatenate([values, keys_ref[...]], axis=1)
            keys_across = keys.T
            query_grad, key_grad, value_grad = [], None, None
            for head in range(2):
                own_queries = head_part(queries, head)
                own_back = head_part(back, head)
                log_total = totals[slot, :, HEAD_DIM * head : HEAD_DIM * head + 1]
                inner = jnp.sum(head_part(product, head), axis=1, keepdims=True)
                left = jnp.concatenate([own_queries, query_lanes(1.0, log_total)], axis=1)
                right = jnp.concatenate([own_back, query_lanes(0.0, inner)], axis=1)
                weights = jnp.exp(dot(wide_keys, left, NT))
                score_grad = (weights * dot(wide_values, right, NT)).astype(BF16)
                value_part = dot(weights.astype(BF16), own_back)
                key_part = dot(score_grad, own_queries)
                value_grad = value_part if value_grad is None else value_grad + value_part
                key_grad = key_part if key_grad is None else key_grad + key_part
                query_grad.append(
                    dot(keys_across[HEAD_DIM * head : HEAD_DIM * (head + 1)], score_grad)
                )
            query_grad = (SCALE * jnp.concatenate(query_grad, axis=0).T).astype(BF16)
            key_grad, value_grad = key_grad.astype(BF16), value_grad.astype(BF16)
            grad_qkv[:, pl.ds(at, LANES)] = query_grad
            grad_qkv[:, pl.ds(key_at, LANES)] = key_grad
            grad_qkv[:, pl.ds(value_at, LANES)] = value_grad
            lines[3:4, pl.ds(at, LANES)] = column_sum(query_grad.astype(F32))
            lines[4:5, pl.ds(at, LANES)] = column_sum(value_grad.astype(F32))
            both = jnp.concatenate([query_grad, key_grad, value_grad], axis=1)
            weight_grad = dot(across[...], both).astype(BF16)
            weight_grad = weight_grad.reshape((GROUPS, share, 3 * LANES))
            for place in range(2):

                @pl.when(lax.rem(index, 2) == place)
                def _():
                    columns = slice(3 * LANES * place, 3 * LANES * (place + 1))
                    store_unit(late, index // 2, weight_grad, columns)

            wave(parts + 2 + index, late=True)

    def line_copy(number):
        partner = item_partner(number)[0] if number < bits else tower_partner()
        return pltpu.make_async_remote_copy(
            src_ref=line_here.at[number],
            dst_ref=line_there.at[number],
            send_sem=line_send.at[number],
            recv_sem=line_recv.at[number],
            device_id=partner,
            device_id_type=MESH,
        )

    def line_step(number):
        if not reducing:
            return
        line_copy(number).wait()
        total = line_here[number] + line_there[number]
        if number < bits:
            line_here[number + 1] = total
            line_copy(number + 1).start()
        else:
            line_out[...] = total

    def last_phase(
        late, grad_qkv, loads, qkv_weight, joined, grad_middle, states, proj_weight,
        last_late, state_grad, leaving,
    ):
        def copy(own, slot, number):
            chunk = chunks_of(own, text_rows)[number]
            return crossing_copy(leaving, returned, slot, chunk, send_sem, recv_sem, number)

        for load in loads[:3]:
            load.wait()
        lines[1:3, :] = jnp.zeros((2, width), F32)

        def rows_back(first, count):
            rows = pl.ds(first, count)
            grad_first = dot(grad_qkv[rows, :], qkv_weight[...], NT)
            scaled, inverse = normalize(joined[rows, :])
            lines[1:2, :] += column_sum(grad_first * scaled)
            lines[2:3, :] += column_sum(grad_first)
            grad_first = grad_first * line_of(gain1_ref)
            grad_joined = grad_middle[rows, :] + inverse * (
                grad_first - row_mean(grad_first) - scaled * row_mean(grad_first * scaled)
            )
            if first + count == ROWS:
                cls = text_rows + PATCH_BIG - first
                lines[0:1, :] = grad_joined[cls : cls + 1, :]
                row = lax.broadcasted_iota(jnp.int32, grad_joined.shape, 0)
                grad_joined = jnp.where(row < cls, grad_joined, 0.0)
            return grad_joined.astype(BF16)

        def on_each_side(act):
            for own in range(2):
                pl.when(side == own)(functools.partial(act, own))

        last = None
        if reducing:
            last = LastReducer(
                bits, HALF_ORDERS,
                (last_late, last_landed, last_crossing, last_crossed, sums, last_send, last_recv),
            )

        def settle(unit, step):
            if reducing:
                last.settle(unit, step)

        def leave(number, own):
            sent = 1 - own
            first, count = chunks_of(sent, text_rows)[number]
            start = first if sent == 1 else text_rows + first
            leaving[first : first + count, :] = rows_back(start, count)
            copy(sent, own, number).start()

        kept_rows = ROWS - text_rows

        def keep(own):
            if own == 1:
                returned[1] = rows_back(0, text_rows)
            else:
                returned[0, 0:kept_rows, :] = rows_back(text_rows, kept_rows)
                for home in range(2):
                    returned[home, kept_rows:text_rows, :] = jnp.zeros(
                        (text_rows - kept_rows, width), BF16
                    )

        def weight_grad(place, own):
            unit = own if place else 1 - own
            rows = pl.ds(0, kept_rows if unit == 0 else text_rows)
            grad = returned[own, rows, :] if place else leaving[rows, :]
            given = states[rows, :] if place else foreign[rows, :]
            block = dot(given, grad, TN)
            if not reducing:
                fill(last_late.at[place], block)
            else:
                middle = width // 2
                for half, order in enumerate(HALF_ORDERS):
                    columns = block[:, half * middle : (half + 1) * middle]
                    fill(last_late.at[place, half], columns, order)
            lines[13 + unit : 14 + unit, :] = column_sum(grad.astype(F32))

        units = early + heads
        on_each_side(functools.partial(leave, 0))
        wave(units)
        on_each_side(functools.partial(leave, 1))
        foreign_copy.wait()
        on_each_side(functools.partial(weight_grad, 0))
        if reducing:
            last.begin(0)
        on_each_side(keep)
        settle(0, 0)
        wave(units + 1)
        for load in loads[3:]:
            load.wait()
        on_each_side(functools.partial(weight_grad, 1))
        if reducing:
            last.begin(1)
            line_here[0] = lines[...]
            line_copy(0).start()
        state_grad[side] = dot(returned[side], proj_weight[...], NT).astype(BF16)
        grad_store = [
            local(state_grad.at[home], state_grad_hbm.at[home], load_sem.at[number])
            for number, home in enumerate((side, 1 - side))
        ]
        grad_store[0].start()
        settle(1, 0)
        line_step(0)
        wave(units + 2)
        settle(0, 1)
        line_step(1)
        wave(units + 3)
        settle(1, 1)
        line_step(2)

        def arrive(own):
            for number in range(2):
                copy(own, 1 - own, number).wait_recv()
                copy(1 - own, own, number).wait_send()

        on_each_side(arrive)
        state_grad[1 - side] = dot(returned[1 - side], proj_weight[...], NT).astype(BF16)
        grad_store[1].start()
        settle(0, 2)
        line_step(3)
        settle(1, 2)
        wave(units + 4)
        settle(0, 3)
        line_step(4)
        if reducing:
            reducer_of(late).finish(0, units)
        settle(1, 3)
        if reducing:
            last.finish()
        else:
            line_out[...] = lines[...]
            sums[0:heads] = late[...]
            sums[heads : heads + 2] = last_late[...]
        for store in grad_store:
            store.wait()

    def late_phase(late, grad_qkv, qkv_weight, joined, grad_middle, states, proj_weight):
        loads = [
            local(source, target, load_sem.at[6 + number])
            for number, (source, target) in enumerate(
                (
                    (qkv_weight_hbm, qkv_weight), (joined_hbm, joined), (middle_hbm, grad_middle),
                    (states_hbm.at[side], states), (proj_hbm, proj_weight),
                )
            )
        ]
        pl.run_scoped(
            functools.partial(attention_phase, late, grad_qkv, loads),
            pltpu.VMEM((ROWS, width), BF16),
            pltpu.VMEM((width, ROWS), BF16),
            pltpu.VMEM((2, 4, ROWS, LANES), BF16),
            pltpu.VMEM((2, ROWS, LANES), F32),
            pltpu.VMEM((ROWS, LANES), BF16),
        )
        pl.run_scoped(
            functools.partial(
                last_phase, late, grad_qkv, loads, qkv_weight, joined, grad_middle, states, proj_weight
            ),
            pltpu.VMEM(last_shape, BF16),
            pltpu.VMEM((2, text_rows, width), BF16),
            pltpu.VMEM((text_rows, width), BF16),
        )

    pl.run_scoped(
        late_phase,
        pltpu.VMEM((heads,) + unit_shape, BF16),
        pltpu.VMEM((ROWS, 3 * width), BF16),
        pltpu.VMEM((width, 3 * width), BF16),
        pltpu.VMEM((ROWS, width), F32),
        pltpu.VMEM((ROWS, width), F32),
        pltpu.VMEM((text_rows, width), BF16),
        pltpu.VMEM((width, width), BF16),
    )


def layer(
    text_rows, bits, group, length, out_bias, gain2, shift2, up_bias, down_bias, gain1,
    joined, attended, out_shape, grad_low, grad_active, out_weight, up_weight, down_weight, qkv,
    log_total, first_normed, qkv_weight, states, proj_weight,
):
    width, hidden = up_weight.shape
    parts = hidden // width
    share = width // GROUPS
    early, heads = 2 * parts + 1, width // LANES // 2
    units = early + heads
    whole = (2,) * bits if bits else (GROUPS,)
    line_shape = (VECTOR_ROWS, width)
    steps = bits + 1
    reducing = []
    if bits:
        for slots, cut in ([(slot,) for slot in SLOTS], 1), ([(2, 2)] * bits, 2):
            reducing += [
                pltpu.VMEM(slots[step] + (2,) * (bits - 1 - step) + (share, width // cut), BF16)
                for step in range(bits)
            ]
        reducing += [
            pltpu.VMEM((units, share, width), BF16),
            pltpu.VMEM((units, share, width), BF16),
            pltpu.VMEM((2, share, width), BF16),
            pltpu.VMEM((share, width), BF16),
            pltpu.VMEM((2,) + (2,) * (bits - 1) + (share, width), BF16),
            pltpu.SemaphoreType.DMA((2,)),
            pltpu.SemaphoreType.DMA((units, steps)),
            pltpu.SemaphoreType.DMA((units, steps)),
            pltpu.SemaphoreType.DMA((2, 2, steps)),
            pltpu.SemaphoreType.DMA((2, 2, steps)),
            pltpu.VMEM((steps,) + line_shape, F32),
            pltpu.VMEM((steps,) + line_shape, F32),
            pltpu.SemaphoreType.DMA((steps,)),
            pltpu.SemaphoreType.DMA((steps,)),
        ]
    sums = (units + 1, share, width) if bits else (heads + 2, GROUPS, share, width)
    outs = pl.pallas_call(
        functools.partial(layer_kernel, text_rows, out_shape[0], bits),
        out_shape=(
            jax.ShapeDtypeStruct((pl.cdiv(out_shape[0], TILE_ROWS) * TILE_ROWS, width), BF16),
            jax.ShapeDtypeStruct(states.shape, BF16),
            jax.ShapeDtypeStruct(sums, F32 if bits else BF16),
            jax.ShapeDtypeStruct(line_shape, F32),
            jax.ShapeDtypeStruct((early,) + whole + (share, width), BF16),
            jax.ShapeDtypeStruct((ROWS, width), F32),
        ),
        in_specs=in_smem(2) + in_vmem(6) + anywhere(13),
        out_specs=tuple(anywhere(2) + [pl.BlockSpec()] * 2 + anywhere(2)),
        scratch_shapes=[
            pltpu.VMEM((ROWS, width), BF16),
            pltpu.VMEM((2, text_rows, width), BF16),
            pltpu.VMEM((text_rows, width), BF16),
            pltpu.VMEM(line_shape, F32),
            pltpu.SemaphoreType.DMA((11,)),
            pltpu.SemaphoreType.DMA((early,)),
            pltpu.SemaphoreType.DMA((2, 5)),
            pltpu.SemaphoreType.DMA((3,)),
            pltpu.SemaphoreType.DMA((3,)),
        ]
        + reducing,
        compiler_params=pltpu.CompilerParams(
            collective_id=1, has_side_effects=True, vmem_limit_bytes=127 << 19
        ),
        name="layer",
    )(
        group, length, out_bias, gain2, shift2, up_bias, down_bias, gain1,
        joined, attended, grad_low, grad_active, out_weight, up_weight, down_weight, qkv, log_total,
        first_normed, qkv_weight, states, proj_weight,
    )
    return outs[:5]


def spread_kernel(layout, sums_ref, lines_ref, layer_hbm, state_hbm, layer_out, state_out, *outs):
    outs, (layer_here, layer_low, state_here, sem) = outs[:-4], outs[-4:]
    passes = [
        [
            pltpu.make_async_copy(source, here, sem.at[number, 0]),
            pltpu.make_async_copy(low, target, sem.at[number, 1]),
        ]
        for number, (source, here, low, target) in enumerate(
            (
                (state_hbm, state_here, state_here, state_out),
                (layer_hbm, layer_here, layer_low, layer_out),
            )
        )
    ]
    for copy in passes:
        copy[0].start()
    for number, copy in enumerate(passes):
        copy[0].wait()
        if number == 1:
            layer_low[...] = layer_here[0 : layer_low.shape[0], :]
        copy[1].start()
    me = lax.axis_index("items")
    rows, width = sums_ref.shape[1:]
    for (kind, first, count), out_ref in zip(layout, outs):
        if kind == "columns":
            for part in range(count):
                out_ref[:, part * width : (part + 1) * width] = sums_ref[first + part]
        elif kind == "heads":
            for part in range(count):
                for place in range(2):
                    for which in range(3):
                        source = (3 * place + which) * LANES
                        target = which * width + (2 * part + place) * LANES
                        out_ref[:, target : target + LANES] = sums_ref[
                            first + part, :, source : source + LANES
                        ]
        elif kind == "rows":
            for part in range(count):
                out_ref[part * rows : (part + 1) * rows, :] = sums_ref[first + part]
        else:
            line = jnp.concatenate(
                [lines_ref[first + part : first + part + 1, :] for part in range(count)], axis=1
            )
            if kind == "side":
                line = jnp.where(
                    lax.axis_index("tower") == 0,
                    lines_ref[first : first + 1, :],
                    lines_ref[first + 1 : first + 2, :],
                )
            share = out_ref.shape[1]
            line = jnp.broadcast_to(line, (8, line.shape[1]))
            line = pltpu.roll(line, lax.rem(line.shape[1] - me * share, line.shape[1]), 1)
            out_ref[...] = line[0:1, :share]
    for copy in passes:
        copy[1].wait()


def spread(layout, shapes, sums, lines, layer_out, state_grad, extent):
    return pl.pallas_call(
        functools.partial(spread_kernel, layout),
        out_shape=(
            jax.ShapeDtypeStruct((extent, layer_out.shape[1]), BF16),
            jax.ShapeDtypeStruct(state_grad.shape, BF16),
        )
        + tuple(jax.ShapeDtypeStruct(shape, F32) for shape in shapes),
        in_specs=[pl.BlockSpec()] * 2 + anywhere(2),
        out_specs=tuple(anywhere(2) + [pl.BlockSpec()] * len(shapes)),
        scratch_shapes=[
            pltpu.VMEM(layer_out.shape, BF16),
            pltpu.VMEM((extent, layer_out.shape[1]), BF16),
            pltpu.VMEM(state_grad.shape, BF16),
            pltpu.SemaphoreType.DMA((2, 2)),
        ],
        compiler_params=pltpu.CompilerParams(vmem_limit_bytes=63 << 20),
        name="spread_shares",
    )(sums, lines, layer_out, state_grad)


def body(
    states,
    proj_weight,
    proj_bias,
    cls_row,
    norm1_gain,
    norm1_shift,
    qkv_weight,
    qv_bias,
    out_weight,
    out_bias,
    norm2_gain,
    norm2_shift,
    up_weight,
    up_bias,
    down_weight,
    down_bias,
    image_group,
    caption_len,
    out_grad,
):
    width = states.shape[-1]
    text_rows = states.shape[3]
    hidden = up_weight.shape[1]
    parts = hidden // width
    own_states = states.reshape(2, text_rows, width)
    given = out_grad[0, 0]
    joined, first_normed, qkv, grad_low, grad_active = entry(
        image_group, caption_len, own_states, proj_weight[0], proj_bias, cls_row, norm1_gain, norm1_shift, qkv_weight, qv_bias,
        given, down_weight,
    )
    attended, log_total = attention(text_rows, image_group, caption_len, qkv)
    items = lax.axis_size("items")
    share = width // items
    bits = items.bit_length() - 1
    if items != GROUPS or share % TILE_ROWS:
        bits = 0
    layer_out, state_grad, sums, lines, grads = layer(
        text_rows, bits, image_group, caption_len, out_bias, norm2_gain, norm2_shift, up_bias,
        down_bias, norm1_gain, joined, attended, given.shape, grad_low, grad_active,
        out_weight, up_weight, down_weight, qkv, log_total, first_normed, qkv_weight, own_states,
        proj_weight[0],
    )
    if not bits:
        return (layer_out[None, None, : given.shape[0]], state_grad.reshape(states.shape)) + plain_sums(
            grads, sums, lines, parts
        )
    heads = width // LANES // 2
    last = 2 * parts + 1 + heads
    layout = (
        ("rows", last, 1), ("side", 9 + parts, 1), ("line", 0, 1), ("line", 1, 1),
        ("line", 2, 1), ("heads", 2 * parts + 1, heads), ("line", 3, 2), ("rows", 2 * parts, 1),
        ("line", 5, 1), ("line", 6, 1), ("line", 7, 1), ("columns", 0, parts),
        ("line", 8, parts), ("rows", parts, parts), ("line", 8 + parts, 1),
    )
    shapes = []
    for kind, _, number in layout:
        if kind == "columns":
            shapes.append((share, number * width))
        elif kind == "heads":
            shapes.append((share, 3 * width))
        elif kind == "rows":
            shapes.append((number * share, width))
        else:
            shapes.append((1, number * share))
    layer_out, state_grad, *shares = spread(
        layout, shapes, sums, lines, layer_out, state_grad, given.shape[0]
    )
    layer_out, state_grad = layer_out[None, None], state_grad.reshape(states.shape)
    shares = [
        piece.reshape(-1) if kind in ("line", "side") else piece
        for piece, (kind, _, _) in zip(shares, layout)
    ]
    return (layer_out, state_grad, shares[0][None], shares[1][None]) + tuple(shares[2:])


def plain_sums(grads, later, lines, parts):
    def over_items(part):
        return lax.psum_scatter(part.astype(F32), "items", scatter_dimension=0, tiled=True)

    def over_both(part):
        return lax.psum(over_items(part).astype(BF16), "tower").astype(F32)

    def over_sides(first, second):
        first, second = over_both(first), over_both(second)
        return jnp.where(lax.axis_index("tower") == 0, first, second)[None]

    width = lines.shape[1]
    heads = later.shape[0] - 2
    up_grad = grads[:parts].transpose(1, 2, 0, 3).reshape(width, parts * width)
    down_grad = grads[parts : 2 * parts].transpose(1, 0, 2, 3).reshape(parts * width, width)
    out_grad = grads[2 * parts].reshape(width, width)
    qkv_grad = later[:heads].reshape(heads, width, 2, 3, LANES).transpose(1, 3, 0, 2, 4)
    qkv_grad = qkv_grad.reshape(width, 3 * width)
    sides = [later[heads + place].reshape(width, width) for place in range(2)]
    image_first = lax.axis_index("tower") == 1
    sides = (
        jnp.where(image_first, sides[0], sides[1]),
        jnp.where(image_first, sides[1], sides[0]),
    )
    return (
        over_sides(*sides),
        over_sides(lines[9 + parts], lines[10 + parts]),
        over_both(lines[0]),
        over_both(lines[1]),
        over_both(lines[2]),
        over_both(qkv_grad),
        over_both(lines[3:5].reshape(-1)),
        over_both(out_grad),
        over_both(lines[5]),
        over_both(lines[6]),
        over_both(lines[7]),
        over_both(up_grad),
        over_both(lines[8 : 8 + parts].reshape(-1)),
        over_both(down_grad),
        over_both(lines[8 + parts]),
    )


def solution(mesh):
    in_specs = (
        P("tower", None, "items", None, None),
        P("tower", None, None),
        P("tower", None),
        P(),
        P(),
        P(),
        P(),
        P(),
        P(),
        P(),
        P(),
        P(),
        P(),
        P(),
        P(),
        P(),
        P("tower", "items"),
        P("tower", "items"),
        P("tower", "items", None, None),
    )
    out_specs = (
        P("tower", "items", None, None),
        P("tower", None, "items", None, None),
        P("tower", "items", None),
        P("tower", "items"),
        P("items"),
        P("items"),
        P("items"),
        P("items", None),
        P("items"),
        P("items", None),
        P("items"),
        P("items"),
        P("items"),
        P("items", None),
        P("items"),
        P("items", None),
        P("items"),
    )
    return jax.shard_map(body, mesh=mesh, in_specs=in_specs, out_specs=out_specs, check_vma=False)
```
